32 devices in a mesh: period: 2 (over x), gx: 16 (over z, y, core).
Axes of the slice: x: 2, y: 2, z: 4, core: 2. Of those that a mesh axis runs over, the one named last changes fastest.
Arguments:
- site_owner: int32 [4096], P(('period', 'gx')), parts along dimension 0, may hold values from 0 to 15, as said below
- site_cell: int32 [3, 4096], P(None, ('period', 'gx')), parts along dimension 1, may hold values from 0 to 125, as said below
- stencil_code: int32 [8, 4096], P(None, ('period', 'gx')), parts along dimension 1, may hold values from 0 to 26
- site_residual: float32 [6, 8, 4096], P(None, None, ('period', 'gx')), parts along dimension 2, may hold values from -4 to 4
- conductivity: float32 [3, 64, 32, 128], P(None, 'gx'), may hold values from 0.2 to 2
- omega: float32 [2], P('period'), parts along dimension 0, may hold values from 0.5 to 1.5
Outputs:
- adjoint_field: float32 [12, 64, 32, 128], P('period', 'gx'), parts along dimension 0
- residual: float32 [12, 64, 32, 128], P('period', 'gx'), parts along dimension 0
The draws below stay inside these ranges and needn't reach their ends.
There are 2 independent parts, one for each index of `period`. The reference program is written for one: setup_inputs(seed, part) draws one part's arguments, and reference() takes and returns one part's arrays. A program takes and returns all parts, laid end to end along the dimension named above; an argument that names none is the same for every part. Nothing has to cross between parts.
Inputs may be any that keep to these rules, and one draw needn't show every extreme that they name: `site_owner`: in each aligned block of 128 sites (the sites of one device) no slab is named more than 16 times, and in every block some slab is named exactly 16 times. `site_cell`: row 0 is the base cell along the first dimension within the owning slab, 0 to 1; row 1 along the second dimension, 0 to 29; row 2 along the third, 0 to 125.
All inputs are finite; a program needn't handle non-finite values.
Results may differ from the reference program's by a relative error of at most 0.0003.
Values sent between devices are 32-bit elements; how exact they have to be, the bound alone decides.
No kernel may reach another device: no remote copies, remote signals or barrier semaphores. Data moves between devices by JAX's collectives and lax.ppermute only.
A program may use at most 128 MiB of HBM per device.

```python
import math
import jax
import jax.numpy as jnp
from jax import lax

CX = 4
NY = 32
NZ = 128
SITE_DEV = 128
STENCIL = 8
ITERS = 4
NX = 64
SITES = 2048
CAP = 16
N_GX = 16


def owner_lists(key):
    position_count = N_GX * CAP
    noise_key, favored_key, shuffle_key = jax.random.split(jax.random.fold_in(key, 11), 3)
    position_holder = jnp.arange(position_count, dtype=jnp.int32) // CAP
    random_jitter = jax.random.randint(noise_key, (N_GX, position_count), 0, 2 ** 18, dtype=jnp.int32)
    linear_slope_bias = position_holder * 2 ** 17 // (N_GX - 1)
    preferred_choice = jax.random.randint(favored_key, (N_GX, 1), 0, N_GX, dtype=jnp.int32)
    reward_addend = jnp.where(position_holder[None, :] == preferred_choice, 2 ** 19, 0).astype(jnp.int32)
    rank_scores = (random_jitter + linear_slope_bias[None, :] + reward_addend) * position_count + jnp.arange(position_count, dtype=jnp.int32)[None, :]
    chosen = lax.top_k(rank_scores, SITE_DEV)[1]
    owners = (chosen // CAP).astype(jnp.int32)
    shuffle_scores = jax.random.randint(shuffle_key, (N_GX, SITE_DEV), 0, 2 ** 20, dtype=jnp.int32) * SITE_DEV + jnp.arange(SITE_DEV, dtype=jnp.int32)[None, :]
    shuffle_order = jnp.argsort(shuffle_scores, axis=1)
    return jnp.take_along_axis(owners, shuffle_order, axis=1).reshape(-1).astype(jnp.int32)


def draw_site_owner(key, part):
    return owner_lists(key)


def draw_site_cell(key, part):
    key = jax.random.fold_in(key, 7)
    key_first, key_second, key_third = jax.random.split(key, 3)
    first_row = jax.random.randint(key_first, (SITES,), 0, CX - 2, dtype=jnp.int32)
    second_row = jax.random.randint(key_second, (SITES,), 0, NY - 2, dtype=jnp.int32)
    third_row = jax.random.randint(key_third, (SITES,), 0, NZ - 2, dtype=jnp.int32)
    return jnp.stack([first_row, second_row, third_row]).astype(jnp.int32)


def draw_site_residual(key, part):
    key = jax.random.fold_in(key, 5)
    channel_scale = jnp.array([1.0, 1.0, 1.0, 0.35, 0.35, 0.35], jnp.float32)[:, None, None]
    values = jnp.clip(jax.random.normal(key, (6, STENCIL, SITES), jnp.float32), -4.0, 4.0) * channel_scale
    return values.astype(jnp.float32)


def place_ends(result, rng, smallest, high):
    index_at = [jax.random.randint(jax.random.fold_in(rng, axis), (), 0, length) for axis, length in enumerate(result.shape)]
    widest = result.shape.index(max(result.shape))
    neighbour = index_at[:widest] + [(index_at[widest] + 1) % result.shape[widest]] + index_at[widest + 1:]
    return result.at[tuple(index_at)].set(smallest).at[tuple(neighbour)].set(high)


def shard_levels(key, dims, shards, least, high):
    loudness, own = 1.0, jax.random.fold_in(key, 6)
    for axis_at, shards_of in shards:
        heights = jnp.exp(jax.random.uniform(jax.random.fold_in(own, axis_at), (shards_of,), jnp.float32, least / len(shards), high / len(shards)))
        loudness = loudness * jnp.repeat(heights, dims[axis_at] // shards_of).reshape([-1 if axis == axis_at else 1 for axis in range(len(dims))])
    return loudness


def setup_inputs(seed: int = 0, part: int = 0) -> dict:
    streams_of = jax.random.split(jax.random.key(seed), 7)
    part_splits = jax.random.split(jax.random.fold_in(streams_of[6], part), 7)
    site_owner = draw_site_owner(jax.random.fold_in(jax.random.fold_in(streams_of[6], part), 71), part)
    site_cell = draw_site_cell(jax.random.fold_in(jax.random.fold_in(streams_of[6], part), 71), part)
    stencil_code = place_ends(jax.random.randint(part_splits[2], (STENCIL, SITES), 0, 27), jax.random.fold_in(part_splits[2], 1), 0, 26).astype(jnp.int32)
    site_residual = draw_site_residual(jax.random.fold_in(jax.random.fold_in(streams_of[6], part), 71), part)
    conductivity = jnp.clip(jnp.exp(math.log(2.0) - 2.3025851 * jax.random.uniform(streams_of[4], (3, NX, NY, NZ), jnp.float32) ** shard_levels(streams_of[4], (3, NX, NY, NZ), ((1, 16),), -0.2, 0.2)), 0.2, 2.0)
    omega = jnp.clip(jnp.exp(jax.random.uniform(part_splits[5], (1,), jnp.float32, math.log(0.5), math.log(1.5))), 0.5, 1.5)
    return {"site_owner": site_owner, "site_cell": site_cell, "stencil_code": stencil_code, "site_residual": site_residual, "conductivity": conductivity, "omega": omega}


def ahead(array, which_axis):
    extent = array.shape[which_axis]
    following = jnp.concatenate([lax.slice_in_dim(array, 1, extent, axis=which_axis), jnp.zeros_like(lax.slice_in_dim(array, 0, 1, axis=which_axis))], axis=which_axis)
    return following - array


def behind(array, which_axis):
    extent = array.shape[which_axis]
    preceding = jnp.concatenate([jnp.zeros_like(lax.slice_in_dim(array, 0, 1, axis=which_axis)), lax.slice_in_dim(array, 0, extent - 1, axis=which_axis)], axis=which_axis)
    return array - preceding


def ahead_of(array, top_plane):
    return jnp.concatenate([array[:, 1:], top_plane], axis=1) - array


def behind_of(array, low_plane):
    return array - jnp.concatenate([low_plane, array[:, :-1]], axis=1)


def face_terms(edge_x, edge_y, edge_z, top_y, top_z):
    face_x = ahead(edge_z, 2) - ahead(edge_y, 3)
    face_y = ahead(edge_x, 3) - ahead_of(edge_z, top_z)
    face_z = ahead_of(edge_y, top_y) - ahead(edge_x, 2)
    return face_x, face_y, face_z


def edge_terms(face_x, face_y, face_z, low_y, low_z):
    curl_x = behind(face_z, 2) - behind(face_y, 3)
    curl_y = behind(face_x, 3) - behind_of(face_z, low_z)
    curl_z = behind_of(face_y, low_y) - behind(face_x, 2)
    return jnp.stack([curl_x, curl_y, curl_z], axis=1)


def couple(curl_curl, halves, coupling):
    real_part = curl_curl[0] + coupling * halves[1]
    imag_part = curl_curl[1] - coupling * halves[0]
    return jnp.concatenate([real_part, imag_part], axis=0)


def apply_operator(field, coupling):
    halves = field.reshape((2, 3) + field.shape[1:])
    zero_plane = jnp.zeros_like(halves[:, 0, :1])
    face_x, face_y, face_z = face_terms(halves[:, 0], halves[:, 1], halves[:, 2], zero_plane, zero_plane)
    return couple(edge_terms(face_x, face_y, face_z, zero_plane, zero_plane), halves, coupling)


def pair_form(first_field, second_field):
    real_sum = jnp.sum(first_field[:3] * second_field[:3]) - jnp.sum(first_field[3:] * second_field[3:])
    imag_sum = jnp.sum(first_field[:3] * second_field[3:]) + jnp.sum(first_field[3:] * second_field[:3])
    return jnp.stack([real_sum, imag_sum])


def divide_complex(numer, denom):
    modulus = denom[0] * denom[0] + denom[1] * denom[1]
    return jnp.stack([(numer[0] * denom[0] + numer[1] * denom[1]) / modulus, (numer[1] * denom[0] - numer[0] * denom[1]) / modulus])


def scale_field(factor, field):
    return jnp.concatenate([factor[0] * field[:3] - factor[1] * field[3:], factor[0] * field[3:] + factor[1] * field[:3]], axis=0)


def reference(site_owner, site_cell, stencil_code, site_residual, conductivity, omega):
    cell_total = NX * NY * NZ
    shift_x = stencil_code // 9
    shift_y = (stencil_code // 3) % 3
    shift_z = stencil_code % 3
    cell_x = site_owner[None, :] * CX + site_cell[0][None, :] + shift_x
    cell_y = site_cell[1][None, :] + shift_y
    cell_z = site_cell[2][None, :] + shift_z
    target = ((cell_x * NY + cell_y) * NZ + cell_z).astype(jnp.int32)
    source = jnp.zeros((6, cell_total), jnp.float32).at[:, target.reshape(-1)].add(site_residual.reshape(6, -1))
    source = source.reshape(6, NX, NY, NZ)
    coupling = omega[0] * conductivity
    solution = jnp.zeros_like(source)
    residual = source
    direction = source
    form_now = pair_form(residual, residual)
    for sweep in range(ITERS):
        applied = apply_operator(direction, coupling)
        step_size = divide_complex(form_now, pair_form(direction, applied))
        solution = solution + scale_field(step_size, direction)
        residual = residual - scale_field(step_size, applied)
        if sweep + 1 < ITERS:
            form_next = pair_form(residual, residual)
            direction = residual + scale_field(divide_complex(form_next, form_now), direction)
            form_now = form_next
    return solution, residual
```

```python
import functools

import jax
import jax.numpy as jnp
from jax import lax
from jax.experimental import pallas as pl
from jax.experimental.pallas import tpu as pltpu
from jax.sharding import PartitionSpec as P

ITERS = 4
CENTRE = 5.0
RADIUS = 5.0
BASIS = ITERS + 1
FORMS = 2 * ITERS
PAIRS = [(i // 2, (i + 1) // 2) for i in range(FORMS)]
VMEM_LIMIT = 40 * 1024 * 1024
CONTRACT_LANES = (((1,), (1,)), ((), ()))


def vmem():
    return pl.BlockSpec(memory_space=pltpu.VMEM)


def smem():
    return pl.BlockSpec(memory_space=pltpu.SMEM)


def split_bf16(x):
    high = x.astype(jnp.bfloat16)
    return high, (x - high.astype(jnp.float32)).astype(jnp.bfloat16)


def bin_kernel(n, half, rows, cols, half_depth, owner_ref, cell_ref, code_ref, value_ref, out_ref):
    sites = owner_ref.shape[1]
    owner = owner_ref[...]
    code = code_ref[...]
    dx = (code >= 9).astype(jnp.int32) + (code >= 18).astype(jnp.int32)
    rest = code - 9 * dx
    dy = (rest >= 3).astype(jnp.int32) + (rest >= 6).astype(jnp.int32)
    dz = rest - 3 * dy
    x = cell_ref[0:1] + dx
    y = cell_ref[1:2] + dy
    z = cell_ref[2:3] + dz
    upper = (x >= half_depth).astype(jnp.int32)
    row = (x - half_depth * upper) * rows + y
    lane = z + cols * upper
    channels, points = value_ref.shape[0], value_ref.shape[1]
    data = jnp.concatenate(
        [value_ref[...].reshape(channels * points, sites), row.astype(jnp.float32), lane.astype(jnp.float32)],
        axis=0,
    )
    blank = jnp.zeros_like(data)

    named = lax.broadcasted_iota(jnp.int32, (n, sites), 0) == owner
    earlier = lax.broadcasted_iota(jnp.int32, (sites, sites), 0) < lax.broadcasted_iota(
        jnp.int32, (sites, sites), 1
    )
    named_f = named.astype(jnp.float32)
    counts = jnp.dot(
        named_f.astype(jnp.bfloat16),
        earlier.astype(jnp.float32).astype(jnp.bfloat16),
        preferred_element_type=jnp.float32,
    )
    rank = jnp.sum(counts * named_f, axis=0, keepdims=True).astype(jnp.int32)
    second = rank >= half
    place = jnp.where(second, rank - half, rank)

    slot = lax.broadcasted_iota(jnp.int32, (out_ref.shape[0], sites), 0)
    hit = jnp.zeros(slot.shape, jnp.bool_)
    for j in range(3):
        hit = hit | (slot == ((owner - j + 1) * 3 + j) * half + place)
    total = jnp.zeros(out_ref.shape, jnp.float32)
    for part, stacked in (
        (jnp.logical_not(second), [data, blank]),
        (second, [blank, data]),
    ):
        chosen = jnp.where(hit & part, 1.0, 0.0).astype(jnp.bfloat16)
        for piece in split_bf16(jnp.concatenate(stacked, axis=0)):
            total = total + lax.dot_general(
                chosen, piece, CONTRACT_LANES, preferred_element_type=jnp.float32
            )
    out_ref[...] = total


def field_kernel(
    n, recv_ref, cond_ref, low_ref, high_ref, omega_ref, forms_ref, own_ref, basis, coupling, left, right
):
    depth, rows, cols = cond_ref.shape[1], cond_ref.shape[2], cond_ref.shape[3]
    half_depth = depth // 2
    channels = 6
    points = 8
    group = recv_ref.shape[1] // 3
    me = lax.axis_index("gx")
    keep_low = jnp.where(me > 0, 1.0, 0.0).astype(jnp.float32)
    keep_high = jnp.where(me < n - 1, 1.0, 0.0).astype(jnp.float32)

    scale = omega_ref[0] * (2.0 / RADIUS)
    halo = low_ref.shape[1]
    coupling[:, 0:halo] = low_ref[...] * scale
    coupling[:, halo : halo + depth] = cond_ref[...] * scale
    coupling[:, halo + depth : 2 * halo + depth] = high_ref[...] * scale

    row_count = half_depth * rows
    lane_count = 2 * cols
    slots = 2 * recv_ref.shape[0] * group
    width = (channels + 2) * points
    row_iota = lax.broadcasted_iota(jnp.int32, (row_count, slots), 0)
    lane_iota = lax.broadcasted_iota(jnp.int32, (lane_count, slots), 0)

    def scatter(j, _):
        packed = recv_ref[:, pl.ds(pl.multiple_of(j * group, 8), group), :].reshape(slots // 2, 2 * width)
        turned = packed.T
        table = jnp.concatenate([turned[:width], turned[width:]], axis=1)
        table_high = table.astype(jnp.bfloat16).astype(jnp.float32)
        table_low = table - table_high
        cell_row = table[channels * points : (channels + 1) * points].astype(jnp.int32)
        cell_lane = table[(channels + 1) * points :].astype(jnp.int32)
        for k in range(points):
            span = slice(k * slots, (k + 1) * slots)
            right[:, span] = jnp.where(lane_iota == cell_lane[k : k + 1], 1.0, 0.0).astype(jnp.bfloat16)
            mask = row_iota == cell_row[k : k + 1]
            for c in range(channels):
                at = c * points + k
                for piece, part in enumerate((table_high, table_low)):
                    first = (piece * channels + c) * row_count
                    left[first : first + row_count, span] = jnp.where(mask, part[at : at + 1], 0.0).astype(
                        jnp.bfloat16
                    )
        both = lax.dot_general(left[...], right[...], CONTRACT_LANES, preferred_element_type=jnp.float32)
        summed = both[: channels * row_count] + both[channels * row_count :]
        for c in range(channels):
            for x in range(depth):
                first = c * row_count + (x % half_depth) * rows
                lanes = slice((x // half_depth) * cols, (x // half_depth + 1) * cols)
                basis[0, c, j * depth + x] = summed[first : first + rows, lanes]
        return 0

    lax.fori_loop(0, 3, scatter, 0)

    y_iota = lax.broadcasted_iota(jnp.int32, (rows, cols), 0)
    z_iota = lax.broadcasted_iota(jnp.int32, (rows, cols), 1)
    y_first, y_last = y_iota == 0, y_iota == rows - 1
    z_first, z_last = z_iota == 0, z_iota == cols - 1

    def ahead_y(f):
        return jnp.where(y_last, 0.0, pltpu.roll(f, rows - 1, 0)) - f

    def ahead_z(f):
        return jnp.where(z_last, 0.0, pltpu.roll(f, cols - 1, 1)) - f

    def behind_y(f):
        return f - jnp.where(y_first, 0.0, pltpu.roll(f, 1, 0))

    def behind_z(f):
        return f - jnp.where(z_first, 0.0, pltpu.roll(f, 1, 1))

    def faces(k, part, p):
        ex, ey, ez = (basis[k, 3 * part + q, p] for q in range(3))
        ey_next, ez_next = basis[k, 3 * part + 1, p + 1], basis[k, 3 * part + 2, p + 1]
        keep = jnp.where(p < depth, keep_low, 1.0)
        hx = ahead_y(ez) - ahead_z(ey)
        hy = (ahead_z(ex) - (ez_next - ez)) * keep
        hz = ((ey_next - ey) - ahead_y(ex)) * keep
        return hx, hy, hz, (ex, ey, ez)

    for k in range(ITERS):
        weight = (1.0 if k == 0 else 2.0) / RADIUS

        def plane(p, carried):
            keep = jnp.where(p >= 2 * depth, keep_high, 1.0)
            result = []
            for part in range(2):
                hy_before, hz_before = carried[2 * part], carried[2 * part + 1]
                hx, hy, hz, edges = faces(k, part, p)
                curls = (
                    behind_y(hz) - behind_z(hy),
                    behind_z(hx) - (hz - hz_before),
                    (hy - hy_before) - behind_y(hx),
                )
                for q in range(3):
                    other = coupling[q, p - (ITERS - halo)] * basis[k, 3 * (1 - part) + q, p]
                    if k == 0:
                        other = 0.5 * other
                    shifted = weight * (curls[q] - CENTRE * edges[q])
                    new = shifted + other if part == 0 else shifted - other
                    if k > 0:
                        new = new - basis[k - 1, 3 * part + q, p]
                    basis[k + 1, 3 * part + q, p] = new * keep
                result += [hy, hz]
            return tuple(result)

        start = []
        for part in range(2):
            _, hy, hz, _ = faces(k, part, k)
            start += [hy, hz]
        lax.fori_loop(k + 1, 3 * depth - k - 1, plane, tuple(start))

    def plane_forms(p, sums):
        sums = list(sums)
        for q in range(3):
            re = [basis[k, q, p] for k in range(BASIS)]
            im = [basis[k, 3 + q, p] for k in range(BASIS)]
            for f, (i, j) in enumerate(PAIRS):
                real = re[i] * re[j] - im[i] * im[j]
                imag = re[i] * im[j] + im[i] * re[j] if i != j else 2.0 * (re[i] * im[i])
                for half, term in ((0, real), (1, imag)):
                    sums[2 * f + half] = sums[2 * f + half] + jnp.sum(term.reshape(rows // 8, 8, cols), axis=0)
        return tuple(sums)

    zero = jnp.zeros((8, cols), jnp.float32)
    sums = lax.fori_loop(depth, 2 * depth, plane_forms, (zero,) * (2 * FORMS))
    for f in range(2 * FORMS):
        forms_ref[f : f + 1] = jnp.sum(sums[f], axis=0, keepdims=True)
    own_ref[...] = basis[:, :, depth : 2 * depth]


def c_add(a, b):
    return a[0] + b[0], a[1] + b[1]


def c_sub(a, b):
    return a[0] - b[0], a[1] - b[1]


def c_mul(a, b):
    return a[0] * b[0] - a[1] * b[1], a[0] * b[1] + a[1] * b[0]


def c_scale(s, a):
    return s * a[0], s * a[1]


def c_div(a, b):
    inverse = 1.0 / (b[0] * b[0] + b[1] * b[1])
    return (a[0] * b[0] + a[1] * b[1]) * inverse, (a[1] * b[0] - a[0] * b[1]) * inverse


def step_scalars(moments):
    resid = list(moments)
    direc = list(moments)
    none = (jnp.zeros_like(moments[0][0]),) * 2
    one = (jnp.ones_like(moments[0][0]), jnp.zeros_like(moments[0][0]))
    resid_at = [one] + [none] * ITERS
    direc_at = [one] + [none] * ITERS
    field_at = [none] * BASIS
    rho = moments[0]
    for n in range(ITERS):
        applied = [c_add(c_scale(CENTRE, direc[0]), c_scale(RADIUS, direc[1]))]
        for l in range(1, len(direc) - 1):
            near = c_scale(RADIUS / 2, c_add(direc[l + 1], direc[l - 1]))
            applied.append(c_add(c_scale(CENTRE, direc[l]), near))
        step = c_div(rho, c_mul(direc_at[n], applied[n]))
        applied_at = [c_scale(CENTRE, direc_at[j]) if j <= n else none for j in range(BASIS)]
        for j in range(n + 1):
            if j == 0:
                applied_at[1] = c_add(applied_at[1], c_scale(RADIUS, direc_at[0]))
            else:
                spread = c_scale(RADIUS / 2, direc_at[j])
                applied_at[j + 1] = c_add(applied_at[j + 1], spread)
                applied_at[j - 1] = c_add(applied_at[j - 1], spread)
        for j in range(n + 1):
            field_at[j] = c_add(field_at[j], c_mul(step, direc_at[j]))
        for j in range(n + 2):
            resid_at[j] = c_sub(resid_at[j], c_mul(step, applied_at[j]))
        if n + 1 < ITERS:
            resid = [c_sub(resid[l], c_mul(step, applied[l])) for l in range(len(applied))]
            rho_next = c_mul(resid_at[n + 1], resid[n + 1])
            ratio = c_div(rho_next, rho)
            direc = [c_add(resid[l], c_mul(ratio, direc[l])) for l in range(len(resid))]
            direc_at = [
                c_add(resid_at[j], c_mul(ratio, direc_at[j])) if j <= n else resid_at[j] for j in range(BASIS)
            ]
            rho = rho_next
    return field_at, resid_at


def combine_kernel(forms_ref, own_ref, field_ref, resid_ref):
    totals = jnp.sum(forms_ref[...], axis=1, keepdims=True)
    forms = [(totals[2 * f : 2 * f + 1], totals[2 * f + 1 : 2 * f + 2]) for f in range(FORMS)]
    moments = forms[:2]
    for f in range(2, FORMS):
        moments.append(c_sub(c_scale(2.0, forms[f]), forms[f % 2]))
    field_at, resid_at = step_scalars(moments)
    depth, rows, cols = field_ref.shape[1:]

    def spread(factors):
        return [tuple(jnp.broadcast_to(half, (rows, cols)) for half in factor) for factor in factors]

    field_at, resid_at = spread(field_at[:ITERS]), spread(resid_at)

    def plane(p, _):
        for q in range(3):
            re = [own_ref[k, q, p] for k in range(BASIS)]
            im = [own_ref[k, 3 + q, p] for k in range(BASIS)]
            for out_ref, factors in ((field_ref, field_at), (resid_ref, resid_at)):
                real = sum(f[0] * re[k] - f[1] * im[k] for k, f in enumerate(factors))
                imag = sum(f[0] * im[k] + f[1] * re[k] for k, f in enumerate(factors))
                out_ref[q, p] = real
                out_ref[3 + q, p] = imag
        return 0

    lax.fori_loop(0, depth, plane, 0)


def params():
    return pltpu.CompilerParams(vmem_limit_bytes=VMEM_LIMIT)


def per_device(n, site_owner, site_cell, stencil_code, site_residual, conductivity, omega):
    depth, rows, cols = conductivity.shape[1:]
    sites = site_owner.shape[0]
    cap = 2 * sites // n
    half = cap // 2
    halo = ITERS - 1
    low = lax.ppermute(conductivity[:, depth - halo :], "gx", [(i, i + 1) for i in range(n - 1)])
    high = lax.ppermute(conductivity[:, :halo], "gx", [(i + 1, i) for i in range(n - 1)])

    packed = pl.pallas_call(
        functools.partial(bin_kernel, n, half, rows, cols, depth // 2),
        out_shape=jax.ShapeDtypeStruct((n * 3 * half, 2 * 8 * 8), jnp.float32),
        in_specs=[vmem()] * 4,
        out_specs=vmem(),
        compiler_params=params(),
        name="bin_sites",
    )(site_owner.reshape(1, sites), site_cell, stencil_code, site_residual)
    recv = lax.all_to_all(packed.reshape(n, 3 * half, -1), "gx", 0, 0)
    if half % 8:
        recv = recv.reshape(n, 3, half, -1).transpose(1, 0, 2, 3).reshape(1, 3 * n * half, -1)

    slots = n * cap
    forms, own = pl.pallas_call(
        functools.partial(field_kernel, n),
        out_shape=(
            jax.ShapeDtypeStruct((2 * FORMS, cols), jnp.float32),
            jax.ShapeDtypeStruct((BASIS, 6, depth, rows, cols), jnp.float32),
        ),
        in_specs=[vmem()] * 4 + [smem()],
        out_specs=(vmem(), vmem()),
        scratch_shapes=[
            pltpu.VMEM((BASIS, 6, 3 * depth, rows, cols), jnp.float32),
            pltpu.VMEM((3, 2 * halo + depth, rows, cols), jnp.float32),
            pltpu.VMEM((2 * 6 * depth // 2 * rows, 8 * slots), jnp.bfloat16),
            pltpu.VMEM((2 * cols, 8 * slots), jnp.bfloat16),
        ],
        compiler_params=params(),
        name="krylov_basis",
    )(recv, conductivity, low, high, omega)

    bit = 1
    while bit < n:
        forms = forms + lax.ppermute(forms, "gx", [(i, i ^ bit) for i in range(n)])
        bit *= 2

    return pl.pallas_call(
        combine_kernel,
        out_shape=(jax.ShapeDtypeStruct((6, depth, rows, cols), jnp.float32),) * 2,
        in_specs=[vmem()] * 2,
        out_specs=(vmem(), vmem()),
        compiler_params=params(),
        name="combine_basis",
    )(forms, own)


def solution(mesh):
    placed = (
        P(("period", "gx")),
        P(None, ("period", "gx")),
        P(None, ("period", "gx")),
        P(None, None, ("period", "gx")),
        P(None, "gx", None, None),
        P("period"),
    )
    return jax.shard_map(
        functools.partial(per_device, mesh.shape["gx"]),
        mesh=mesh,
        in_specs=placed,
        out_specs=(P("period", "gx", None, None), P("period", "gx", None, None)),
        check_vma=False,
    )
```

```python
import functools

import jax
import jax.numpy as jnp
from jax import lax
from jax.experimental import pallas as pl
from jax.experimental.pallas import tpu as pltpu
from jax.sharding import PartitionSpec as P

ITERS = 4
CENTRE = 5.0
RADIUS = 5.0
BASIS = ITERS + 1
FORMS = 2 * ITERS
PAIRS = [(i // 2, (i + 1) // 2) for i in range(FORMS)]
HALO = ITERS - 1
VMEM_LIMIT = 40 * 1024 * 1024
FULL_LIMIT = 62 * 1024 * 1024
CONTRACT_LANES = (((1,), (1,)), ((), ()))


def vmem():
    return pl.BlockSpec(memory_space=pltpu.VMEM)


def hbm():
    return pl.BlockSpec(memory_space=pltpu.HBM)


def split_bf16(x):
    high = x.astype(jnp.bfloat16)
    return high, (x - high.astype(jnp.float32)).astype(jnp.bfloat16)


def bin_kernel(n, half, rows, cols, half_depth, *refs):
    count = len(refs) // 2 - 1
    sources, out_ref, held, arrived = refs[:count], refs[count], refs[count + 1 : -1], refs[-1]
    copies = [pltpu.make_async_copy(sources[i], held[i], arrived.at[i]) for i in range(count)]
    for copy in copies:
        copy.start()
    for copy in copies:
        copy.wait()
    owner_ref, cell_ref, code_ref, value_ref = held
    sites = owner_ref.shape[1]
    owner = owner_ref[...]
    code = code_ref[...]
    dx = (code >= 9).astype(jnp.int32) + (code >= 18).astype(jnp.int32)
    rest = code - 9 * dx
    dy = (rest >= 3).astype(jnp.int32) + (rest >= 6).astype(jnp.int32)
    dz = rest - 3 * dy
    x = cell_ref[0:1] + dx
    y = cell_ref[1:2] + dy
    z = cell_ref[2:3] + dz
    upper = (x >= half_depth).astype(jnp.int32)
    folds = rows // 8
    row = (x - half_depth * upper) * rows + (y % folds) * 8 + y // folds
    lane = z + cols * upper
    channels, points = value_ref.shape[0], value_ref.shape[1]
    data = jnp.concatenate(
        [value_ref[...].reshape(channels * points, sites), row.astype(jnp.float32), lane.astype(jnp.float32)],
        axis=0,
    )
    blank = jnp.zeros_like(data)

    named = lax.broadcasted_iota(jnp.int32, (n, sites), 0) == owner
    earlier = lax.broadcasted_iota(jnp.int32, (sites, sites), 0) < lax.broadcasted_iota(
        jnp.int32, (sites, sites), 1
    )
    named_f = named.astype(jnp.float32)
    counts = jnp.dot(
        named_f.astype(jnp.bfloat16),
        earlier.astype(jnp.float32).astype(jnp.bfloat16),
        preferred_element_type=jnp.float32,
    )
    rank = jnp.sum(counts * named_f, axis=0, keepdims=True).astype(jnp.int32)
    second = rank >= half
    place = jnp.where(second, rank - half, rank)

    slot = lax.broadcasted_iota(jnp.int32, (out_ref.shape[0], sites), 0)
    hit = jnp.zeros(slot.shape, jnp.bool_)
    for j in range(3):
        hit = hit | (slot == ((owner - j + 1) * 3 + j) * half + place)
    total = jnp.zeros(out_ref.shape, jnp.float32)
    for part, stacked in (
        (jnp.logical_not(second), [data, blank]),
        (second, [blank, data]),
    ):
        chosen = jnp.where(hit & part, 1.0, 0.0).astype(jnp.bfloat16)
        for piece in split_bf16(jnp.concatenate(stacked, axis=0)):
            total = total + lax.dot_general(
                chosen, piece, CONTRACT_LANES, preferred_element_type=jnp.float32
            )
    out_ref[...] = total


def field_kernel(n, recv_ref, coupling, forms_ref, basis, left, right):
    depth, folds, cols = basis.shape[2] // 3, basis.shape[3], basis.shape[5]
    rows = 8 * folds
    half_depth = depth // 2
    channels = 6
    points = 8
    group = recv_ref.shape[1] // 3
    me = lax.axis_index("gx")
    keep_low = jnp.where(me > 0, 1.0, 0.0).astype(jnp.float32)
    keep_high = jnp.where(me < n - 1, 1.0, 0.0).astype(jnp.float32)

    row_count = half_depth * rows
    lane_count = 2 * cols
    slots = 2 * recv_ref.shape[0] * group
    width = (channels + 2) * points
    row_iota = lax.broadcasted_iota(jnp.int32, (row_count, slots), 0)
    lane_iota = lax.broadcasted_iota(jnp.int32, (lane_count, slots), 0)

    def scatter(j, _):
        packed = recv_ref[:, pl.ds(pl.multiple_of(j * group, 8), group), :].reshape(slots // 2, 2 * width)
        turned = packed.T
        table = jnp.concatenate([turned[:width], turned[width:]], axis=1)
        table_high = table.astype(jnp.bfloat16).astype(jnp.float32)
        table_low = table - table_high
        cell_row = table[channels * points : (channels + 1) * points].astype(jnp.int32)
        cell_lane = table[(channels + 1) * points :].astype(jnp.int32)
        for k in range(points):
            span = slice(k * slots, (k + 1) * slots)
            right[:, span] = jnp.where(lane_iota == cell_lane[k : k + 1], 1.0, 0.0).astype(jnp.bfloat16)
            mask = row_iota == cell_row[k : k + 1]
            for c in range(channels):
                at = c * points + k
                for piece, part in enumerate((table_high, table_low)):
                    first = (piece * channels + c) * row_count
                    left[first : first + row_count, span] = jnp.where(mask, part[at : at + 1], 0.0).astype(
                        jnp.bfloat16
                    )
        both = lax.dot_general(left[...], right[...], CONTRACT_LANES, preferred_element_type=jnp.float32)
        summed = both[: channels * row_count] + both[channels * row_count :]
        for c in range(channels):
            for x in range(depth):
                first = c * row_count + (x % half_depth) * rows
                lanes = slice((x // half_depth) * cols, (x // half_depth + 1) * cols)
                basis[1, c, j * depth + x] = summed[first : first + rows, lanes].reshape(folds, 8, cols)
        return 0

    lax.fori_loop(0, 3, scatter, 0)

    basis[0] = jnp.zeros(basis.shape[1:], jnp.float32)
    s_iota = lax.broadcasted_iota(jnp.int32, (8, cols), 0)
    z_iota = lax.broadcasted_iota(jnp.int32, (folds, 8, cols), 2)
    s_first, s_last = s_iota == 0, s_iota == 7
    z_first, z_last = z_iota == 0, z_iota == cols - 1

    def ahead_y(f):
        wrapped = jnp.where(s_last, 0.0, pltpu.roll(f[0], 7, 0))
        return jnp.concatenate([f[1:], wrapped[None]], axis=0) - f

    def ahead_z(f):
        return jnp.where(z_last, 0.0, pltpu.roll(f, cols - 1, 2)) - f

    def behind_y(f):
        wrapped = jnp.where(s_first, 0.0, pltpu.roll(f[folds - 1], 1, 0))
        return f - jnp.concatenate([wrapped[None], f[:-1]], axis=0)

    def behind_z(f):
        return f - jnp.where(z_first, 0.0, pltpu.roll(f, 1, 2))

    def faces(k, part, p):
        ex, ey, ez = (basis[k, 3 * part + q, p] for q in range(3))
        ey_next, ez_next = basis[k, 3 * part + 1, p + 1], basis[k, 3 * part + 2, p + 1]
        hx = ahead_y(ez) - ahead_z(ey)
        hy = ahead_z(ex) - (ez_next - ez)
        hz = (ey_next - ey) - ahead_y(ex)
        return hx, hy, hz, (ex, ey, ez)

    weight = 2.0 / RADIUS
    centre = 2.0 * CENTRE / RADIUS

    def plane(k, p, carried):
        result = []
        for part in range(2):
            hy_before, hz_before = carried[2 * part], carried[2 * part + 1]
            hx, hy, hz, edges = faces(k, part, p)
            curls = (
                behind_y(hz) - behind_z(hy),
                behind_z(hx) - (hz - hz_before),
                (hy - hy_before) - behind_y(hx),
            )
            for q in range(3):
                other = coupling[q, p - (depth - HALO)] * basis[k, 3 * (1 - part) + q, p]
                rest = centre * edges[q] + basis[k - 1, 3 * part + q, p]
                new = weight * curls[q] - rest
                basis[k + 1, 3 * part + q, p] = new + other if part == 0 else new - other
            result += [hy, hz]
        return tuple(result)

    def apply(k, _):
        start = []
        for part in range(2):
            _, hy, hz, _ = faces(k, part, k - 1)
            start += [hy, hz]

        def pair(i, carried):
            p = k + 2 * i
            for _ in range(2):
                keep = jnp.where(p == depth, keep_low, 1.0)
                carried = plane(k, p, tuple(keep * f for f in carried))
                p = p + 1
            return carried

        lax.fori_loop(0, (3 * depth - 2 * k) // 2, pair, tuple(start))
        for c in range(channels):
            basis[k + 1, c, 2 * depth] = basis[k + 1, c, 2 * depth] * keep_high
        return 0

    lax.fori_loop(1, BASIS, apply, 0)

    def plane_forms(p, sums):
        sums = list(sums)
        for q in range(3):
            re = [basis[k + 1, q, p] for k in range(BASIS)]
            im = [basis[k + 1, 3 + q, p] for k in range(BASIS)]
            for f, (i, j) in enumerate(PAIRS):
                real = re[i] * re[j] - im[i] * im[j]
                imag = re[i] * im[j] + im[i] * re[j] if i != j else 2.0 * (re[i] * im[i])
                for half, term in ((0, real), (1, imag)):
                    sums[2 * f + half] = sums[2 * f + half] + jnp.sum(term, axis=0)
        return tuple(sums)

    zero = jnp.zeros((8, cols), jnp.float32)
    sums = lax.fori_loop(depth, 2 * depth, plane_forms, (zero,) * (2 * FORMS))
    folded = jnp.concatenate([jnp.sum(total, axis=0, keepdims=True) for total in sums], axis=0)
    totals = jnp.sum(folded, axis=1, keepdims=True)
    diagonal = lax.broadcasted_iota(jnp.int32, folded.shape, 0) == lax.broadcasted_iota(jnp.int32, folded.shape, 1)
    line = jnp.sum(jnp.where(diagonal, totals, 0.0), axis=0, keepdims=True)
    forms_ref[...] = jnp.broadcast_to(line, forms_ref.shape)


def c_add(a, b):
    return a[0] + b[0], a[1] + b[1]


def c_sub(a, b):
    return a[0] - b[0], a[1] - b[1]


def c_mul(a, b):
    return a[0] * b[0] - a[1] * b[1], a[0] * b[1] + a[1] * b[0]


def c_scale(s, a):
    return s * a[0], s * a[1]


def c_div(a, b):
    inverse = 1.0 / (b[0] * b[0] + b[1] * b[1])
    return (a[0] * b[0] + a[1] * b[1]) * inverse, (a[1] * b[0] - a[0] * b[1]) * inverse


def step_scalars(moments):
    resid = list(moments)
    direc = list(moments)
    none = (jnp.zeros_like(moments[0][0]),) * 2
    one = (jnp.ones_like(moments[0][0]), jnp.zeros_like(moments[0][0]))
    resid_at = [one] + [none] * ITERS
    direc_at = [one] + [none] * ITERS
    field_at = [none] * BASIS
    rho = moments[0]
    for n in range(ITERS):
        applied = [c_add(c_scale(CENTRE, direc[0]), c_scale(RADIUS / 2, direc[1]))]
        for l in range(1, len(direc) - 1):
            near = c_scale(RADIUS / 2, c_add(direc[l + 1], direc[l - 1]))
            applied.append(c_add(c_scale(CENTRE, direc[l]), near))
        step = c_div(rho, c_mul(direc_at[n], applied[n]))
        applied_at = [c_scale(CENTRE, direc_at[j]) if j <= n else none for j in range(BASIS)]
        for j in range(n + 1):
            spread = c_scale(RADIUS / 2, direc_at[j])
            applied_at[j + 1] = c_add(applied_at[j + 1], spread)
            if j > 0:
                applied_at[j - 1] = c_add(applied_at[j - 1], spread)
        for j in range(n + 1):
            field_at[j] = c_add(field_at[j], c_mul(step, direc_at[j]))
        for j in range(n + 2):
            resid_at[j] = c_sub(resid_at[j], c_mul(step, applied_at[j]))
        if n + 1 < ITERS:
            resid = [c_sub(resid[l], c_mul(step, applied[l])) for l in range(len(applied))]
            rho_next = c_mul(resid_at[n + 1], resid[n + 1])
            ratio = c_div(rho_next, rho)
            direc = [c_add(resid[l], c_mul(ratio, direc[l])) for l in range(len(resid))]
            direc_at = [
                c_add(resid_at[j], c_mul(ratio, direc_at[j])) if j <= n else resid_at[j] for j in range(BASIS)
            ]
            rho = rho_next
    return field_at, resid_at


def combine_kernel(forms_ref, basis, field_ref, resid_ref):
    depth, folds, cols = basis.shape[2] // 3, basis.shape[3], basis.shape[5]
    totals = jnp.broadcast_to(jnp.sum(forms_ref[...], axis=0, keepdims=True), (8, cols))
    lane = lax.broadcasted_iota(jnp.int32, (8, cols), 1)
    sums = [
        jnp.broadcast_to(jnp.sum(jnp.where(lane == i, totals, 0.0), axis=1, keepdims=True), (8, cols))
        for i in range(2 * FORMS)
    ]
    forms = [(sums[2 * f], sums[2 * f + 1]) for f in range(FORMS)]
    moments = forms[:2] + [c_sub(forms[f], forms[f - 2]) for f in range(2, FORMS)]
    field_at, resid_at = step_scalars(moments)

    def plane(p, _):
        for q in range(3):
            for j in range(folds):
                re = [basis[k + 1, q, depth + p, j] for k in range(BASIS)]
                im = [basis[k + 1, 3 + q, depth + p, j] for k in range(BASIS)]
                rows = pl.ds(j, 8, stride=folds)
                for out_ref, factors in ((field_ref, field_at[:ITERS]), (resid_ref, resid_at)):
                    out_ref[q, p, rows] = sum(f[0] * re[k] - f[1] * im[k] for k, f in enumerate(factors))
                    out_ref[3 + q, p, rows] = sum(f[0] * im[k] + f[1] * re[k] for k, f in enumerate(factors))
        return 0

    lax.fori_loop(0, depth, plane, 0)


def params(limit=VMEM_LIMIT):
    return pltpu.CompilerParams(vmem_limit_bytes=limit)


def krylov(n, recv, coupling):
    depth, folds, cols = coupling.shape[1] - 2 * HALO, coupling.shape[2], coupling.shape[4]
    slots = 2 * recv.shape[0] * recv.shape[1] // 3
    return pl.pallas_call(
        functools.partial(field_kernel, n),
        out_shape=(
            jax.ShapeDtypeStruct((n, cols), jnp.float32),
            jax.ShapeDtypeStruct((BASIS + 1, 6, 3 * depth, folds, 8, cols), jnp.float32),
        ),
        in_specs=[vmem()] * 2,
        out_specs=(vmem(), vmem()),
        scratch_shapes=[
            pltpu.VMEM((2 * 6 * depth // 2 * 8 * folds, 8 * slots), jnp.bfloat16),
            pltpu.VMEM((2 * cols, 8 * slots), jnp.bfloat16),
        ],
        compiler_params=params(),
        name="krylov_basis",
    )(recv, coupling)


def per_device(n, site_owner, site_cell, stencil_code, site_residual, conductivity, omega):
    depth, rows, cols = conductivity.shape[1:]
    sites = site_owner.shape[0]
    cap = 2 * sites // n
    half = cap // 2
    listed = (site_owner.reshape(1, sites), site_cell, stencil_code, site_residual)
    packed = pl.pallas_call(
        functools.partial(bin_kernel, n, half, rows, cols, depth // 2),
        out_shape=jax.ShapeDtypeStruct((n * 3 * half, 2 * 8 * 8), jnp.float32),
        in_specs=[hbm()] * len(listed),
        out_specs=vmem(),
        scratch_shapes=[pltpu.VMEM(x.shape, x.dtype) for x in listed] + [pltpu.SemaphoreType.DMA((len(listed),))],
        compiler_params=params(FULL_LIMIT),
        name="bin_sites",
    )(*listed)
    mate = lax.ppermute(conductivity, "gx", [(i, i ^ 1) for i in range(n)])
    other = lax.ppermute(conductivity, "gx", [(i, ((i + 1) ^ 1) - 1) for i in range(1, n - 1)])
    even = lax.axis_index("gx") % 2 == 0
    below = jnp.where(even, other[:, depth - HALO :], mate[:, depth - HALO :])
    above = jnp.where(even, mate[:, :HALO], other[:, :HALO])
    coupling = jnp.concatenate([below, conductivity, above], axis=1) * (omega[0] * (2.0 / RADIUS))
    coupling = coupling.reshape(3, 2 * HALO + depth, 8, rows // 8, cols).swapaxes(2, 3)
    recv = lax.all_to_all(packed.reshape(n, 3 * half, -1), "gx", 0, 0)
    if half % 8:
        recv = recv.reshape(n, 3, half, -1).transpose(1, 0, 2, 3).reshape(1, 3 * n * half, -1)

    forms, basis = krylov(n, recv, coupling)

    forms = lax.all_to_all(forms, "gx", 0, 0, tiled=True)

    return pl.pallas_call(
        combine_kernel,
        out_shape=(jax.ShapeDtypeStruct((6, depth, rows, cols), jnp.float32),) * 2,
        in_specs=[vmem()] * 2,
        out_specs=(vmem(), vmem()),
        compiler_params=params(),
        name="combine_basis",
    )(forms, basis)


def solution(mesh):
    placed = (
        P(("period", "gx")),
        P(None, ("period", "gx")),
        P(None, ("period", "gx")),
        P(None, None, ("period", "gx")),
        P(None, "gx", None, None),
        P("period"),
    )
    return jax.shard_map(
        functools.partial(per_device, mesh.shape["gx"]),
        mesh=mesh,
        in_specs=placed,
        out_specs=(P("period", "gx", None, None), P("period", "gx", None, None)),
        check_vma=False,
    )
```

```python
import functools

import jax
import jax.numpy as jnp
from jax import lax
from jax.experimental import pallas as pl
from jax.experimental.pallas import tpu as pltpu
from jax.sharding import PartitionSpec as P

ITERS = 4
CENTRE = 5.0
RADIUS = 5.0
BASIS = ITERS + 1
FORMS = 2 * ITERS
PAIRS = [(i // 2, (i + 1) // 2) for i in range(FORMS)]
HALO = ITERS - 1
VMEM_LIMIT = 40 * 1024 * 1024
FULL_LIMIT = 62 * 1024 * 1024
CONTRACT_LANES = (((1,), (1,)), ((), ()))


def vmem():
    return pl.BlockSpec(memory_space=pltpu.VMEM)


def smem():
    return pl.BlockSpec(memory_space=pltpu.SMEM)


def hbm():
    return pl.BlockSpec(memory_space=pltpu.HBM)


def split_bf16(x):
    high = x.astype(jnp.bfloat16)
    return high, (x - high.astype(jnp.float32)).astype(jnp.bfloat16)


def bin_kernel(n, half, rows, cols, half_depth, *refs):
    count = len(refs) // 2 - 1
    sources, out_ref, held, arrived = refs[:count], refs[count], refs[count + 1 : -1], refs[-1]
    copies = [pltpu.make_async_copy(sources[i], held[i], arrived.at[i]) for i in range(count)]
    for copy in copies:
        copy.start()
    for copy in copies:
        copy.wait()
    owner_ref, cell_ref, code_ref, value_ref = held
    sites = owner_ref.shape[1]
    owner = owner_ref[...]
    code = code_ref[...]
    dx = (code >= 9).astype(jnp.int32) + (code >= 18).astype(jnp.int32)
    rest = code - 9 * dx
    dy = (rest >= 3).astype(jnp.int32) + (rest >= 6).astype(jnp.int32)
    dz = rest - 3 * dy
    x = cell_ref[0:1] + dx
    y = cell_ref[1:2] + dy
    z = cell_ref[2:3] + dz
    upper = (x >= half_depth).astype(jnp.int32)
    folds = rows // 8
    row = (x - half_depth * upper) * rows + (y % folds) * 8 + y // folds
    lane = z + cols * upper
    channels, points = value_ref.shape[0], value_ref.shape[1]
    data = jnp.concatenate(
        [value_ref[...].reshape(channels * points, sites), row.astype(jnp.float32), lane.astype(jnp.float32)],
        axis=0,
    )
    blank = jnp.zeros_like(data)

    named = lax.broadcasted_iota(jnp.int32, (n, sites), 0) == owner
    earlier = lax.broadcasted_iota(jnp.int32, (sites, sites), 0) < lax.broadcasted_iota(
        jnp.int32, (sites, sites), 1
    )
    named_f = named.astype(jnp.float32)
    counts = jnp.dot(
        named_f.astype(jnp.bfloat16),
        earlier.astype(jnp.float32).astype(jnp.bfloat16),
        preferred_element_type=jnp.float32,
    )
    rank = jnp.sum(counts * named_f, axis=0, keepdims=True).astype(jnp.int32)
    second = rank >= half
    place = jnp.where(second, rank - half, rank)

    slot = lax.broadcasted_iota(jnp.int32, (out_ref.shape[0], sites), 0)
    hit = jnp.zeros(slot.shape, jnp.bool_)
    for j in range(3):
        hit = hit | (slot == ((owner - j + 1) * 3 + j) * half + place)
    total = jnp.zeros(out_ref.shape, jnp.float32)
    for part, stacked in (
        (jnp.logical_not(second), [data, blank]),
        (second, [blank, data]),
    ):
        chosen = jnp.where(hit & part, 1.0, 0.0).astype(jnp.bfloat16)
        for piece in split_bf16(jnp.concatenate(stacked, axis=0)):
            total = total + lax.dot_general(
                chosen, piece, CONTRACT_LANES, preferred_element_type=jnp.float32
            )
    out_ref[...] = total


def scatter_kernel(recv_ref, cond_hbm, omega_ref, basis, mine_ref, left, right, cond_ref, arrived):
    conductivity = pltpu.make_async_copy(cond_hbm, cond_ref, arrived)
    conductivity.start()
    depth, folds, cols = basis.shape[2] // 3, basis.shape[3], basis.shape[5]
    rows = 8 * folds
    half_depth = depth // 2
    channels = 6
    points = 8
    group = recv_ref.shape[1] // 3
    basis[0] = jnp.zeros(basis.shape[1:], jnp.float32)
    row_count = half_depth * rows
    lane_count = 2 * cols
    slots = 2 * recv_ref.shape[0] * group
    width = (channels + 2) * points
    row_iota = lax.broadcasted_iota(jnp.int32, (row_count, slots), 0)
    lane_iota = lax.broadcasted_iota(jnp.int32, (lane_count, slots), 0)

    def scatter(j, _):
        packed = recv_ref[:, pl.ds(pl.multiple_of(j * group, 8), group), :].reshape(slots // 2, 2 * width)
        turned = packed.T
        table = jnp.concatenate([turned[:width], turned[width:]], axis=1)
        table_high = table.astype(jnp.bfloat16).astype(jnp.float32)
        table_low = table - table_high
        cell_row = table[channels * points : (channels + 1) * points].astype(jnp.int32)
        cell_lane = table[(channels + 1) * points :].astype(jnp.int32)
        for k in range(points):
            span = slice(k * slots, (k + 1) * slots)
            right[:, span] = jnp.where(lane_iota == cell_lane[k : k + 1], 1.0, 0.0).astype(jnp.bfloat16)
            mask = row_iota == cell_row[k : k + 1]
            for c in range(channels):
                at = c * points + k
                for piece, part in enumerate((table_high, table_low)):
                    first = (piece * channels + c) * row_count
                    left[first : first + row_count, span] = jnp.where(mask, part[at : at + 1], 0.0).astype(
                        jnp.bfloat16
                    )
        both = lax.dot_general(left[...], right[...], CONTRACT_LANES, preferred_element_type=jnp.float32)
        summed = both[: channels * row_count] + both[channels * row_count :]
        for c in range(channels):
            for x in range(depth):
                first = c * row_count + (x % half_depth) * rows
                lanes = slice((x // half_depth) * cols, (x // half_depth + 1) * cols)
                basis[1, c, j * depth + x] = summed[first : first + rows, lanes].reshape(folds, 8, cols)
        return 0

    lax.fori_loop(0, 3, scatter, 0)

    conductivity.wait()
    scale = omega_ref[0] * (2.0 / RADIUS)
    for q in range(3):
        for j in range(folds):
            for x in range(depth):
                mine_ref[q, x, j] = cond_ref[q, x, pl.ds(j, 8, stride=folds)] * scale


def field_kernel(n, mate_ref, other_ref, mine_ref, omega_ref, _, forms_ref, basis, coupling):
    depth, folds, cols = basis.shape[2] // 3, basis.shape[3], basis.shape[5]
    channels = 6
    me = lax.axis_index("gx")
    keep_low = jnp.where(me > 0, 1.0, 0.0).astype(jnp.float32)
    keep_high = jnp.where(me < n - 1, 1.0, 0.0).astype(jnp.float32)

    scale = omega_ref[0] * (2.0 / RADIUS)
    even = me % 2 == 0
    for q in range(3):
        coupling[q, HALO : HALO + depth] = mine_ref[q]
        for j in range(folds):
            fold = pl.ds(j, 8, stride=folds)
            for i in range(HALO):
                below, above = depth - HALO + i, i
                coupling[q, i, j] = jnp.where(even, other_ref[q, below, fold], mate_ref[q, below, fold]) * scale
                coupling[q, HALO + depth + i, j] = (
                    jnp.where(even, mate_ref[q, above, fold], other_ref[q, above, fold]) * scale
                )

    s_iota = lax.broadcasted_iota(jnp.int32, (8, cols), 0)
    z_iota = lax.broadcasted_iota(jnp.int32, (folds, 8, cols), 2)
    s_first, s_last = s_iota == 0, s_iota == 7
    z_first, z_last = z_iota == 0, z_iota == cols - 1

    def ahead_y(f):
        wrapped = jnp.where(s_last, 0.0, pltpu.roll(f[0], 7, 0))
        return jnp.concatenate([f[1:], wrapped[None]], axis=0) - f

    def ahead_z(f):
        return jnp.where(z_last, 0.0, pltpu.roll(f, cols - 1, 2)) - f

    def behind_y(f):
        wrapped = jnp.where(s_first, 0.0, pltpu.roll(f[folds - 1], 1, 0))
        return f - jnp.concatenate([wrapped[None], f[:-1]], axis=0)

    def behind_z(f):
        return f - jnp.where(z_first, 0.0, pltpu.roll(f, 1, 2))

    weight = 2.0 / RADIUS
    centre = 2.0 * CENTRE / RADIUS

    def edges(k, p):
        return [basis[k, c, p] for c in range(channels)]

    def faces(here, there, part):
        ex, ey, ez = here[3 * part : 3 * part + 3]
        ey_next, ez_next = there[3 * part + 1], there[3 * part + 2]
        hx = ahead_y(ez) - ahead_z(ey)
        hy = ahead_z(ex) - (ez_next - ez)
        hz = (ey_next - ey) - ahead_y(ex)
        return hx, hy, hz

    def plane(here, there, older, coupled, carried):
        new, result = [], []
        for part in range(2):
            hy_before, hz_before = carried[2 * part], carried[2 * part + 1]
            hx, hy, hz = faces(here, there, part)
            curls = (
                behind_y(hz) - behind_z(hy),
                behind_z(hx) - (hz - hz_before),
                (hy - hy_before) - behind_y(hx),
            )
            for q in range(3):
                other = coupled[q] * here[3 * (1 - part) + q]
                value = weight * curls[q] - (centre * here[3 * part + q] + older[3 * part + q])
                new.append(value + other if part == 0 else value - other)
            result += [hy, hz]
        return new, tuple(result)

    def apply(k, _):
        first, second = edges(k, k - 1), edges(k, k)
        start = []
        for part in range(2):
            start += faces(first, second, part)[1:]

        def step(i, carried):
            p = k + 2 * i
            fields = [edges(k, p + d) for d in range(2 + 1)]
            older = [edges(k - 1, p + d) for d in range(2)]
            coupled = [[coupling[q, p + d - (depth - HALO)] for q in range(3)] for d in range(2)]
            results = []
            for d in range(2):
                keep = jnp.where(p + d == depth, keep_low, 1.0)
                carried = tuple(keep * f for f in carried)
                new, carried = plane(fields[d], fields[d + 1], older[d], coupled[d], carried)
                results.append(new)
            for d in range(2):
                for c in range(channels):
                    basis[k + 1, c, p + d] = results[d][c]
            return carried

        lax.fori_loop(0, (3 * depth - 2 * k) // 2, step, tuple(start))
        for c in range(channels):
            basis[k + 1, c, 2 * depth] = basis[k + 1, c, 2 * depth] * keep_high
        return 0

    lax.fori_loop(1, BASIS, apply, 0)

    def plane_forms(p, sums):
        sums = list(sums)
        for q in range(3):
            re = [basis[k + 1, q, p] for k in range(BASIS)]
            im = [basis[k + 1, 3 + q, p] for k in range(BASIS)]
            for f, (i, j) in enumerate(PAIRS):
                real = re[i] * re[j] - im[i] * im[j]
                imag = re[i] * im[j] + im[i] * re[j] if i != j else 2.0 * (re[i] * im[i])
                for half, term in ((0, real), (1, imag)):
                    sums[2 * f + half] = sums[2 * f + half] + jnp.sum(term, axis=0)
        return tuple(sums)

    zero = jnp.zeros((8, cols), jnp.float32)
    sums = lax.fori_loop(depth, 2 * depth, plane_forms, (zero,) * (2 * FORMS))
    folded = jnp.concatenate([jnp.sum(total, axis=0, keepdims=True) for total in sums], axis=0)
    totals = jnp.sum(folded, axis=1, keepdims=True)
    diagonal = lax.broadcasted_iota(jnp.int32, folded.shape, 0) == lax.broadcasted_iota(jnp.int32, folded.shape, 1)
    line = jnp.sum(jnp.where(diagonal, totals, 0.0), axis=0, keepdims=True)
    forms_ref[...] = jnp.broadcast_to(line, forms_ref.shape)


def c_add(a, b):
    return a[0] + b[0], a[1] + b[1]


def c_sub(a, b):
    return a[0] - b[0], a[1] - b[1]


def c_mul(a, b):
    return a[0] * b[0] - a[1] * b[1], a[0] * b[1] + a[1] * b[0]


def c_scale(s, a):
    return s * a[0], s * a[1]


def c_div(a, b):
    inverse = 1.0 / (b[0] * b[0] + b[1] * b[1])
    return (a[0] * b[0] + a[1] * b[1]) * inverse, (a[1] * b[0] - a[0] * b[1]) * inverse


def step_scalars(moments):
    resid = list(moments)
    direc = list(moments)
    none = (jnp.zeros_like(moments[0][0]),) * 2
    one = (jnp.ones_like(moments[0][0]), jnp.zeros_like(moments[0][0]))
    resid_at = [one] + [none] * ITERS
    direc_at = [one] + [none] * ITERS
    field_at = [none] * BASIS
    rho = moments[0]
    for n in range(ITERS):
        applied = [c_add(c_scale(CENTRE, direc[0]), c_scale(RADIUS / 2, direc[1]))]
        for l in range(1, len(direc) - 1):
            near = c_scale(RADIUS / 2, c_add(direc[l + 1], direc[l - 1]))
            applied.append(c_add(c_scale(CENTRE, direc[l]), near))
        step = c_div(rho, c_mul(direc_at[n], applied[n]))
        applied_at = [c_scale(CENTRE, direc_at[j]) if j <= n else none for j in range(BASIS)]
        for j in range(n + 1):
            spread = c_scale(RADIUS / 2, direc_at[j])
            applied_at[j + 1] = c_add(applied_at[j + 1], spread)
            if j > 0:
                applied_at[j - 1] = c_add(applied_at[j - 1], spread)
        for j in range(n + 1):
            field_at[j] = c_add(field_at[j], c_mul(step, direc_at[j]))
        for j in range(n + 2):
            resid_at[j] = c_sub(resid_at[j], c_mul(step, applied_at[j]))
        if n + 1 < ITERS:
            resid = [c_sub(resid[l], c_mul(step, applied[l])) for l in range(len(applied))]
            rho_next = c_mul(resid_at[n + 1], resid[n + 1])
            ratio = c_div(rho_next, rho)
            direc = [c_add(resid[l], c_mul(ratio, direc[l])) for l in range(len(resid))]
            direc_at = [
                c_add(resid_at[j], c_mul(ratio, direc_at[j])) if j <= n else resid_at[j] for j in range(BASIS)
            ]
            rho = rho_next
    return field_at, resid_at


def combine_kernel(forms_ref, basis, field_ref, resid_ref):
    depth, folds, cols = basis.shape[2] // 3, basis.shape[3], basis.shape[5]
    totals = jnp.broadcast_to(jnp.sum(forms_ref[...], axis=0, keepdims=True), (8, cols))
    lane = lax.broadcasted_iota(jnp.int32, (8, cols), 1)
    sums = [
        jnp.broadcast_to(jnp.sum(jnp.where(lane == i, totals, 0.0), axis=1, keepdims=True), (8, cols))
        for i in range(2 * FORMS)
    ]
    forms = [(sums[2 * f], sums[2 * f + 1]) for f in range(FORMS)]
    moments = forms[:2] + [c_sub(forms[f], forms[f - 2]) for f in range(2, FORMS)]
    field_at, resid_at = step_scalars(moments)

    def plane(p, _):
        for q in range(3):
            for j in range(folds):
                re = [basis[k + 1, q, depth + p, j] for k in range(BASIS)]
                im = [basis[k + 1, 3 + q, depth + p, j] for k in range(BASIS)]
                rows = pl.ds(j, 8, stride=folds)
                for out_ref, factors in ((field_ref, field_at[:ITERS]), (resid_ref, resid_at)):
                    out_ref[q, p, rows] = sum(f[0] * re[k] - f[1] * im[k] for k, f in enumerate(factors))
                    out_ref[3 + q, p, rows] = sum(f[0] * im[k] + f[1] * re[k] for k, f in enumerate(factors))
        return 0

    lax.fori_loop(0, depth, plane, 0)


def params(limit=VMEM_LIMIT):
    return pltpu.CompilerParams(vmem_limit_bytes=limit)


def krylov(n, recv, mate, other, conductivity, omega):
    depth, folds, cols = conductivity.shape[1], conductivity.shape[2] // 8, conductivity.shape[3]
    slots = 2 * recv.shape[0] * recv.shape[1] // 3
    left_rows, right_rows = 2 * 6 * depth // 2 * 8 * folds, 2 * cols
    bases = jax.ShapeDtypeStruct((BASIS + 1, 6, 3 * depth, folds, 8, cols), jnp.float32)
    basis, mine = pl.pallas_call(
        scatter_kernel,
        out_shape=(bases, jax.ShapeDtypeStruct((3, depth, folds, 8, cols), jnp.float32)),
        in_specs=[vmem(), hbm(), smem()],
        out_specs=(vmem(), vmem()),
        scratch_shapes=[
            pltpu.VMEM((left_rows, 8 * slots), jnp.bfloat16),
            pltpu.VMEM((right_rows, 8 * slots), jnp.bfloat16),
            pltpu.VMEM(conductivity.shape, jnp.float32),
            pltpu.SemaphoreType.DMA,
        ],
        cost_estimate=pl.CostEstimate(
            flops=6 * left_rows * right_rows * 8 * slots, bytes_accessed=4 * 1024 * 1024, transcendentals=0
        ),
        compiler_params=params(),
        name="scatter_source",
    )(recv, pltpu.with_memory_space_constraint(conductivity, pltpu.HBM), omega)
    return pl.pallas_call(
        functools.partial(field_kernel, n),
        out_shape=(jax.ShapeDtypeStruct((n, cols), jnp.float32), bases),
        in_specs=[vmem()] * 3 + [smem(), vmem()],
        out_specs=(vmem(), vmem()),
        scratch_shapes=[pltpu.VMEM((3, 2 * HALO + depth, folds, 8, cols), jnp.float32)],
        input_output_aliases={4: 1},
        compiler_params=params(),
        name="krylov_basis",
    )(mate, other, mine, omega, basis)


def per_device(n, site_owner, site_cell, stencil_code, site_residual, conductivity, omega):
    depth, rows, cols = conductivity.shape[1:]
    sites = site_owner.shape[0]
    cap = 2 * sites // n
    half = cap // 2
    listed = (site_owner.reshape(1, sites), site_cell, stencil_code, site_residual)
    packed = pl.pallas_call(
        functools.partial(bin_kernel, n, half, rows, cols, depth // 2),
        out_shape=jax.ShapeDtypeStruct((n * 3 * half, 2 * 8 * 8), jnp.float32),
        in_specs=[hbm()] * len(listed),
        out_specs=vmem(),
        scratch_shapes=[pltpu.VMEM(x.shape, x.dtype) for x in listed] + [pltpu.SemaphoreType.DMA((len(listed),))],
        compiler_params=params(),
        name="bin_sites",
    )(*(pltpu.with_memory_space_constraint(x, pltpu.HBM) for x in listed))
    mate = lax.ppermute(conductivity, "gx", [(i, i ^ 1) for i in range(n)])
    other = lax.ppermute(conductivity, "gx", [(i, ((i + 1) ^ 1) - 1) for i in range(1, n - 1)])
    recv = lax.all_to_all(packed.reshape(n, 3 * half, -1), "gx", 0, 0)
    if half % 8:
        recv = recv.reshape(n, 3, half, -1).transpose(1, 0, 2, 3).reshape(1, 3 * n * half, -1)

    forms, basis = krylov(n, recv, mate, other, conductivity, omega)

    forms = lax.all_to_all(forms, "gx", 0, 0, tiled=True)

    return pl.pallas_call(
        combine_kernel,
        out_shape=(jax.ShapeDtypeStruct((6, depth, rows, cols), jnp.float32),) * 2,
        in_specs=[vmem()] * 2,
        out_specs=(vmem(), vmem()),
        compiler_params=params(),
        name="combine_basis",
    )(forms, basis)


def solution(mesh):
    placed = (
        P(("period", "gx")),
        P(None, ("period", "gx")),
        P(None, ("period", "gx")),
        P(None, None, ("period", "gx")),
        P(None, "gx", None, None),
        P("period"),
    )
    return jax.shard_map(
        functools.partial(per_device, mesh.shape["gx"]),
        mesh=mesh,
        in_specs=placed,
        out_specs=(P("period", "gx", None, None), P("period", "gx", None, None)),
        check_vma=False,
    )
```

```python
import functools

import jax
import jax.numpy as jnp
from jax import lax
from jax.experimental import pallas as pl
from jax.experimental.pallas import tpu as pltpu
from jax.sharding import PartitionSpec as P

ITERS = 4
CENTRE = 5.0
RADIUS = 5.0
BASIS = ITERS + 1
FORMS = 2 * ITERS
PAIRS = [(i // 2, (i + 1) // 2) for i in range(FORMS)]
HALO = ITERS - 1
VMEM_LIMIT = 40 * 1024 * 1024
FULL_LIMIT = 62 * 1024 * 1024
CONTRACT_LANES = (((1,), (1,)), ((), ()))


def vmem():
    return pl.BlockSpec(memory_space=pltpu.VMEM)


def smem():
    return pl.BlockSpec(memory_space=pltpu.SMEM)


def hbm():
    return pl.BlockSpec(memory_space=pltpu.HBM)


def split_bf16(x):
    high = x.astype(jnp.bfloat16)
    return high, (x - high.astype(jnp.float32)).astype(jnp.bfloat16)


def bin_kernel(n, half, rows, cols, half_depth, *refs):
    sources, cond_hbm, out_ref, cut_ref, held, arrived = refs[:4], refs[4], refs[5], refs[6], refs[7:11], refs[11]
    copies = [pltpu.make_async_copy(sources[i], held[i], arrived.at[i]) for i in range(4)]
    first = (2 * half_depth - HALO) * (lax.axis_index("gx") % 2)
    copies.append(pltpu.make_async_copy(cond_hbm.at[:, pl.ds(first, HALO)], cut_ref, arrived.at[4]))
    for copy in copies:
        copy.start()
    for copy in copies[:4]:
        copy.wait()
    owner_ref, cell_ref, code_ref, value_ref = held
    sites = owner_ref.shape[1]
    owner = owner_ref[...]
    code = code_ref[...]
    dx = (code >= 9).astype(jnp.int32) + (code >= 18).astype(jnp.int32)
    rest = code - 9 * dx
    dy = (rest >= 3).astype(jnp.int32) + (rest >= 6).astype(jnp.int32)
    dz = rest - 3 * dy
    x = cell_ref[0:1] + dx
    y = cell_ref[1:2] + dy
    z = cell_ref[2:3] + dz
    upper = (x >= half_depth).astype(jnp.int32)
    folds = rows // 8
    row = (x - half_depth * upper) * rows + (y % folds) * 8 + y // folds
    lane = z + cols * upper
    channels, points = value_ref.shape[0], value_ref.shape[1]
    data = jnp.concatenate(
        [value_ref[...].reshape(channels * points, sites), row.astype(jnp.float32), lane.astype(jnp.float32)],
        axis=0,
    )
    blank = jnp.zeros_like(data)

    named = lax.broadcasted_iota(jnp.int32, (n, sites), 0) == owner
    earlier = lax.broadcasted_iota(jnp.int32, (sites, sites), 0) < lax.broadcasted_iota(
        jnp.int32, (sites, sites), 1
    )
    named_f = named.astype(jnp.float32)
    counts = jnp.dot(
        named_f.astype(jnp.bfloat16),
        earlier.astype(jnp.float32).astype(jnp.bfloat16),
        preferred_element_type=jnp.float32,
    )
    rank = jnp.sum(counts * named_f, axis=0, keepdims=True).astype(jnp.int32)
    second = rank >= half
    place = jnp.where(second, rank - half, rank)

    slot = lax.broadcasted_iota(jnp.int32, (out_ref.shape[0], sites), 0)
    hit = jnp.zeros(slot.shape, jnp.bool_)
    for j in range(3):
        hit = hit | (slot == ((owner - j + 1) * 3 + j) * half + place)
    total = jnp.zeros(out_ref.shape, jnp.float32)
    for part, stacked in (
        (jnp.logical_not(second), [data, blank]),
        (second, [blank, data]),
    ):
        chosen = jnp.where(hit & part, 1.0, 0.0).astype(jnp.bfloat16)
        for piece in split_bf16(jnp.concatenate(stacked, axis=0)):
            total = total + lax.dot_general(
                chosen, piece, CONTRACT_LANES, preferred_element_type=jnp.float32
            )
    out_ref[...] = total
    copies[4].wait()


def scatter_kernel(recv_ref, cond_hbm, omega_ref, basis, mine_ref, left, right, cond_ref, arrived):
    conductivity = pltpu.make_async_copy(cond_hbm, cond_ref, arrived)
    conductivity.start()
    depth, folds, cols = basis.shape[2] // 3, basis.shape[3], basis.shape[5]
    rows = 8 * folds
    half_depth = depth // 2
    channels = 6
    points = 8
    group = recv_ref.shape[1] // 3
    basis[0] = jnp.zeros(basis.shape[1:], jnp.float32)
    row_count = half_depth * rows
    lane_count = 2 * cols
    slots = 2 * recv_ref.shape[0] * group
    width = (channels + 2) * points
    row_iota = lax.broadcasted_iota(jnp.int32, (row_count, slots), 0)
    lane_iota = lax.broadcasted_iota(jnp.int32, (lane_count, slots), 0)

    def scatter(j, _):
        packed = recv_ref[:, pl.ds(pl.multiple_of(j * group, 8), group), :].reshape(slots // 2, 2 * width)
        turned = packed.T
        table = jnp.concatenate([turned[:width], turned[width:]], axis=1)
        table_high = table.astype(jnp.bfloat16).astype(jnp.float32)
        table_low = table - table_high
        cell_row = table[channels * points : (channels + 1) * points].astype(jnp.int32)
        cell_lane = table[(channels + 1) * points :].astype(jnp.int32)
        for k in range(points):
            span = slice(k * slots, (k + 1) * slots)
            right[:, span] = jnp.where(lane_iota == cell_lane[k : k + 1], 1.0, 0.0).astype(jnp.bfloat16)
            mask = row_iota == cell_row[k : k + 1]
            for c in range(channels):
                at = c * points + k
                for piece, part in enumerate((table_high, table_low)):
                    first = (piece * channels + c) * row_count
                    left[first : first + row_count, span] = jnp.where(mask, part[at : at + 1], 0.0).astype(
                        jnp.bfloat16
                    )
        both = lax.dot_general(left[...], right[...], CONTRACT_LANES, preferred_element_type=jnp.float32)
        summed = both[: channels * row_count] + both[channels * row_count :]
        for c in range(channels):
            for x in range(depth):
                first = c * row_count + (x % half_depth) * rows
                lanes = slice((x // half_depth) * cols, (x // half_depth + 1) * cols)
                basis[1, c, j * depth + x] = summed[first : first + rows, lanes].reshape(folds, 8, cols)
        return 0

    lax.fori_loop(0, 3, scatter, 0, unroll=True)

    conductivity.wait()
    scale = omega_ref[0] * (2.0 / RADIUS)
    for q in range(3):
        for j in range(folds):
            for x in range(depth):
                mine_ref[q, x, j] = cond_ref[q, x, pl.ds(j, 8, stride=folds)] * scale


def field_kernel(n, mate_ref, other_ref, mine_ref, omega_ref, _, forms_ref, basis, coupling, faces):
    depth, folds, cols = basis.shape[2] // 3, basis.shape[3], basis.shape[5]
    channels = 6
    me = lax.axis_index("gx")
    keep_low = jnp.where(me > 0, 1.0, 0.0).astype(jnp.float32)
    keep_high = jnp.where(me < n - 1, 1.0, 0.0).astype(jnp.float32)

    scale = omega_ref[0] * (2.0 / RADIUS)
    even = me % 2 == 0
    for q in range(3):
        coupling[q, HALO : HALO + depth] = mine_ref[q]
        for j in range(folds):
            fold = pl.ds(j, 8, stride=folds)
            for i in range(HALO):
                below, above = depth - HALO + i, i
                coupling[q, i, j] = jnp.where(even, other_ref[q, i, fold], mate_ref[q, below, fold]) * scale
                coupling[q, HALO + depth + i, j] = (
                    jnp.where(even, mate_ref[q, above, fold], other_ref[q, i, fold]) * scale
                )

    s_iota = lax.broadcasted_iota(jnp.int32, (8, cols), 0)
    z_iota = lax.broadcasted_iota(jnp.int32, (folds, 8, cols), 2)
    s_first, s_last = s_iota == 0, s_iota == 7
    z_first, z_last = z_iota == 0, z_iota == cols - 1

    def ahead_y(f):
        wrapped = jnp.where(s_last, 0.0, pltpu.roll(f[0], 7, 0))
        return jnp.concatenate([f[1:], wrapped[None]], axis=0) - f

    def ahead_z(f):
        return jnp.where(z_last, 0.0, pltpu.roll(f, cols - 1, 2)) - f

    def behind_y(f):
        wrapped = jnp.where(s_first, 0.0, pltpu.roll(f[folds - 1], 1, 0))
        return f - jnp.concatenate([wrapped[None], f[:-1]], axis=0)

    def behind_z(f):
        return f - jnp.where(z_first, 0.0, pltpu.roll(f, 1, 2))

    weight = 2.0 / RADIUS
    centre = 2.0 * CENTRE / RADIUS

    def edges(k, p):
        return [basis[k, c, p] for c in range(channels)]

    def faces_of(here, there):
        result = []
        for part in range(2):
            ex, ey, ez = here[3 * part : 3 * part + 3]
            ey_next, ez_next = there[3 * part + 1], there[3 * part + 2]
            result.append(ahead_y(ez) - ahead_z(ey))
            result.append(ahead_z(ex) - (ez_next - ez))
            result.append((ey_next - ey) - ahead_y(ex))
        return result

    def keep_faces(p, values):
        for c in range(channels):
            faces[c, p] = values[c]

    def plane(here, older, coupled, face, face_before):
        new = []
        for part in range(2):
            hx, hy, hz = face[3 * part : 3 * part + 3]
            hy_before, hz_before = face_before[2 * part], face_before[2 * part + 1]
            curls = (
                behind_y(hz) - behind_z(hy),
                behind_z(hx) - (hz - hz_before),
                (hy - hy_before) - behind_y(hx),
            )
            for q in range(3):
                other = coupled[q] * here[3 * (1 - part) + q]
                value = weight * curls[q] - (centre * here[3 * part + q] + older[3 * part + q])
                new.append(value + other if part == 0 else value - other)
        return new

    last_pair = 3 * depth - 3

    def apply(k, _):
        first = [edges(k, k - 1 + d) for d in range(4)]
        for d in range(3):
            keep_faces(k - 1 + d, faces_of(first[d], first[d + 1]))

        def step(i, _):
            p = k + 2 * i
            ahead = jnp.minimum(p + 2, last_pair)
            fields = [edges(k, p + d) for d in range(2)]
            older = [edges(k - 1, p + d) for d in range(2)]
            coupled = [[coupling[q, p + d - (depth - HALO)] for q in range(3)] for d in range(2)]
            face = [[faces[c, p + d] for c in range(channels)] for d in range(2)]
            before = [faces[c, p - 1] * jnp.where(p == depth, keep_low, 1.0) for c in (1, 2, 4, 5)]
            middle = [face[0][c] * jnp.where(p + 1 == depth, keep_low, 1.0) for c in (1, 2, 4, 5)]
            following = [edges(k, ahead + d) for d in range(3)]
            next_faces = [faces_of(following[d], following[d + 1]) for d in range(2)]
            new = [
                plane(fields[0], older[0], coupled[0], face[0], before),
                plane(fields[1], older[1], coupled[1], face[1], middle),
            ]
            for d in range(2):
                for c in range(channels):
                    basis[k + 1, c, p + d] = new[d][c]
            for d in range(2):
                keep_faces(ahead + d, next_faces[d])
            return 0

        lax.fori_loop(0, (3 * depth - 2 * k) // 2, step, 0)
        for c in range(channels):
            basis[k + 1, c, 2 * depth] = basis[k + 1, c, 2 * depth] * keep_high
        return 0

    lax.fori_loop(1, BASIS, apply, 0)

    def plane_forms(p, sums):
        sums = list(sums)
        for q in range(3):
            re = [basis[k + 1, q, p] for k in range(BASIS)]
            im = [basis[k + 1, 3 + q, p] for k in range(BASIS)]
            for f, (i, j) in enumerate(PAIRS):
                real = re[i] * re[j] - im[i] * im[j]
                imag = re[i] * im[j] + im[i] * re[j] if i != j else 2.0 * (re[i] * im[i])
                for half, term in ((0, real), (1, imag)):
                    sums[2 * f + half] = sums[2 * f + half] + jnp.sum(term, axis=0)
        return tuple(sums)

    zero = jnp.zeros((8, cols), jnp.float32)
    sums = lax.fori_loop(depth, 2 * depth, plane_forms, (zero,) * (2 * FORMS))
    folded = jnp.concatenate([jnp.sum(total, axis=0, keepdims=True) for total in sums], axis=0)
    totals = jnp.sum(folded, axis=1, keepdims=True)
    diagonal = lax.broadcasted_iota(jnp.int32, folded.shape, 0) == lax.broadcasted_iota(jnp.int32, folded.shape, 1)
    line = jnp.sum(jnp.where(diagonal, totals, 0.0), axis=0, keepdims=True)
    forms_ref[...] = jnp.broadcast_to(line, forms_ref.shape)


def c_add(a, b):
    return a[0] + b[0], a[1] + b[1]


def c_sub(a, b):
    return a[0] - b[0], a[1] - b[1]


def c_mul(a, b):
    return a[0] * b[0] - a[1] * b[1], a[0] * b[1] + a[1] * b[0]


def c_scale(s, a):
    return s * a[0], s * a[1]


def c_div(a, b):
    inverse = 1.0 / (b[0] * b[0] + b[1] * b[1])
    return (a[0] * b[0] + a[1] * b[1]) * inverse, (a[1] * b[0] - a[0] * b[1]) * inverse


def step_scalars(moments):
    resid = list(moments)
    direc = list(moments)
    none = (jnp.zeros_like(moments[0][0]),) * 2
    one = (jnp.ones_like(moments[0][0]), jnp.zeros_like(moments[0][0]))
    resid_at = [one] + [none] * ITERS
    direc_at = [one] + [none] * ITERS
    field_at = [none] * BASIS
    rho = moments[0]
    for n in range(ITERS):
        applied = [c_add(c_scale(CENTRE, direc[0]), c_scale(RADIUS / 2, direc[1]))]
        for l in range(1, len(direc) - 1):
            near = c_scale(RADIUS / 2, c_add(direc[l + 1], direc[l - 1]))
            applied.append(c_add(c_scale(CENTRE, direc[l]), near))
        step = c_div(rho, c_mul(direc_at[n], applied[n]))
        applied_at = [c_scale(CENTRE, direc_at[j]) if j <= n else none for j in range(BASIS)]
        for j in range(n + 1):
            spread = c_scale(RADIUS / 2, direc_at[j])
            applied_at[j + 1] = c_add(applied_at[j + 1], spread)
            if j > 0:
                applied_at[j - 1] = c_add(applied_at[j - 1], spread)
        for j in range(n + 1):
            field_at[j] = c_add(field_at[j], c_mul(step, direc_at[j]))
        for j in range(n + 2):
            resid_at[j] = c_sub(resid_at[j], c_mul(step, applied_at[j]))
        if n + 1 < ITERS:
            resid = [c_sub(resid[l], c_mul(step, applied[l])) for l in range(len(applied))]
            rho_next = c_mul(resid_at[n + 1], resid[n + 1])
            ratio = c_div(rho_next, rho)
            direc = [c_add(resid[l], c_mul(ratio, direc[l])) for l in range(len(resid))]
            direc_at = [
                c_add(resid_at[j], c_mul(ratio, direc_at[j])) if j <= n else resid_at[j] for j in range(BASIS)
            ]
            rho = rho_next
    return field_at, resid_at


def combine_kernel(forms_ref, basis, field_ref, resid_ref):
    depth, folds, cols = basis.shape[2] // 3, basis.shape[3], basis.shape[5]
    totals = jnp.broadcast_to(jnp.sum(forms_ref[...], axis=0, keepdims=True), (8, cols))
    lane = lax.broadcasted_iota(jnp.int32, (8, cols), 1)
    sums = [
        jnp.broadcast_to(jnp.sum(jnp.where(lane == i, totals, 0.0), axis=1, keepdims=True), (8, cols))
        for i in range(2 * FORMS)
    ]
    forms = [(sums[2 * f], sums[2 * f + 1]) for f in range(FORMS)]
    moments = forms[:2] + [c_sub(forms[f], forms[f - 2]) for f in range(2, FORMS)]
    field_at, resid_at = step_scalars(moments)

    def plane(p, _):
        for q in range(3):
            for j in range(folds):
                re = [basis[k + 1, q, depth + p, j] for k in range(BASIS)]
                im = [basis[k + 1, 3 + q, depth + p, j] for k in range(BASIS)]
                rows = pl.ds(j, 8, stride=folds)
                for out_ref, factors in ((field_ref, field_at[:ITERS]), (resid_ref, resid_at)):
                    out_ref[q, p, rows] = sum(f[0] * re[k] - f[1] * im[k] for k, f in enumerate(factors))
                    out_ref[3 + q, p, rows] = sum(f[0] * im[k] + f[1] * re[k] for k, f in enumerate(factors))
        return 0

    lax.fori_loop(0, depth, plane, 0)


def params(limit=VMEM_LIMIT):
    return pltpu.CompilerParams(vmem_limit_bytes=limit)


def krylov(n, recv, mate, other, conductivity, omega):
    depth, folds, cols = conductivity.shape[1], conductivity.shape[2] // 8, conductivity.shape[3]
    slots = 2 * recv.shape[0] * recv.shape[1] // 3
    left_rows, right_rows = 2 * 6 * depth // 2 * 8 * folds, 2 * cols
    bases = jax.ShapeDtypeStruct((BASIS + 1, 6, 3 * depth, folds, 8, cols), jnp.float32)
    basis, mine = pl.pallas_call(
        scatter_kernel,
        out_shape=(bases, jax.ShapeDtypeStruct((3, depth, folds, 8, cols), jnp.float32)),
        in_specs=[vmem(), hbm(), smem()],
        out_specs=(vmem(), vmem()),
        scratch_shapes=[
            pltpu.VMEM((left_rows, 8 * slots), jnp.bfloat16),
            pltpu.VMEM((right_rows, 8 * slots), jnp.bfloat16),
            pltpu.VMEM(conductivity.shape, jnp.float32),
            pltpu.SemaphoreType.DMA,
        ],
        cost_estimate=pl.CostEstimate(
            flops=6 * left_rows * right_rows * 8 * slots, bytes_accessed=4 * 1024 * 1024, transcendentals=0
        ),
        compiler_params=params(),
        name="scatter_source",
    )(recv, pltpu.with_memory_space_constraint(conductivity, pltpu.HBM), omega)
    return pl.pallas_call(
        functools.partial(field_kernel, n),
        out_shape=(jax.ShapeDtypeStruct((n, cols), jnp.float32), bases),
        in_specs=[vmem()] * 3 + [smem(), vmem()],
        out_specs=(vmem(), vmem()),
        scratch_shapes=[
            pltpu.VMEM((3, 2 * HALO + depth, folds, 8, cols), jnp.float32),
            pltpu.VMEM((6, 3 * depth, folds, 8, cols), jnp.float32),
        ],
        input_output_aliases={4: 1},
        compiler_params=params(),
        name="krylov_basis",
    )(mate, other, mine, omega, basis)


def combine(forms, basis):
    depth, folds, cols = basis.shape[2] // 3, basis.shape[3], basis.shape[5]
    rows = 8 * folds
    return pl.pallas_call(
        combine_kernel,
        out_shape=(jax.ShapeDtypeStruct((6, depth, rows, cols), jnp.float32),) * 2,
        in_specs=[vmem()] * 2,
        out_specs=(vmem(), vmem()),
        compiler_params=params(),
        name="combine_basis",
    )(forms, basis)


def per_device(n, site_owner, site_cell, stencil_code, site_residual, conductivity, omega):
    depth, rows, cols = conductivity.shape[1:]
    sites = site_owner.shape[0]
    cap = 2 * sites // n
    half = cap // 2
    listed = (site_owner.reshape(1, sites), site_cell, stencil_code, site_residual)
    packed, cut = pl.pallas_call(
        functools.partial(bin_kernel, n, half, rows, cols, depth // 2),
        out_shape=(
            jax.ShapeDtypeStruct((n * 3 * half, 2 * 8 * 8), jnp.float32),
            jax.ShapeDtypeStruct((3, HALO, rows, cols), jnp.float32),
        ),
        in_specs=[hbm()] * 5,
        out_specs=(vmem(), vmem()),
        scratch_shapes=[pltpu.VMEM(x.shape, x.dtype) for x in listed] + [pltpu.SemaphoreType.DMA((5,))],
        compiler_params=params(),
        name="bin_sites",
    )(*(pltpu.with_memory_space_constraint(x, pltpu.HBM) for x in (*listed, conductivity)))
    mate = lax.ppermute(conductivity, "gx", [(i, i ^ 1) for i in range(n)])
    other = lax.ppermute(cut, "gx", [(i, ((i + 1) ^ 1) - 1) for i in range(1, n - 1)])
    recv = lax.all_to_all(packed.reshape(n, 3 * half, -1), "gx", 0, 0)
    if half % 8:
        recv = recv.reshape(n, 3, half, -1).transpose(1, 0, 2, 3).reshape(1, 3 * n * half, -1)

    forms, basis = krylov(n, recv, mate, other, conductivity, omega)

    forms = lax.all_to_all(forms, "gx", 0, 0, tiled=True)

    return combine(forms, basis)


def solution(mesh):
    placed = (
        P(("period", "gx")),
        P(None, ("period", "gx")),
        P(None, ("period", "gx")),
        P(None, None, ("period", "gx")),
        P(None, "gx", None, None),
        P("period"),
    )
    return jax.shard_map(
        functools.partial(per_device, mesh.shape["gx"]),
        mesh=mesh,
        in_specs=placed,
        out_specs=(P("period", "gx", None, None), P("period", "gx", None, None)),
        check_vma=False,
    )
```

```python
import functools

import jax
import jax.numpy as jnp
from jax import lax
from jax.experimental import pallas as pl
from jax.experimental.pallas import tpu as pltpu
from jax.sharding import PartitionSpec as P

ITERS = 4
CENTRE = 5.0
RADIUS = 5.0
BASIS = ITERS + 1
FORMS = 2 * ITERS
PAIRS = [(i // 2, (i + 1) // 2) for i in range(FORMS)]
HALO = ITERS - 1
VMEM_LIMIT = 40 * 1024 * 1024
FULL_LIMIT = 62 * 1024 * 1024
CONTRACT_LANES = (((1,), (1,)), ((), ()))


def vmem():
    return pl.BlockSpec(memory_space=pltpu.VMEM)


def smem():
    return pl.BlockSpec(memory_space=pltpu.SMEM)


def hbm():
    return pl.BlockSpec(memory_space=pltpu.HBM)


def split_bf16(x):
    high = x.astype(jnp.bfloat16)
    return high, (x - high.astype(jnp.float32)).astype(jnp.bfloat16)


def bin_kernel(n, half, rows, cols, half_depth, *refs):
    sources, cond_hbm, out_ref, cut_ref, held, arrived = refs[:4], refs[4], refs[5], refs[6], refs[7:11], refs[11]
    copies = [pltpu.make_async_copy(sources[i], held[i], arrived.at[i]) for i in range(4)]
    first = (2 * half_depth - HALO) * (lax.axis_index("gx") % 2)
    copies.append(pltpu.make_async_copy(cond_hbm.at[:, pl.ds(first, HALO)], cut_ref, arrived.at[4]))
    for copy in copies:
        copy.start()
    for copy in copies[:4]:
        copy.wait()
    owner_ref, cell_ref, code_ref, value_ref = held
    sites = owner_ref.shape[1]
    owner = owner_ref[...]
    code = code_ref[...]
    dx = (code >= 9).astype(jnp.int32) + (code >= 18).astype(jnp.int32)
    rest = code - 9 * dx
    dy = (rest >= 3).astype(jnp.int32) + (rest >= 6).astype(jnp.int32)
    dz = rest - 3 * dy
    x = cell_ref[0:1] + dx
    y = cell_ref[1:2] + dy
    z = cell_ref[2:3] + dz
    upper = (x >= half_depth).astype(jnp.int32)
    folds = rows // 8
    row = (x - half_depth * upper) * rows + (y % folds) * 8 + y // folds
    lane = z + cols * upper
    channels, points = value_ref.shape[0], value_ref.shape[1]
    data = jnp.concatenate(
        [value_ref[...].reshape(channels * points, sites), row.astype(jnp.float32), lane.astype(jnp.float32)],
        axis=0,
    )
    blank = jnp.zeros_like(data)

    named = lax.broadcasted_iota(jnp.int32, (n, sites), 0) == owner
    earlier = lax.broadcasted_iota(jnp.int32, (sites, sites), 0) < lax.broadcasted_iota(
        jnp.int32, (sites, sites), 1
    )
    named_f = named.astype(jnp.float32)
    counts = jnp.dot(
        named_f.astype(jnp.bfloat16),
        earlier.astype(jnp.float32).astype(jnp.bfloat16),
        preferred_element_type=jnp.float32,
    )
    rank = jnp.sum(counts * named_f, axis=0, keepdims=True).astype(jnp.int32)
    second = rank >= half
    place = jnp.where(second, rank - half, rank)

    slot = lax.broadcasted_iota(jnp.int32, (out_ref.shape[0], sites), 0)
    odd = owner % 2
    beside = owner + 2 * odd - 1
    hit = jnp.zeros(slot.shape, jnp.bool_)
    for first_row in (2 * owner + 1, 2 * beside):
        hit = hit | (slot == first_row * half + place)
    total = jnp.zeros(out_ref.shape, jnp.float32)
    for part, stacked in (
        (jnp.logical_not(second), [data, blank]),
        (second, [blank, data]),
    ):
        chosen = jnp.where(hit & part, 1.0, 0.0).astype(jnp.bfloat16)
        for piece in split_bf16(jnp.concatenate(stacked, axis=0)):
            total = total + lax.dot_general(
                chosen, piece, CONTRACT_LANES, preferred_element_type=jnp.float32
            )
    out_ref[...] = total
    copies[4].wait()


def scatter_slab(packed, left, right, depth, folds, cols):
    rows = 8 * folds
    half_depth = depth // 2
    channels, points = 6, 8
    row_count, lane_count, slots, width = half_depth * rows, 2 * cols, 2 * packed.shape[0], packed.shape[1] // 2
    row_iota = lax.broadcasted_iota(jnp.int32, (row_count, slots), 0)
    lane_iota = lax.broadcasted_iota(jnp.int32, (lane_count, slots), 0)
    turned = packed.T
    table = jnp.concatenate([turned[:width], turned[width:]], axis=1)
    table_high = table.astype(jnp.bfloat16).astype(jnp.float32)
    table_low = table - table_high
    cell_row = table[channels * points : (channels + 1) * points].astype(jnp.int32)
    cell_lane = table[(channels + 1) * points :].astype(jnp.int32)
    for k in range(points):
        span = slice(k * slots, (k + 1) * slots)
        right[:, span] = jnp.where(lane_iota == cell_lane[k : k + 1], 1.0, 0.0).astype(jnp.bfloat16)
        mask = row_iota == cell_row[k : k + 1]
        for c in range(channels):
            at = c * points + k
            for piece, part in enumerate((table_high, table_low)):
                first = (piece * channels + c) * row_count
                left[first : first + row_count, span] = jnp.where(mask, part[at : at + 1], 0.0).astype(jnp.bfloat16)
    both = lax.dot_general(left[...], right[...], CONTRACT_LANES, preferred_element_type=jnp.float32)
    return both[: channels * row_count] + both[channels * row_count :]


def store_slab(summed, basis, first_plane):
    depth, folds, cols = basis.shape[2] // 3, basis.shape[3], basis.shape[5]
    rows = 8 * folds
    half_depth = depth // 2
    row_count = half_depth * rows
    for c in range(6):
        for x in range(depth):
            first = c * row_count + (x % half_depth) * rows
            lanes = slice((x // half_depth) * cols, (x // half_depth + 1) * cols)
            basis[1, c, first_plane + x] = summed[first : first + rows, lanes].reshape(folds, 8, cols)


def scatter_kernel(list_ref, cond_hbm, omega_ref, basis, mine_ref, left, right, cond_ref, arrived):
    conductivity = pltpu.make_async_copy(cond_hbm, cond_ref, arrived)
    conductivity.start()
    depth, folds = mine_ref.shape[1], mine_ref.shape[2]
    basis[0] = jnp.zeros(basis.shape[1:], jnp.float32)
    cols = basis.shape[5]
    outer, own = (scatter_slab(list_ref[j], left.at[j], right.at[j], depth, folds, cols) for j in range(2))
    store_slab(own, basis, depth)
    store_slab(outer, basis, 2 * depth * (lax.axis_index("gx") % 2))
    conductivity.wait()
    scale = omega_ref[0] * (2.0 / RADIUS)
    for q in range(3):
        for j in range(folds):
            for x in range(depth):
                mine_ref[q, x, j] = cond_ref[q, x, pl.ds(j, 8, stride=folds)] * scale


def field_kernel(
    n, list_ref, mate_ref, other_ref, mine_ref, omega_ref, _, forms_ref, basis, coupling, faces, left, right
):
    depth, folds, cols = basis.shape[2] // 3, basis.shape[3], basis.shape[5]
    channels = 6
    me = lax.axis_index("gx")
    keep_low = jnp.where(me > 0, 1.0, 0.0).astype(jnp.float32)
    keep_high = jnp.where(me < n - 1, 1.0, 0.0).astype(jnp.float32)

    store_slab(scatter_slab(list_ref[...], left, right, depth, folds, cols), basis, 2 * depth * (1 - me % 2))

    scale = omega_ref[0] * (2.0 / RADIUS)
    even = me % 2 == 0
    for q in range(3):
        coupling[q, HALO : HALO + depth] = mine_ref[q]
        for j in range(folds):
            fold = pl.ds(j, 8, stride=folds)
            for i in range(HALO):
                below, above = depth - HALO + i, i
                coupling[q, i, j] = jnp.where(even, other_ref[q, i, fold], mate_ref[q, below, fold]) * scale
                coupling[q, HALO + depth + i, j] = (
                    jnp.where(even, mate_ref[q, above, fold], other_ref[q, i, fold]) * scale
                )

    s_iota = lax.broadcasted_iota(jnp.int32, (8, cols), 0)
    z_iota = lax.broadcasted_iota(jnp.int32, (folds, 8, cols), 2)
    s_first, s_last = s_iota == 0, s_iota == 7
    z_first, z_last = z_iota == 0, z_iota == cols - 1

    def ahead_y(f):
        wrapped = jnp.where(s_last, 0.0, pltpu.roll(f[0], 7, 0))
        return jnp.concatenate([f[1:], wrapped[None]], axis=0) - f

    def ahead_z(f):
        return jnp.where(z_last, 0.0, pltpu.roll(f, cols - 1, 2)) - f

    def behind_y(f):
        wrapped = jnp.where(s_first, 0.0, pltpu.roll(f[folds - 1], 1, 0))
        return f - jnp.concatenate([wrapped[None], f[:-1]], axis=0)

    def behind_z(f):
        return f - jnp.where(z_first, 0.0, pltpu.roll(f, 1, 2))

    weight = 2.0 / RADIUS
    centre = 2.0 * CENTRE / RADIUS

    def edges(k, p):
        return [basis[k, c, p] for c in range(channels)]

    def faces_of(here, there):
        result = []
        for part in range(2):
            ex, ey, ez = here[3 * part : 3 * part + 3]
            ey_next, ez_next = there[3 * part + 1], there[3 * part + 2]
            result.append(ahead_y(ez) - ahead_z(ey))
            result.append(ahead_z(ex) - (ez_next - ez))
            result.append((ey_next - ey) - ahead_y(ex))
        return result

    def keep_faces(p, values):
        for c in range(channels):
            faces[c, p] = values[c]

    def plane(here, older, coupled, face, face_before):
        new = []
        for part in range(2):
            hx, hy, hz = face[3 * part : 3 * part + 3]
            hy_before, hz_before = face_before[2 * part], face_before[2 * part + 1]
            curls = (
                behind_y(hz) - behind_z(hy),
                behind_z(hx) - (hz - hz_before),
                (hy - hy_before) - behind_y(hx),
            )
            for q in range(3):
                other = coupled[q] * here[3 * (1 - part) + q]
                value = weight * curls[q] - (centre * here[3 * part + q] + older[3 * part + q])
                new.append(value + other if part == 0 else value - other)
        return new

    last_pair = 3 * depth - 3

    def apply(k, _):
        first = [edges(k, k - 1 + d) for d in range(4)]
        for d in range(3):
            keep_faces(k - 1 + d, faces_of(first[d], first[d + 1]))

        def step(i, _):
            p = k + 2 * i
            ahead = jnp.minimum(p + 2, last_pair)
            fields = [edges(k, p + d) for d in range(2)]
            older = [edges(k - 1, p + d) for d in range(2)]
            coupled = [[coupling[q, p + d - (depth - HALO)] for q in range(3)] for d in range(2)]
            face = [[faces[c, p + d] for c in range(channels)] for d in range(2)]
            before = [faces[c, p - 1] * jnp.where(p == depth, keep_low, 1.0) for c in (1, 2, 4, 5)]
            middle = [face[0][c] * jnp.where(p + 1 == depth, keep_low, 1.0) for c in (1, 2, 4, 5)]
            following = [edges(k, ahead + d) for d in range(3)]
            next_faces = [faces_of(following[d], following[d + 1]) for d in range(2)]
            new = [
                plane(fields[0], older[0], coupled[0], face[0], before),
                plane(fields[1], older[1], coupled[1], face[1], middle),
            ]
            for d in range(2):
                for c in range(channels):
                    basis[k + 1, c, p + d] = new[d][c]
            for d in range(2):
                keep_faces(ahead + d, next_faces[d])
            return 0

        lax.fori_loop(0, (3 * depth - 2 * k) // 2, step, 0)
        for c in range(channels):
            basis[k + 1, c, 2 * depth] = basis[k + 1, c, 2 * depth] * keep_high
        return 0

    lax.fori_loop(1, BASIS, apply, 0)

    def plane_forms(p, sums):
        sums = list(sums)
        for q in range(3):
            re = [basis[k + 1, q, p] for k in range(BASIS)]
            im = [basis[k + 1, 3 + q, p] for k in range(BASIS)]
            for f, (i, j) in enumerate(PAIRS):
                real = re[i] * re[j] - im[i] * im[j]
                imag = re[i] * im[j] + im[i] * re[j] if i != j else 2.0 * (re[i] * im[i])
                for half, term in ((0, real), (1, imag)):
                    sums[2 * f + half] = sums[2 * f + half] + jnp.sum(term, axis=0)
        return tuple(sums)

    zero = jnp.zeros((8, cols), jnp.float32)
    sums = lax.fori_loop(depth, 2 * depth, plane_forms, (zero,) * (2 * FORMS))
    folded = jnp.concatenate([jnp.sum(total, axis=0, keepdims=True) for total in sums], axis=0)
    totals = jnp.sum(folded, axis=1, keepdims=True)
    diagonal = lax.broadcasted_iota(jnp.int32, folded.shape, 0) == lax.broadcasted_iota(jnp.int32, folded.shape, 1)
    line = jnp.sum(jnp.where(diagonal, totals, 0.0), axis=0, keepdims=True)
    forms_ref[...] = jnp.broadcast_to(line, forms_ref.shape)


def c_add(a, b):
    return a[0] + b[0], a[1] + b[1]


def c_sub(a, b):
    return a[0] - b[0], a[1] - b[1]


def c_mul(a, b):
    return a[0] * b[0] - a[1] * b[1], a[0] * b[1] + a[1] * b[0]


def c_scale(s, a):
    return s * a[0], s * a[1]


def c_div(a, b):
    inverse = 1.0 / (b[0] * b[0] + b[1] * b[1])
    return (a[0] * b[0] + a[1] * b[1]) * inverse, (a[1] * b[0] - a[0] * b[1]) * inverse


def step_scalars(moments):
    resid = list(moments)
    direc = list(moments)
    none = (jnp.zeros_like(moments[0][0]),) * 2
    one = (jnp.ones_like(moments[0][0]), jnp.zeros_like(moments[0][0]))
    resid_at = [one] + [none] * ITERS
    direc_at = [one] + [none] * ITERS
    field_at = [none] * BASIS
    rho = moments[0]
    for n in range(ITERS):
        applied = [c_add(c_scale(CENTRE, direc[0]), c_scale(RADIUS / 2, direc[1]))]
        for l in range(1, len(direc) - 1):
            near = c_scale(RADIUS / 2, c_add(direc[l + 1], direc[l - 1]))
            applied.append(c_add(c_scale(CENTRE, direc[l]), near))
        step = c_div(rho, c_mul(direc_at[n], applied[n]))
        applied_at = [c_scale(CENTRE, direc_at[j]) if j <= n else none for j in range(BASIS)]
        for j in range(n + 1):
            spread = c_scale(RADIUS / 2, direc_at[j])
            applied_at[j + 1] = c_add(applied_at[j + 1], spread)
            if j > 0:
                applied_at[j - 1] = c_add(applied_at[j - 1], spread)
        for j in range(n + 1):
            field_at[j] = c_add(field_at[j], c_mul(step, direc_at[j]))
        for j in range(n + 2):
            resid_at[j] = c_sub(resid_at[j], c_mul(step, applied_at[j]))
        if n + 1 < ITERS:
            resid = [c_sub(resid[l], c_mul(step, applied[l])) for l in range(len(applied))]
            rho_next = c_mul(resid_at[n + 1], resid[n + 1])
            ratio = c_div(rho_next, rho)
            direc = [c_add(resid[l], c_mul(ratio, direc[l])) for l in range(len(resid))]
            direc_at = [
                c_add(resid_at[j], c_mul(ratio, direc_at[j])) if j <= n else resid_at[j] for j in range(BASIS)
            ]
            rho = rho_next
    return field_at, resid_at


def combine_kernel(forms_ref, basis, field_hbm, resid_hbm, field_ref, resid_ref, sent):
    depth, folds, cols = basis.shape[2] // 3, basis.shape[3], basis.shape[5]
    totals = jnp.broadcast_to(jnp.sum(forms_ref[...], axis=0, keepdims=True), (8, cols))
    lane = lax.broadcasted_iota(jnp.int32, (8, cols), 1)
    sums = [
        jnp.broadcast_to(jnp.sum(jnp.where(lane == i, totals, 0.0), axis=1, keepdims=True), (8, cols))
        for i in range(2 * FORMS)
    ]
    forms = [(sums[2 * f], sums[2 * f + 1]) for f in range(FORMS)]
    moments = forms[:2] + [c_sub(forms[f], forms[f - 2]) for f in range(2, FORMS)]
    field_at, resid_at = step_scalars(moments)

    def copies(p):
        return [
            pltpu.make_async_copy(ref.at[:, p], hbm_ref.at[:, p], sent.at[i, p])
            for i, (ref, hbm_ref) in enumerate(((field_ref, field_hbm), (resid_ref, resid_hbm)))
        ]

    def plane(p, _):
        for q in range(3):
            for j in range(folds):
                re = [basis[k + 1, q, depth + p, j] for k in range(BASIS)]
                im = [basis[k + 1, 3 + q, depth + p, j] for k in range(BASIS)]
                rows = pl.ds(j, 8, stride=folds)
                for out_ref, factors in ((field_ref, field_at[:ITERS]), (resid_ref, resid_at)):
                    out_ref[q, p, rows] = sum(f[0] * re[k] - f[1] * im[k] for k, f in enumerate(factors))
                    out_ref[3 + q, p, rows] = sum(f[0] * im[k] + f[1] * re[k] for k, f in enumerate(factors))
        for copy in copies(p):
            copy.start()
        return 0

    lax.fori_loop(0, depth, plane, 0)
    for p in range(depth):
        for copy in copies(p):
            copy.wait()


def params(limit=VMEM_LIMIT):
    return pltpu.CompilerParams(vmem_limit_bytes=limit)


def krylov(n, lists, mate_list, mate, other, conductivity, omega):
    depth, folds, cols = conductivity.shape[1], conductivity.shape[2] // 8, conductivity.shape[3]
    slots = 2 * lists.shape[1]
    left_shape, right_shape = (2 * 6 * depth // 2 * 8 * folds, 8 * slots), (2 * cols, 8 * slots)
    bases = jax.ShapeDtypeStruct((BASIS + 1, 6, 3 * depth, folds, 8, cols), jnp.float32)
    basis, mine = pl.pallas_call(
        scatter_kernel,
        out_shape=(bases, jax.ShapeDtypeStruct((3, depth, folds, 8, cols), jnp.float32)),
        in_specs=[vmem(), hbm(), smem()],
        out_specs=(vmem(), vmem()),
        scratch_shapes=[
            pltpu.VMEM((2, *left_shape), jnp.bfloat16),
            pltpu.VMEM((2, *right_shape), jnp.bfloat16),
            pltpu.VMEM(conductivity.shape, jnp.float32),
            pltpu.SemaphoreType.DMA,
        ],
        cost_estimate=pl.CostEstimate(
            flops=4 * left_shape[0] * right_shape[0] * 8 * slots, bytes_accessed=4 * 1024 * 1024, transcendentals=0
        ),
        compiler_params=params(),
        name="scatter_source",
    )(lists, pltpu.with_memory_space_constraint(conductivity, pltpu.HBM), omega)
    return pl.pallas_call(
        functools.partial(field_kernel, n),
        out_shape=(jax.ShapeDtypeStruct((n, cols), jnp.float32), bases),
        in_specs=[vmem()] * 4 + [smem(), vmem()],
        out_specs=(vmem(), vmem()),
        scratch_shapes=[
            pltpu.VMEM((3, 2 * HALO + depth, folds, 8, cols), jnp.float32),
            pltpu.VMEM((6, 3 * depth, folds, 8, cols), jnp.float32),
            pltpu.VMEM(left_shape, jnp.bfloat16),
            pltpu.VMEM(right_shape, jnp.bfloat16),
        ],
        input_output_aliases={5: 1},
        compiler_params=params(),
        name="krylov_basis",
    )(mate_list, mate, other, mine, omega, basis)


def combine(forms, basis):
    depth, folds, cols = basis.shape[2] // 3, basis.shape[3], basis.shape[5]
    rows = 8 * folds
    out = jax.ShapeDtypeStruct((6, depth, rows, cols), jnp.float32)
    return pl.pallas_call(
        combine_kernel,
        out_shape=(out, out),
        in_specs=[vmem()] * 2,
        out_specs=(hbm(), hbm()),
        scratch_shapes=[pltpu.VMEM(out.shape, out.dtype)] * 2 + [pltpu.SemaphoreType.DMA((2, depth))],
        compiler_params=params(),
        name="combine_basis",
    )(forms, basis)


def per_device(n, site_owner, site_cell, stencil_code, site_residual, conductivity, omega):
    depth, rows, cols = conductivity.shape[1:]
    sites = site_owner.shape[0]
    cap = 2 * sites // n
    half = cap // 2
    listed = (site_owner.reshape(1, sites), site_cell, stencil_code, site_residual)
    packed, cut = pl.pallas_call(
        functools.partial(bin_kernel, n, half, rows, cols, depth // 2),
        out_shape=(
            jax.ShapeDtypeStruct((n * 2 * half, 2 * 8 * 8), jnp.float32),
            jax.ShapeDtypeStruct((3, HALO, rows, cols), jnp.float32),
        ),
        in_specs=[hbm()] * 5,
        out_specs=(vmem(), vmem()),
        scratch_shapes=[pltpu.VMEM(x.shape, x.dtype) for x in listed] + [pltpu.SemaphoreType.DMA((5,))],
        compiler_params=params(),
        name="bin_sites",
    )(*(pltpu.with_memory_space_constraint(x, pltpu.HBM) for x in (*listed, conductivity)))
    other = lax.ppermute(cut, "gx", [(i, ((i + 1) ^ 1) - 1) for i in range(1, n - 1)])
    late, _ = lax.optimization_barrier((conductivity, cut))
    mate = lax.ppermute(late, "gx", [(i, i ^ 1) for i in range(n)])
    recv = lax.all_to_all(packed.reshape(n, 2 * half, -1), "gx", 0, 0)
    lists = recv.reshape(n, 2, half, -1).transpose(1, 0, 2, 3).reshape(2, n * half, -1)
    mate_list = lax.ppermute(lists[1], "gx", [(i, i ^ 1) for i in range(n)])
    forms, basis = krylov(n, lists, mate_list, mate, other, conductivity, omega)

    forms = lax.all_to_all(forms, "gx", 0, 0, tiled=True)

    return combine(forms, basis)


def solution(mesh):
    placed = (
        P(("period", "gx")),
        P(None, ("period", "gx")),
        P(None, ("period", "gx")),
        P(None, None, ("period", "gx")),
        P(None, "gx", None, None),
        P("period"),
    )
    return jax.shard_map(
        functools.partial(per_device, mesh.shape["gx"]),
        mesh=mesh,
        in_specs=placed,
        out_specs=(P("period", "gx", None, None), P("period", "gx", None, None)),
        check_vma=False,
    )
```

```python
import functools

import jax
import jax.numpy as jnp
from jax import lax
from jax.experimental import pallas as pl
from jax.experimental.pallas import tpu as pltpu
from jax.sharding import PartitionSpec as P

ITERS = 4
CENTRE = 5.0
RADIUS = 5.0
BASIS = ITERS + 1
FORMS = 2 * ITERS
PAIRS = [(i // 2, (i + 1) // 2) for i in range(FORMS)]
HALO = ITERS - 1
STEP = 5
VMEM_LIMIT = 40 * 1024 * 1024
FULL_LIMIT = 62 * 1024 * 1024
CONTRACT_LANES = (((1,), (1,)), ((), ()))


def vmem():
    return pl.BlockSpec(memory_space=pltpu.VMEM)


def smem():
    return pl.BlockSpec(memory_space=pltpu.SMEM)


def hbm():
    return pl.BlockSpec(memory_space=pltpu.HBM)


def split_bf16(x):
    high = x.astype(jnp.bfloat16)
    return high, (x - high.astype(jnp.float32)).astype(jnp.bfloat16)


def bin_kernel(n, half, rows, cols, half_depth, *refs):
    sources, cond_hbm, out_ref, cut_ref, held, arrived = refs[:4], refs[4], refs[5], refs[6], refs[7:11], refs[11]
    copies = [pltpu.make_async_copy(sources[i], held[i], arrived.at[i]) for i in range(4)]
    first = (2 * half_depth - HALO) * (lax.axis_index("gx") % 2)
    copies.append(pltpu.make_async_copy(cond_hbm.at[:, pl.ds(first, HALO)], cut_ref, arrived.at[4]))
    for copy in copies:
        copy.start()
    for copy in copies[:4]:
        copy.wait()
    owner_ref, cell_ref, code_ref, value_ref = held
    sites = owner_ref.shape[1]
    owner = owner_ref[...]
    code = code_ref[...]
    dx = (code >= 9).astype(jnp.int32) + (code >= 18).astype(jnp.int32)
    rest = code - 9 * dx
    dy = (rest >= 3).astype(jnp.int32) + (rest >= 6).astype(jnp.int32)
    dz = rest - 3 * dy
    x = cell_ref[0:1] + dx
    y = cell_ref[1:2] + dy
    z = cell_ref[2:3] + dz
    upper = (x >= half_depth).astype(jnp.int32)
    folds = rows // 8
    row = (x - half_depth * upper) * rows + (y % folds) * 8 + y // folds
    lane = z + cols * upper
    channels, points = value_ref.shape[0], value_ref.shape[1]
    data = jnp.concatenate(
        [value_ref[...].reshape(channels * points, sites), row.astype(jnp.float32), lane.astype(jnp.float32)],
        axis=0,
    )
    blank = jnp.zeros_like(data)

    named = lax.broadcasted_iota(jnp.int32, (n, sites), 0) == owner
    earlier = lax.broadcasted_iota(jnp.int32, (sites, sites), 0) < lax.broadcasted_iota(
        jnp.int32, (sites, sites), 1
    )
    named_f = named.astype(jnp.float32)
    counts = jnp.dot(
        named_f.astype(jnp.bfloat16),
        earlier.astype(jnp.float32).astype(jnp.bfloat16),
        preferred_element_type=jnp.float32,
    )
    rank = jnp.sum(counts * named_f, axis=0, keepdims=True).astype(jnp.int32)
    second = rank >= half
    place = jnp.where(second, rank - half, rank)

    slot = lax.broadcasted_iota(jnp.int32, (out_ref.shape[0], sites), 0)
    odd = owner % 2
    beside = owner + 2 * odd - 1
    hit = jnp.zeros(slot.shape, jnp.bool_)
    for first_row in (2 * owner + 1, 2 * beside):
        hit = hit | (slot == first_row * half + place)
    total = jnp.zeros(out_ref.shape, jnp.float32)
    for part, stacked in (
        (jnp.logical_not(second), [data, blank]),
        (second, [blank, data]),
    ):
        chosen = jnp.where(hit & part, 1.0, 0.0).astype(jnp.bfloat16)
        for piece in split_bf16(jnp.concatenate(stacked, axis=0)):
            total = total + lax.dot_general(
                chosen, piece, CONTRACT_LANES, preferred_element_type=jnp.float32
            )
    out_ref[...] = total
    copies[4].wait()


def scatter_slab(packed, left, right, depth, folds, cols):
    rows = 8 * folds
    half_depth = depth // 2
    channels, points = 6, 8
    row_count, lane_count, slots, width = half_depth * rows, 2 * cols, 2 * packed.shape[0], packed.shape[1] // 2
    row_iota = lax.broadcasted_iota(jnp.int32, (row_count, slots), 0)
    lane_iota = lax.broadcasted_iota(jnp.int32, (lane_count, slots), 0)
    turned = packed.T
    table = jnp.concatenate([turned[:width], turned[width:]], axis=1)
    table_high = table.astype(jnp.bfloat16).astype(jnp.float32)
    table_low = table - table_high
    cell_row = table[channels * points : (channels + 1) * points].astype(jnp.int32)
    cell_lane = table[(channels + 1) * points :].astype(jnp.int32)
    for k in range(points):
        span = slice(k * slots, (k + 1) * slots)
        right[:, span] = jnp.where(lane_iota == cell_lane[k : k + 1], 1.0, 0.0).astype(jnp.bfloat16)
        mask = row_iota == cell_row[k : k + 1]
        for c in range(channels):
            at = c * points + k
            for piece, part in enumerate((table_high, table_low)):
                first = (piece * channels + c) * row_count
                left[first : first + row_count, span] = jnp.where(mask, part[at : at + 1], 0.0).astype(jnp.bfloat16)
    both = lax.dot_general(left[...], right[...], CONTRACT_LANES, preferred_element_type=jnp.float32)
    return both[: channels * row_count] + both[channels * row_count :]


def store_slab(summed, basis, first_plane):
    depth, folds, cols = basis.shape[2] // 3, basis.shape[3], basis.shape[5]
    rows = 8 * folds
    half_depth = depth // 2
    row_count = half_depth * rows
    for c in range(6):
        for x in range(depth):
            first = c * row_count + (x % half_depth) * rows
            lanes = slice((x // half_depth) * cols, (x // half_depth + 1) * cols)
            basis[1, c, first_plane + x] = summed[first : first + rows, lanes].reshape(folds, 8, cols)


def scatter_kernel(list_ref, cond_hbm, omega_ref, basis, mine_ref, left, right, cond_ref, arrived):
    conductivity = pltpu.make_async_copy(cond_hbm, cond_ref, arrived)
    conductivity.start()
    depth, folds = mine_ref.shape[1], mine_ref.shape[2]
    cols = basis.shape[5]
    outer, own = (scatter_slab(list_ref[j], left.at[j], right.at[j], depth, folds, cols) for j in range(2))
    store_slab(own, basis, depth)
    store_slab(outer, basis, 2 * depth * (lax.axis_index("gx") % 2))
    conductivity.wait()
    scale = omega_ref[0] * (2.0 / RADIUS)
    for q in range(3):
        for j in range(folds):
            for x in range(depth):
                mine_ref[q, x, j] = cond_ref[q, x, pl.ds(j, 8, stride=folds)] * scale


def field_kernel(
    n, list_ref, mate_ref, other_ref, mine_ref, omega_ref, _, forms_ref, basis, coupling, faces, left, right
):
    depth, folds, cols = basis.shape[2] // 3, basis.shape[3], basis.shape[5]
    channels = 6
    me = lax.axis_index("gx")
    keep_low = jnp.where(me > 0, 1.0, 0.0).astype(jnp.float32)
    keep_high = jnp.where(me < n - 1, 1.0, 0.0).astype(jnp.float32)

    store_slab(scatter_slab(list_ref[...], left, right, depth, folds, cols), basis, 2 * depth * (1 - me % 2))

    scale = omega_ref[0] * (2.0 / RADIUS)
    even = me % 2 == 0
    for q in range(3):
        coupling[q, HALO : HALO + depth] = mine_ref[q]
        for j in range(folds):
            fold = pl.ds(j, 8, stride=folds)
            for i in range(HALO):
                below, above = depth - HALO + i, i
                coupling[q, i, j] = jnp.where(even, other_ref[q, i, fold], mate_ref[q, below, fold]) * scale
                coupling[q, HALO + depth + i, j] = (
                    jnp.where(even, mate_ref[q, above, fold], other_ref[q, i, fold]) * scale
                )

    s_iota = lax.broadcasted_iota(jnp.int32, (8, cols), 0)
    z_iota = lax.broadcasted_iota(jnp.int32, (folds, 8, cols), 2)
    s_first, s_last = s_iota == 0, s_iota == 7
    z_first, z_last = z_iota == 0, z_iota == cols - 1

    def ahead_y(f):
        wrapped = jnp.where(s_last, 0.0, pltpu.roll(f[0], 7, 0))
        return jnp.concatenate([f[1:], wrapped[None]], axis=0) - f

    def ahead_z(f):
        return jnp.where(z_last, 0.0, pltpu.roll(f, cols - 1, 2)) - f

    def behind_y(f):
        wrapped = jnp.where(s_first, 0.0, pltpu.roll(f[folds - 1], 1, 0))
        return f - jnp.concatenate([wrapped[None], f[:-1]], axis=0)

    def behind_z(f):
        return f - jnp.where(z_first, 0.0, pltpu.roll(f, 1, 2))

    weight = 2.0 / RADIUS
    centre = 2.0 * CENTRE / RADIUS

    def edges(k, p):
        return [basis[k, c, p] for c in range(channels)]

    def faces_of(here, there):
        result = []
        for part in range(2):
            ex, ey, ez = here[3 * part : 3 * part + 3]
            ey_next, ez_next = there[3 * part + 1], there[3 * part + 2]
            result.append(ahead_y(ez) - ahead_z(ey))
            result.append(ahead_z(ex) - (ez_next - ez))
            result.append((ey_next - ey) - ahead_y(ex))
        return result

    def keep_faces(p, values):
        for c in range(channels):
            faces[c, p] = values[c]

    def plane(here, older, coupled, face, face_before):
        new = []
        for part in range(2):
            hx, hy, hz = face[3 * part : 3 * part + 3]
            hy_before, hz_before = face_before[2 * part], face_before[2 * part + 1]
            curls = (
                behind_y(hz) - behind_z(hy),
                behind_z(hx) - (hz - hz_before),
                (hy - hy_before) - behind_y(hx),
            )
            for q in range(3):
                other = coupled[q] * here[3 * (1 - part) + q]
                rest = centre * here[3 * part + q]
                if older[3 * part + q] is not None:
                    rest = rest + older[3 * part + q]
                value = weight * curls[q] - rest
                new.append(value + other if part == 0 else value - other)
        return new

    def apply(k):
        end = 3 * depth - k

        def step(p, count):
            after = range(p + count, min(p + 2 * count, end))
            fields = [edges(k, p + d) for d in range(count)]
            older = [edges(k - 1, p + d) if k > 1 else [None] * channels for d in range(count)]
            coupled = [[coupling[q, p + d - (depth - HALO)] for q in range(3)] for d in range(count)]
            face = [[faces[c, p + d] for c in range(channels)] for d in range(-1, count)]
            following = [edges(k, x) for x in range(p + count, after.stop + 1)] if after else []
            next_faces = [faces_of(following[d], following[d + 1]) for d in range(len(after))]
            new = []
            for d in range(count):
                before = [face[d][c] for c in (1, 2, 4, 5)]
                if p + d == depth:
                    before = [f * keep_low for f in before]
                new.append(plane(fields[d], older[d], coupled[d], face[d + 1], before))
                if p + d == 2 * depth:
                    new[d] = [f * keep_high for f in new[d]]
            for d in range(count):
                for c in range(channels):
                    basis[k + 1, c, p + d] = new[d][c]
            for x, values in zip(after, next_faces):
                keep_faces(x, values)

        first = [edges(k, x) for x in range(k - 1, min(k + STEP, end) + 1)]
        for d in range(len(first) - 1):
            keep_faces(k - 1 + d, faces_of(first[d], first[d + 1]))
        for p in range(k, end, STEP):
            step(p, min(STEP, end - p))

    for k in range(1, BASIS):
        apply(k)

    def plane_forms(p, sums):
        sums = list(sums)
        for q in range(3):
            re = [basis[k + 1, q, p] for k in range(BASIS)]
            im = [basis[k + 1, 3 + q, p] for k in range(BASIS)]
            for f, (i, j) in enumerate(PAIRS):
                real = re[i] * re[j] - im[i] * im[j]
                imag = re[i] * im[j] + im[i] * re[j] if i != j else 2.0 * (re[i] * im[i])
                for half, term in ((0, real), (1, imag)):
                    sums[2 * f + half] = sums[2 * f + half] + jnp.sum(term, axis=0)
        return tuple(sums)

    zero = jnp.zeros((8, cols), jnp.float32)
    sums = lax.fori_loop(depth, 2 * depth, plane_forms, (zero,) * (2 * FORMS))
    folded = jnp.concatenate([jnp.sum(total, axis=0, keepdims=True) for total in sums], axis=0)
    totals = jnp.sum(folded, axis=1, keepdims=True)
    diagonal = lax.broadcasted_iota(jnp.int32, folded.shape, 0) == lax.broadcasted_iota(jnp.int32, folded.shape, 1)
    line = jnp.sum(jnp.where(diagonal, totals, 0.0), axis=0, keepdims=True)
    forms_ref[...] = jnp.broadcast_to(line, forms_ref.shape)


def c_add(a, b):
    return a[0] + b[0], a[1] + b[1]


def c_sub(a, b):
    return a[0] - b[0], a[1] - b[1]


def c_mul(a, b):
    return a[0] * b[0] - a[1] * b[1], a[0] * b[1] + a[1] * b[0]


def c_scale(s, a):
    return s * a[0], s * a[1]


def c_div(a, b):
    inverse = 1.0 / (b[0] * b[0] + b[1] * b[1])
    return (a[0] * b[0] + a[1] * b[1]) * inverse, (a[1] * b[0] - a[0] * b[1]) * inverse


def step_scalars(moments):
    resid = list(moments)
    direc = list(moments)
    none = (jnp.zeros_like(moments[0][0]),) * 2
    one = (jnp.ones_like(moments[0][0]), jnp.zeros_like(moments[0][0]))
    resid_at = [one] + [none] * ITERS
    direc_at = [one] + [none] * ITERS
    field_at = [none] * BASIS
    rho = moments[0]
    for n in range(ITERS):
        applied = [c_add(c_scale(CENTRE, direc[0]), c_scale(RADIUS / 2, direc[1]))]
        for l in range(1, len(direc) - 1):
            near = c_scale(RADIUS / 2, c_add(direc[l + 1], direc[l - 1]))
            applied.append(c_add(c_scale(CENTRE, direc[l]), near))
        step = c_div(rho, c_mul(direc_at[n], applied[n]))
        applied_at = [c_scale(CENTRE, direc_at[j]) if j <= n else none for j in range(BASIS)]
        for j in range(n + 1):
            spread = c_scale(RADIUS / 2, direc_at[j])
            applied_at[j + 1] = c_add(applied_at[j + 1], spread)
            if j > 0:
                applied_at[j - 1] = c_add(applied_at[j - 1], spread)
        for j in range(n + 1):
            field_at[j] = c_add(field_at[j], c_mul(step, direc_at[j]))
        for j in range(n + 2):
            resid_at[j] = c_sub(resid_at[j], c_mul(step, applied_at[j]))
        if n + 1 < ITERS:
            resid = [c_sub(resid[l], c_mul(step, applied[l])) for l in range(len(applied))]
            rho_next = c_mul(resid_at[n + 1], resid[n + 1])
            ratio = c_div(rho_next, rho)
            direc = [c_add(resid[l], c_mul(ratio, direc[l])) for l in range(len(resid))]
            direc_at = [
                c_add(resid_at[j], c_mul(ratio, direc_at[j])) if j <= n else resid_at[j] for j in range(BASIS)
            ]
            rho = rho_next
    return field_at, resid_at


def combine_kernel(forms_ref, basis, field_hbm, resid_hbm, field_ref, resid_ref, sent):
    depth, folds, cols = basis.shape[2] // 3, basis.shape[3], basis.shape[5]
    totals = jnp.broadcast_to(jnp.sum(forms_ref[...], axis=0, keepdims=True), (8, cols))
    lane = lax.broadcasted_iota(jnp.int32, (8, cols), 1)
    sums = [
        jnp.broadcast_to(jnp.sum(jnp.where(lane == i, totals, 0.0), axis=1, keepdims=True), (8, cols))
        for i in range(2 * FORMS)
    ]
    forms = [(sums[2 * f], sums[2 * f + 1]) for f in range(FORMS)]
    moments = forms[:2] + [c_sub(forms[f], forms[f - 2]) for f in range(2, FORMS)]
    field_at, resid_at = step_scalars(moments)

    def copies(p):
        return [
            pltpu.make_async_copy(ref.at[:, p], hbm_ref.at[:, p], sent.at[i, p])
            for i, (ref, hbm_ref) in enumerate(((field_ref, field_hbm), (resid_ref, resid_hbm)))
        ]

    def plane(p, _):
        for q in range(3):
            for j in range(folds):
                re = [basis[k + 1, q, depth + p, j] for k in range(BASIS)]
                im = [basis[k + 1, 3 + q, depth + p, j] for k in range(BASIS)]
                rows = pl.ds(j, 8, stride=folds)
                for out_ref, factors in ((field_ref, field_at[:ITERS]), (resid_ref, resid_at)):
                    out_ref[q, p, rows] = sum(f[0] * re[k] - f[1] * im[k] for k, f in enumerate(factors))
                    out_ref[3 + q, p, rows] = sum(f[0] * im[k] + f[1] * re[k] for k, f in enumerate(factors))
        for copy in copies(p):
            copy.start()
        return 0

    lax.fori_loop(0, depth, plane, 0)
    for p in range(depth):
        for copy in copies(p):
            copy.wait()


def params(limit=VMEM_LIMIT):
    return pltpu.CompilerParams(vmem_limit_bytes=limit)


def krylov(n, lists, mate_list, mate, other, conductivity, omega):
    depth, folds, cols = conductivity.shape[1], conductivity.shape[2] // 8, conductivity.shape[3]
    slots = 2 * lists.shape[1]
    left_shape, right_shape = (2 * 6 * depth // 2 * 8 * folds, 8 * slots), (2 * cols, 8 * slots)
    bases = jax.ShapeDtypeStruct((BASIS + 1, 6, 3 * depth, folds, 8, cols), jnp.float32)
    basis, mine = pl.pallas_call(
        scatter_kernel,
        out_shape=(bases, jax.ShapeDtypeStruct((3, depth, folds, 8, cols), jnp.float32)),
        in_specs=[vmem(), hbm(), smem()],
        out_specs=(vmem(), vmem()),
        scratch_shapes=[
            pltpu.VMEM((2, *left_shape), jnp.bfloat16),
            pltpu.VMEM((2, *right_shape), jnp.bfloat16),
            pltpu.VMEM(conductivity.shape, jnp.float32),
            pltpu.SemaphoreType.DMA,
        ],
        cost_estimate=pl.CostEstimate(
            flops=4 * left_shape[0] * right_shape[0] * 8 * slots, bytes_accessed=4 * 1024 * 1024, transcendentals=0
        ),
        compiler_params=params(),
        name="scatter_source",
    )(lists, pltpu.with_memory_space_constraint(conductivity, pltpu.HBM), omega)
    return pl.pallas_call(
        functools.partial(field_kernel, n),
        out_shape=(jax.ShapeDtypeStruct((n, cols), jnp.float32), bases),
        in_specs=[vmem()] * 4 + [smem(), vmem()],
        out_specs=(vmem(), vmem()),
        scratch_shapes=[
            pltpu.VMEM((3, 2 * HALO + depth, folds, 8, cols), jnp.float32),
            pltpu.VMEM((6, 3 * depth, folds, 8, cols), jnp.float32),
            pltpu.VMEM(left_shape, jnp.bfloat16),
            pltpu.VMEM(right_shape, jnp.bfloat16),
        ],
        input_output_aliases={5: 1},
        compiler_params=params(),
        name="krylov_basis",
    )(mate_list, mate, other, mine, omega, basis)


def combine(forms, basis):
    depth, folds, cols = basis.shape[2] // 3, basis.shape[3], basis.shape[5]
    rows = 8 * folds
    out = jax.ShapeDtypeStruct((6, depth, rows, cols), jnp.float32)
    return pl.pallas_call(
        combine_kernel,
        out_shape=(out, out),
        in_specs=[vmem()] * 2,
        out_specs=(hbm(), hbm()),
        scratch_shapes=[pltpu.VMEM(out.shape, out.dtype)] * 2 + [pltpu.SemaphoreType.DMA((2, depth))],
        compiler_params=params(),
        name="combine_basis",
    )(forms, basis)


def per_device(n, site_owner, site_cell, stencil_code, site_residual, conductivity, omega):
    depth, rows, cols = conductivity.shape[1:]
    sites = site_owner.shape[0]
    cap = 2 * sites // n
    half = cap // 2
    listed = (site_owner.reshape(1, sites), site_cell, stencil_code, site_residual)
    packed, cut = pl.pallas_call(
        functools.partial(bin_kernel, n, half, rows, cols, depth // 2),
        out_shape=(
            jax.ShapeDtypeStruct((n * 2 * half, 2 * 8 * 8), jnp.float32),
            jax.ShapeDtypeStruct((3, HALO, rows, cols), jnp.float32),
        ),
        in_specs=[hbm()] * 5,
        out_specs=(vmem(), vmem()),
        scratch_shapes=[pltpu.VMEM(x.shape, x.dtype) for x in listed] + [pltpu.SemaphoreType.DMA((5,))],
        compiler_params=params(),
        name="bin_sites",
    )(*(pltpu.with_memory_space_constraint(x, pltpu.HBM) for x in (*listed, conductivity)))
    other = lax.ppermute(cut, "gx", [(i, ((i + 1) ^ 1) - 1) for i in range(1, n - 1)])
    late, _ = lax.optimization_barrier((conductivity, cut))
    mate = lax.ppermute(late, "gx", [(i, i ^ 1) for i in range(n)])
    recv = lax.all_to_all(packed.reshape(n, 2 * half, -1), "gx", 0, 0)
    lists = recv.reshape(n, 2, half, -1).transpose(1, 0, 2, 3).reshape(2, n * half, -1)
    mate_list = lax.ppermute(lists[1], "gx", [(i, i ^ 1) for i in range(n)])
    forms, basis = krylov(n, lists, mate_list, mate, other, conductivity, omega)

    forms = lax.all_to_all(forms, "gx", 0, 0, tiled=True)

    return combine(forms, basis)


def solution(mesh):
    placed = (
        P(("period", "gx")),
        P(None, ("period", "gx")),
        P(None, ("period", "gx")),
        P(None, None, ("period", "gx")),
        P(None, "gx", None, None),
        P("period"),
    )
    return jax.shard_map(
        functools.partial(per_device, mesh.shape["gx"]),
        mesh=mesh,
        in_specs=placed,
        out_specs=(P("period", "gx", None, None), P("period", "gx", None, None)),
        check_vma=False,
    )
```

```python
import functools

import jax
import jax.numpy as jnp
from jax import lax
from jax.experimental import pallas as pl
from jax.experimental.pallas import tpu as pltpu
from jax.sharding import PartitionSpec as P

ITERS = 4
CENTRE = 5.0
RADIUS = 5.0
BASIS = ITERS + 1
FORMS = 2 * ITERS
PAIRS = [(i // 2, (i + 1) // 2) for i in range(FORMS)]
HALO = ITERS - 1
STEP = 5
VMEM_LIMIT = 40 * 1024 * 1024
FULL_LIMIT = 62 * 1024 * 1024
CONTRACT_LANES = (((1,), (1,)), ((), ()))


def vmem():
    return pl.BlockSpec(memory_space=pltpu.VMEM)


def smem():
    return pl.BlockSpec(memory_space=pltpu.SMEM)


def hbm():
    return pl.BlockSpec(memory_space=pltpu.HBM)


def split_bf16(x):
    high = x.astype(jnp.bfloat16)
    return high, (x - high.astype(jnp.float32)).astype(jnp.bfloat16)


def bin_kernel(n, half, rows, cols, half_depth, *refs):
    sources, cond_hbm, out_ref, cut_ref, held, arrived = refs[:4], refs[4], refs[5], refs[6], refs[7:11], refs[11]
    copies = [pltpu.make_async_copy(sources[i], held[i], arrived.at[i]) for i in range(4)]
    first = (2 * half_depth - HALO) * (lax.axis_index("gx") % 2)
    copies.append(pltpu.make_async_copy(cond_hbm.at[:, pl.ds(first, HALO)], cut_ref, arrived.at[4]))
    for copy in copies:
        copy.start()
    for copy in copies[:4]:
        copy.wait()
    owner_ref, cell_ref, code_ref, value_ref = held
    sites = owner_ref.shape[1]
    owner = owner_ref[...]
    code = code_ref[...]
    dx = (code >= 9).astype(jnp.int32) + (code >= 18).astype(jnp.int32)
    rest = code - 9 * dx
    dy = (rest >= 3).astype(jnp.int32) + (rest >= 6).astype(jnp.int32)
    dz = rest - 3 * dy
    x = cell_ref[0:1] + dx
    y = cell_ref[1:2] + dy
    z = cell_ref[2:3] + dz
    upper = (x >= half_depth).astype(jnp.int32)
    folds = rows // 8
    row = (x - half_depth * upper) * rows + (y % folds) * 8 + y // folds
    lane = z + cols * upper
    channels, points = value_ref.shape[0], value_ref.shape[1]
    data = jnp.concatenate(
        [value_ref[...].reshape(channels * points, sites), row.astype(jnp.float32), lane.astype(jnp.float32)],
        axis=0,
    )
    blank = jnp.zeros_like(data)

    named = lax.broadcasted_iota(jnp.int32, (n, sites), 0) == owner
    earlier = lax.broadcasted_iota(jnp.int32, (sites, sites), 0) < lax.broadcasted_iota(
        jnp.int32, (sites, sites), 1
    )
    named_f = named.astype(jnp.float32)
    counts = jnp.dot(
        named_f.astype(jnp.bfloat16),
        earlier.astype(jnp.float32).astype(jnp.bfloat16),
        preferred_element_type=jnp.float32,
    )
    rank = jnp.sum(counts * named_f, axis=0, keepdims=True).astype(jnp.int32)
    second = rank >= half
    place = jnp.where(second, rank - half, rank)

    slot = lax.broadcasted_iota(jnp.int32, (out_ref.shape[0], sites), 0)
    odd = owner % 2
    beside = owner + 2 * odd - 1
    hit = jnp.zeros(slot.shape, jnp.bool_)
    for first_row in (2 * owner + 1, 2 * beside):
        hit = hit | (slot == first_row * half + place)
    total = jnp.zeros(out_ref.shape, jnp.float32)
    for part, stacked in (
        (jnp.logical_not(second), [data, blank]),
        (second, [blank, data]),
    ):
        chosen = jnp.where(hit & part, 1.0, 0.0).astype(jnp.bfloat16)
        for piece in split_bf16(jnp.concatenate(stacked, axis=0)):
            total = total + lax.dot_general(
                chosen, piece, CONTRACT_LANES, preferred_element_type=jnp.float32
            )
    out_ref[...] = total
    copies[4].wait()


def scatter_slab(packed, left, right, depth, folds, cols):
    rows = 8 * folds
    half_depth = depth // 2
    channels, points = 6, 8
    row_count, lane_count, slots, width = half_depth * rows, 2 * cols, 2 * packed.shape[0], packed.shape[1] // 2
    row_iota = lax.broadcasted_iota(jnp.int32, (row_count, slots), 0)
    lane_iota = lax.broadcasted_iota(jnp.int32, (lane_count, slots), 0)
    turned = packed.T
    table = jnp.concatenate([turned[:width], turned[width:]], axis=1)
    table_high = table.astype(jnp.bfloat16).astype(jnp.float32)
    table_low = table - table_high
    cell_row = table[channels * points : (channels + 1) * points].astype(jnp.int32)
    cell_lane = table[(channels + 1) * points :].astype(jnp.int32)
    for k in range(points):
        span = slice(k * slots, (k + 1) * slots)
        right[:, span] = jnp.where(lane_iota == cell_lane[k : k + 1], 1.0, 0.0).astype(jnp.bfloat16)
        mask = row_iota == cell_row[k : k + 1]
        for c in range(channels):
            at = c * points + k
            for piece, part in enumerate((table_high, table_low)):
                first = (piece * channels + c) * row_count
                left[first : first + row_count, span] = jnp.where(mask, part[at : at + 1], 0.0).astype(jnp.bfloat16)
    both = lax.dot_general(left[...], right[...], CONTRACT_LANES, preferred_element_type=jnp.float32)
    return both[: channels * row_count] + both[channels * row_count :]


def store_slab(summed, basis, first_plane):
    depth, folds, cols = basis.shape[2] // 3, basis.shape[3], basis.shape[5]
    rows = 8 * folds
    half_depth = depth // 2
    row_count = half_depth * rows
    for c in range(6):
        for x in range(depth):
            first = c * row_count + (x % half_depth) * rows
            lanes = slice((x // half_depth) * cols, (x // half_depth + 1) * cols)
            basis[1, c, first_plane + x] = summed[first : first + rows, lanes].reshape(folds, 8, cols)


def scatter_kernel(list_ref, cond_hbm, omega_ref, basis, mine_ref, left, right, cond_ref, arrived):
    conductivity = pltpu.make_async_copy(cond_hbm, cond_ref, arrived)
    conductivity.start()
    depth, folds = mine_ref.shape[1], mine_ref.shape[2]
    cols = basis.shape[5]
    outer, own = (scatter_slab(list_ref[j], left.at[j], right.at[j], depth, folds, cols) for j in range(2))
    store_slab(own, basis, depth)
    store_slab(outer, basis, 2 * depth * (lax.axis_index("gx") % 2))
    conductivity.wait()
    scale = omega_ref[0] * (2.0 / RADIUS)
    for q in range(3):
        for j in range(folds):
            for x in range(depth):
                mine_ref[q, x, j] = cond_ref[q, x, pl.ds(j, 8, stride=folds)] * scale


def field_kernel(
    n, list_ref, mate_ref, other_ref, mine_ref, omega_ref, _, forms_ref, basis, coupling, faces, left, right
):
    depth, folds, cols = basis.shape[2] // 3, basis.shape[3], basis.shape[5]
    channels = 6
    me = lax.axis_index("gx")
    keep_low = jnp.where(me > 0, 1.0, 0.0).astype(jnp.float32)
    keep_high = jnp.where(me < n - 1, 1.0, 0.0).astype(jnp.float32)

    @pl.when(me >= 0)
    def _():
        store_slab(scatter_slab(list_ref[...], left, right, depth, folds, cols), basis, 2 * depth * (1 - me % 2))


    scale = omega_ref[0] * (2.0 / RADIUS)
    even = me % 2 == 0
    for q in range(3):
        coupling[q, HALO : HALO + depth] = mine_ref[q]
        for j in range(folds):
            fold = pl.ds(j, 8, stride=folds)
            for i in range(HALO):
                below, above = depth - HALO + i, i
                coupling[q, i, j] = jnp.where(even, other_ref[q, i, fold], mate_ref[q, below, fold]) * scale
                coupling[q, HALO + depth + i, j] = (
                    jnp.where(even, mate_ref[q, above, fold], other_ref[q, i, fold]) * scale
                )

    s_iota = lax.broadcasted_iota(jnp.int32, (8, cols), 0)
    z_iota = lax.broadcasted_iota(jnp.int32, (folds, 8, cols), 2)
    s_first, s_last = s_iota == 0, s_iota == 7
    z_first, z_last = z_iota == 0, z_iota == cols - 1

    def ahead_y(f):
        wrapped = jnp.where(s_last, 0.0, pltpu.roll(f[0], 7, 0))
        return jnp.concatenate([f[1:], wrapped[None]], axis=0) - f

    def ahead_z(f):
        return jnp.where(z_last, 0.0, pltpu.roll(f, cols - 1, 2)) - f

    def behind_y(f):
        wrapped = jnp.where(s_first, 0.0, pltpu.roll(f[folds - 1], 1, 0))
        return f - jnp.concatenate([wrapped[None], f[:-1]], axis=0)

    def behind_z(f):
        return f - jnp.where(z_first, 0.0, pltpu.roll(f, 1, 2))

    weight = 2.0 / RADIUS
    centre = 2.0 * CENTRE / RADIUS

    def edges(k, p):
        return [basis[k, c, p] for c in range(channels)]

    def faces_of(here, there):
        result = []
        for part in range(2):
            ex, ey, ez = here[3 * part : 3 * part + 3]
            ey_next, ez_next = there[3 * part + 1], there[3 * part + 2]
            result.append(ahead_y(ez) - ahead_z(ey))
            result.append(ahead_z(ex) - (ez_next - ez))
            result.append((ey_next - ey) - ahead_y(ex))
        return result

    def keep_faces(p, values):
        for c in range(channels):
            faces[c, p] = values[c]

    def plane(here, older, coupled, face, face_before):
        new = []
        for part in range(2):
            hx, hy, hz = face[3 * part : 3 * part + 3]
            hy_before, hz_before = face_before[2 * part], face_before[2 * part + 1]
            curls = (
                behind_y(hz) - behind_z(hy),
                behind_z(hx) - (hz - hz_before),
                (hy - hy_before) - behind_y(hx),
            )
            for q in range(3):
                other = coupled[q] * here[3 * (1 - part) + q]
                rest = centre * here[3 * part + q]
                if older[3 * part + q] is not None:
                    rest = rest + older[3 * part + q]
                value = weight * curls[q] - rest
                new.append(value + other if part == 0 else value - other)
        return new

    def apply(k):
        end = 3 * depth - k

        def step(p, count):
            after = range(p + count, min(p + 2 * count, end))
            fields = [edges(k, p + d) for d in range(count)]
            older = [edges(k - 1, p + d) if k > 1 else [None] * channels for d in range(count)]
            coupled = [[coupling[q, p + d - (depth - HALO)] for q in range(3)] for d in range(count)]
            face = [[faces[c, p + d] for c in range(channels)] for d in range(-1, count)]
            following = [edges(k, x) for x in range(p + count, after.stop + 1)] if after else []
            next_faces = [faces_of(following[d], following[d + 1]) for d in range(len(after))]
            new = []
            for d in range(count):
                before = [face[d][c] for c in (1, 2, 4, 5)]
                if p + d == depth:
                    before = [f * keep_low for f in before]
                new.append(plane(fields[d], older[d], coupled[d], face[d + 1], before))
                if p + d == 2 * depth:
                    new[d] = [f * keep_high for f in new[d]]
            for d in range(count):
                for c in range(channels):
                    basis[k + 1, c, p + d] = new[d][c]
            for x, values in zip(after, next_faces):
                keep_faces(x, values)

        first = [edges(k, x) for x in range(k - 1, min(k + STEP, end) + 1)]
        for d in range(len(first) - 1):
            keep_faces(k - 1 + d, faces_of(first[d], first[d + 1]))
        for p in range(k, end, STEP):
            step(p, min(STEP, end - p))

    for k in range(1, BASIS):
        pl.when(me >= 0)(functools.partial(apply, k))

    def plane_forms(p, sums):
        sums = list(sums)
        for q in range(3):
            re = [basis[k + 1, q, p] for k in range(BASIS)]
            im = [basis[k + 1, 3 + q, p] for k in range(BASIS)]
            for f, (i, j) in enumerate(PAIRS):
                real = re[i] * re[j] - im[i] * im[j]
                imag = re[i] * im[j] + im[i] * re[j] if i != j else 2.0 * (re[i] * im[i])
                for half, term in ((0, real), (1, imag)):
                    sums[2 * f + half] = sums[2 * f + half] + jnp.sum(term, axis=0)
        return tuple(sums)

    zero = jnp.zeros((8, cols), jnp.float32)
    sums = lax.fori_loop(depth, 2 * depth, plane_forms, (zero,) * (2 * FORMS), unroll=2)
    folded = jnp.concatenate([jnp.sum(total, axis=0, keepdims=True) for total in sums], axis=0)
    totals = jnp.sum(folded, axis=1, keepdims=True)
    diagonal = lax.broadcasted_iota(jnp.int32, folded.shape, 0) == lax.broadcasted_iota(jnp.int32, folded.shape, 1)
    line = jnp.sum(jnp.where(diagonal, totals, 0.0), axis=0, keepdims=True)
    forms_ref[...] = jnp.broadcast_to(line, forms_ref.shape)


def c_add(a, b):
    return a[0] + b[0], a[1] + b[1]


def c_sub(a, b):
    return a[0] - b[0], a[1] - b[1]


def c_mul(a, b):
    return a[0] * b[0] - a[1] * b[1], a[0] * b[1] + a[1] * b[0]


def c_scale(s, a):
    return s * a[0], s * a[1]


def c_div(a, b):
    inverse = 1.0 / (b[0] * b[0] + b[1] * b[1])
    return (a[0] * b[0] + a[1] * b[1]) * inverse, (a[1] * b[0] - a[0] * b[1]) * inverse


def step_scalars(moments):
    resid = list(moments)
    direc = list(moments)
    none = (jnp.zeros_like(moments[0][0]),) * 2
    one = (jnp.ones_like(moments[0][0]), jnp.zeros_like(moments[0][0]))
    resid_at = [one] + [none] * ITERS
    direc_at = [one] + [none] * ITERS
    field_at = [none] * BASIS
    rho = moments[0]
    for n in range(ITERS):
        applied = [c_add(c_scale(CENTRE, direc[0]), c_scale(RADIUS / 2, direc[1]))]
        for l in range(1, len(direc) - 1):
            near = c_scale(RADIUS / 2, c_add(direc[l + 1], direc[l - 1]))
            applied.append(c_add(c_scale(CENTRE, direc[l]), near))
        step = c_div(rho, c_mul(direc_at[n], applied[n]))
        applied_at = [c_scale(CENTRE, direc_at[j]) if j <= n else none for j in range(BASIS)]
        for j in range(n + 1):
            spread = c_scale(RADIUS / 2, direc_at[j])
            applied_at[j + 1] = c_add(applied_at[j + 1], spread)
            if j > 0:
                applied_at[j - 1] = c_add(applied_at[j - 1], spread)
        for j in range(n + 1):
            field_at[j] = c_add(field_at[j], c_mul(step, direc_at[j]))
        for j in range(n + 2):
            resid_at[j] = c_sub(resid_at[j], c_mul(step, applied_at[j]))
        if n + 1 < ITERS:
            resid = [c_sub(resid[l], c_mul(step, applied[l])) for l in range(len(applied))]
            rho_next = c_mul(resid_at[n + 1], resid[n + 1])
            ratio = c_div(rho_next, rho)
            direc = [c_add(resid[l], c_mul(ratio, direc[l])) for l in range(len(resid))]
            direc_at = [
                c_add(resid_at[j], c_mul(ratio, direc_at[j])) if j <= n else resid_at[j] for j in range(BASIS)
            ]
            rho = rho_next
    return field_at, resid_at


def combine_kernel(forms_ref, basis, field_hbm, resid_hbm, field_ref, resid_ref, sent):
    depth, folds, cols = basis.shape[2] // 3, basis.shape[3], basis.shape[5]
    totals = jnp.broadcast_to(jnp.sum(forms_ref[...], axis=0, keepdims=True), (8, cols))
    lane = lax.broadcasted_iota(jnp.int32, (8, cols), 1)
    sums = [
        jnp.broadcast_to(jnp.sum(jnp.where(lane == i, totals, 0.0), axis=1, keepdims=True), (8, cols))
        for i in range(2 * FORMS)
    ]
    forms = [(sums[2 * f], sums[2 * f + 1]) for f in range(FORMS)]
    moments = forms[:2] + [c_sub(forms[f], forms[f - 2]) for f in range(2, FORMS)]
    field_at, resid_at = step_scalars(moments)

    def copies(p):
        return [
            pltpu.make_async_copy(ref.at[:, p], hbm_ref.at[:, p], sent.at[i, p])
            for i, (ref, hbm_ref) in enumerate(((field_ref, field_hbm), (resid_ref, resid_hbm)))
        ]

    def plane(p, _):
        for q in range(3):
            for j in range(folds):
                re = [basis[k + 1, q, depth + p, j] for k in range(BASIS)]
                im = [basis[k + 1, 3 + q, depth + p, j] for k in range(BASIS)]
                rows = pl.ds(j, 8, stride=folds)
                for out_ref, factors in ((field_ref, field_at[:ITERS]), (resid_ref, resid_at)):
                    out_ref[q, p, rows] = sum(f[0] * re[k] - f[1] * im[k] for k, f in enumerate(factors))
                    out_ref[3 + q, p, rows] = sum(f[0] * im[k] + f[1] * re[k] for k, f in enumerate(factors))
        for copy in copies(p):
            copy.start()
        return 0

    lax.fori_loop(0, depth, plane, 0)
    for p in range(depth):
        for copy in copies(p):
            copy.wait()


def params(limit=VMEM_LIMIT):
    return pltpu.CompilerParams(vmem_limit_bytes=limit)


def krylov(n, lists, mate_list, mate, other, conductivity, omega):
    depth, folds, cols = conductivity.shape[1], conductivity.shape[2] // 8, conductivity.shape[3]
    slots = 2 * lists.shape[1]
    left_shape, right_shape = (2 * 6 * depth // 2 * 8 * folds, 8 * slots), (2 * cols, 8 * slots)
    bases = jax.ShapeDtypeStruct((BASIS + 1, 6, 3 * depth, folds, 8, cols), jnp.float32)
    basis, mine = pl.pallas_call(
        scatter_kernel,
        out_shape=(bases, jax.ShapeDtypeStruct((3, depth, folds, 8, cols), jnp.float32)),
        in_specs=[vmem(), hbm(), smem()],
        out_specs=(vmem(), vmem()),
        scratch_shapes=[
            pltpu.VMEM((2, *left_shape), jnp.bfloat16),
            pltpu.VMEM((2, *right_shape), jnp.bfloat16),
            pltpu.VMEM(conductivity.shape, jnp.float32),
            pltpu.SemaphoreType.DMA,
        ],
        cost_estimate=pl.CostEstimate(
            flops=4 * left_shape[0] * right_shape[0] * 8 * slots, bytes_accessed=4 * 1024 * 1024, transcendentals=0
        ),
        compiler_params=params(),
        name="scatter_source",
    )(lists, pltpu.with_memory_space_constraint(conductivity, pltpu.HBM), omega)
    return pl.pallas_call(
        functools.partial(field_kernel, n),
        out_shape=(jax.ShapeDtypeStruct((n, cols), jnp.float32), bases),
        in_specs=[vmem()] * 4 + [smem(), vmem()],
        out_specs=(vmem(), vmem()),
        scratch_shapes=[
            pltpu.VMEM((3, 2 * HALO + depth, folds, 8, cols), jnp.float32),
            pltpu.VMEM((6, 3 * depth, folds, 8, cols), jnp.float32),
            pltpu.VMEM(left_shape, jnp.bfloat16),
            pltpu.VMEM(right_shape, jnp.bfloat16),
        ],
        input_output_aliases={5: 1},
        compiler_params=params(),
        name="krylov_basis",
    )(mate_list, mate, other, mine, omega, basis)


def combine(forms, basis):
    depth, folds, cols = basis.shape[2] // 3, basis.shape[3], basis.shape[5]
    rows = 8 * folds
    out = jax.ShapeDtypeStruct((6, depth, rows, cols), jnp.float32)
    return pl.pallas_call(
        combine_kernel,
        out_shape=(out, out),
        in_specs=[vmem()] * 2,
        out_specs=(hbm(), hbm()),
        scratch_shapes=[pltpu.VMEM(out.shape, out.dtype)] * 2 + [pltpu.SemaphoreType.DMA((2, depth))],
        compiler_params=params(),
        name="combine_basis",
    )(forms, basis)


def outer_pairs(periods, n):
    pairs = []
    for p in range(periods):
        pairs += [(p * n + i, p * n + ((i + 1) ^ 1) - 1) for i in range(1, n - 1)]
        if periods % 2 == 0:
            pairs += [(p * n + i, (p ^ 1) * n + i) for i in (0, n - 1)]
    return pairs


def per_device(periods, n, site_owner, site_cell, stencil_code, site_residual, conductivity, omega):
    depth, rows, cols = conductivity.shape[1:]
    sites = site_owner.shape[0]
    cap = 2 * sites // n
    half = cap // 2
    listed = (site_owner.reshape(1, sites), site_cell, stencil_code, site_residual)
    packed, cut = pl.pallas_call(
        functools.partial(bin_kernel, n, half, rows, cols, depth // 2),
        out_shape=(
            jax.ShapeDtypeStruct((n * 2 * half, 2 * 8 * 8), jnp.float32),
            jax.ShapeDtypeStruct((3, HALO, rows, cols), jnp.float32),
        ),
        in_specs=[hbm()] * 5,
        out_specs=(vmem(), vmem()),
        scratch_shapes=[pltpu.VMEM(x.shape, x.dtype) for x in listed] + [pltpu.SemaphoreType.DMA((5,))],
        compiler_params=params(),
        name="bin_sites",
    )(*(pltpu.with_memory_space_constraint(x, pltpu.HBM) for x in (*listed, conductivity)))
    other = lax.ppermute(cut, ("period", "gx"), outer_pairs(periods, n))
    mate = lax.ppermute(conductivity, "gx", [(i, i ^ 1) for i in range(n)])
    recv = lax.all_to_all(packed.reshape(n, 2 * half, -1), "gx", 0, 0)
    lists = recv.reshape(n, 2, half, -1).transpose(1, 0, 2, 3).reshape(2, n * half, -1)
    mate_list = lax.ppermute(lists[1], "gx", [(i, i ^ 1) for i in range(n)])
    forms, basis = krylov(n, lists, mate_list, mate, other, conductivity, omega)

    forms = lax.all_to_all(forms, "gx", 0, 0, tiled=True)

    return combine(forms, basis)


def solution(mesh):
    placed = (
        P(("period", "gx")),
        P(None, ("period", "gx")),
        P(None, ("period", "gx")),
        P(None, None, ("period", "gx")),
        P(None, "gx", None, None),
        P("period"),
    )
    return jax.shard_map(
        functools.partial(per_device, mesh.shape["period"], mesh.shape["gx"]),
        mesh=mesh,
        in_specs=placed,
        out_specs=(P("period", "gx", None, None), P("period", "gx", None, None)),
        check_vma=False,
    )
```

```python
import functools

import jax
import jax.numpy as jnp
from jax import lax
from jax.experimental import pallas as pl
from jax.experimental.pallas import tpu as pltpu
from jax.sharding import PartitionSpec as P

ITERS = 4
CENTRE = 5.0
RADIUS = 5.0
BASIS = ITERS + 1
FORMS = 2 * ITERS
PAIRS = [(i // 2, (i + 1) // 2) for i in range(FORMS)]
HALO = ITERS - 1
STEP = 5
VMEM_LIMIT = 40 * 1024 * 1024
FULL_LIMIT = 62 * 1024 * 1024
CONTRACT_LANES = (((1,), (1,)), ((), ()))


def vmem():
    return pl.BlockSpec(memory_space=pltpu.VMEM)


def smem():
    return pl.BlockSpec(memory_space=pltpu.SMEM)


def hbm():
    return pl.BlockSpec(memory_space=pltpu.HBM)


def split_bf16(x):
    high = x.astype(jnp.bfloat16)
    return high, (x - high.astype(jnp.float32)).astype(jnp.bfloat16)


def bin_kernel(n, half, rows, cols, half_depth, *refs):
    sources, cond_hbm, out_ref, cut_ref, held, arrived = refs[:4], refs[4], refs[5], refs[6], refs[7:11], refs[11]
    copies = [pltpu.make_async_copy(sources[i], held[i], arrived.at[i]) for i in range(4)]
    first = (2 * half_depth - HALO) * (lax.axis_index("gx") % 2)
    copies.append(pltpu.make_async_copy(cond_hbm.at[:, pl.ds(first, HALO)], cut_ref, arrived.at[4]))
    for copy in copies:
        copy.start()
    for copy in copies[:4]:
        copy.wait()
    owner_ref, cell_ref, code_ref, value_ref = held
    sites = owner_ref.shape[1]
    owner = owner_ref[...]
    code = code_ref[...]
    dx = (code >= 9).astype(jnp.int32) + (code >= 18).astype(jnp.int32)
    rest = code - 9 * dx
    dy = (rest >= 3).astype(jnp.int32) + (rest >= 6).astype(jnp.int32)
    dz = rest - 3 * dy
    x = cell_ref[0:1] + dx
    y = cell_ref[1:2] + dy
    z = cell_ref[2:3] + dz
    upper = (x >= half_depth).astype(jnp.int32)
    folds = rows // 8
    row = (x - half_depth * upper) * rows + (y % folds) * 8 + y // folds
    lane = z + cols * upper
    channels, points = value_ref.shape[0], value_ref.shape[1]
    data = jnp.concatenate(
        [value_ref[...].reshape(channels * points, sites), row.astype(jnp.float32), lane.astype(jnp.float32)],
        axis=0,
    )

    named = lax.broadcasted_iota(jnp.int32, (n, sites), 0) == owner
    earlier = lax.broadcasted_iota(jnp.int32, (sites, sites), 0) < lax.broadcasted_iota(
        jnp.int32, (sites, sites), 1
    )
    named_f = named.astype(jnp.float32)
    counts = jnp.dot(
        named_f.astype(jnp.bfloat16),
        earlier.astype(jnp.float32).astype(jnp.bfloat16),
        preferred_element_type=jnp.float32,
    )
    rank = jnp.sum(counts * named_f, axis=0, keepdims=True).astype(jnp.int32)
    second = rank >= half
    place = jnp.where(second, rank - half, rank)

    slot = lax.broadcasted_iota(jnp.int32, (out_ref.shape[0], sites), 0)
    odd = owner % 2
    beside = owner + 2 * odd - 1
    hit = jnp.zeros(slot.shape, jnp.bool_)
    for first_row in (2 * owner + 1, 2 * beside):
        hit = hit | (slot == first_row * half + place)
    chosen = [jnp.where(hit & part, 1.0, 0.0).astype(jnp.bfloat16) for part in (jnp.logical_not(second), second)]
    stacked = []
    for piece in split_bf16(data):
        blank = jnp.zeros_like(piece)
        stacked += [jnp.concatenate([piece, blank], axis=1), jnp.concatenate([blank, piece], axis=1)]
    both = lax.dot_general(
        jnp.concatenate(chosen, axis=1),
        jnp.concatenate(stacked, axis=0),
        CONTRACT_LANES,
        preferred_element_type=jnp.float32,
    )
    width = out_ref.shape[1]
    total = both[:, :width] + both[:, width:]
    out_ref[...] = total
    copies[4].wait()


def scatter_slab(packed, left, right, depth, folds, cols):
    rows = 8 * folds
    half_depth = depth // 2
    channels, points = 6, 8
    row_count, lane_count, slots, width = half_depth * rows, 2 * cols, 2 * packed.shape[0], packed.shape[1] // 2
    row_iota = lax.broadcasted_iota(jnp.int32, (row_count, slots), 0)
    lane_iota = lax.broadcasted_iota(jnp.int32, (lane_count, slots), 0)
    turned = packed.T
    table = jnp.concatenate([turned[:width], turned[width:]], axis=1)
    table_high = table.astype(jnp.bfloat16).astype(jnp.float32)
    table_low = table - table_high
    cell_row = table[channels * points : (channels + 1) * points].astype(jnp.int32)
    cell_lane = table[(channels + 1) * points :].astype(jnp.int32)
    for k in range(points):
        span = slice(k * slots, (k + 1) * slots)
        right[:, span] = jnp.where(lane_iota == cell_lane[k : k + 1], 1.0, 0.0).astype(jnp.bfloat16)
        mask = row_iota == cell_row[k : k + 1]
        for c in range(channels):
            at = c * points + k
            for piece, part in enumerate((table_high, table_low)):
                first = (piece * channels + c) * row_count
                left[first : first + row_count, span] = jnp.where(mask, part[at : at + 1], 0.0).astype(jnp.bfloat16)
    both = lax.dot_general(left[...], right[...], CONTRACT_LANES, preferred_element_type=jnp.float32)
    return both[: channels * row_count] + both[channels * row_count :]


def store_slab(summed, basis, first_plane):
    depth, folds, cols = basis.shape[2] // 3, basis.shape[3], basis.shape[5]
    rows = 8 * folds
    half_depth = depth // 2
    row_count = half_depth * rows
    for c in range(6):
        for x in range(depth):
            first = c * row_count + (x % half_depth) * rows
            lanes = slice((x // half_depth) * cols, (x // half_depth + 1) * cols)
            basis[1, c, first_plane + x] = summed[first : first + rows, lanes].reshape(folds, 8, cols)


def scatter_kernel(list_ref, cond_hbm, basis, mine_ref, left, right, arrived):
    conductivity = pltpu.make_async_copy(cond_hbm, mine_ref, arrived)
    conductivity.start()
    depth, folds, cols = basis.shape[2] // 3, basis.shape[3], basis.shape[5]
    outer, own = (scatter_slab(list_ref[j], left.at[j], right.at[j], depth, folds, cols) for j in range(2))
    store_slab(own, basis, depth)
    store_slab(outer, basis, 2 * depth * (lax.axis_index("gx") % 2))
    conductivity.wait()


def field_kernel(
    n, list_ref, mate_ref, other_ref, mine_ref, omega_ref, _, forms_ref, basis, coupling, faces, left, right
):
    depth, folds, cols = basis.shape[2] // 3, basis.shape[3], basis.shape[5]
    channels = 6
    me = lax.axis_index("gx")
    keep_low = jnp.where(me > 0, 1.0, 0.0).astype(jnp.float32)
    keep_high = jnp.where(me < n - 1, 1.0, 0.0).astype(jnp.float32)

    scale = omega_ref[0] * (2.0 / RADIUS)
    even = me % 2 == 0

    @pl.when(me >= 0)
    def _():
        third = scatter_slab(list_ref[...], left, right, depth, folds, cols)
        for q in range(3):
            for j in range(folds):
                fold = pl.ds(j, 8, stride=folds)
                for x in range(depth):
                    coupling[q, HALO + x, j] = mine_ref[q, x, fold] * scale
                for i in range(HALO):
                    below, above = depth - HALO + i, i
                    coupling[q, i, j] = jnp.where(even, other_ref[q, i, fold], mate_ref[q, below, fold]) * scale
                    coupling[q, HALO + depth + i, j] = (
                        jnp.where(even, mate_ref[q, above, fold], other_ref[q, i, fold]) * scale
                    )
        store_slab(third, basis, 2 * depth * (1 - me % 2))

    s_iota = lax.broadcasted_iota(jnp.int32, (8, cols), 0)
    z_iota = lax.broadcasted_iota(jnp.int32, (folds, 8, cols), 2)
    s_first, s_last = s_iota == 0, s_iota == 7
    z_first, z_last = z_iota == 0, z_iota == cols - 1

    def ahead_y(f):
        wrapped = jnp.where(s_last, 0.0, pltpu.roll(f[0], 7, 0))
        return jnp.concatenate([f[1:], wrapped[None]], axis=0) - f

    def ahead_z(f):
        return jnp.where(z_last, 0.0, pltpu.roll(f, cols - 1, 2)) - f

    def behind_y(f):
        wrapped = jnp.where(s_first, 0.0, pltpu.roll(f[folds - 1], 1, 0))
        return f - jnp.concatenate([wrapped[None], f[:-1]], axis=0)

    def behind_z(f):
        return f - jnp.where(z_first, 0.0, pltpu.roll(f, 1, 2))

    weight = 2.0 / RADIUS
    centre = 2.0 * CENTRE / RADIUS

    def edges(k, p):
        return [basis[k, c, p] for c in range(channels)]

    def faces_of(here, there):
        result = []
        for part in range(2):
            ex, ey, ez = here[3 * part : 3 * part + 3]
            ey_next, ez_next = there[3 * part + 1], there[3 * part + 2]
            result.append(ahead_y(ez) - ahead_z(ey))
            result.append(ahead_z(ex) - (ez_next - ez))
            result.append((ey_next - ey) - ahead_y(ex))
        return result

    def keep_faces(p, values):
        for c in range(channels):
            faces[c, p] = values[c]

    def plane(here, older, coupled, face, face_before):
        new = []
        for part in range(2):
            hx, hy, hz = face[3 * part : 3 * part + 3]
            hy_before, hz_before = face_before[2 * part], face_before[2 * part + 1]
            curls = (
                behind_y(hz) - behind_z(hy),
                behind_z(hx) - (hz - hz_before),
                (hy - hy_before) - behind_y(hx),
            )
            for q in range(3):
                other = coupled[q] * here[3 * (1 - part) + q]
                rest = centre * here[3 * part + q]
                if older[3 * part + q] is not None:
                    rest = rest + older[3 * part + q]
                value = weight * curls[q] - rest
                new.append(value + other if part == 0 else value - other)
        return new

    def apply(k):
        end = 3 * depth - k

        def step(p, count):
            after = range(p + count, min(p + 2 * count, end))
            fields = [edges(k, p + d) for d in range(count)]
            older = [edges(k - 1, p + d) if k > 1 else [None] * channels for d in range(count)]
            coupled = [[coupling[q, p + d - (depth - HALO)] for q in range(3)] for d in range(count)]
            face = [[faces[c, p + d] for c in range(channels)] for d in range(-1, count)]
            following = [edges(k, x) for x in range(p + count, after.stop + 1)] if after else []
            next_faces = [faces_of(following[d], following[d + 1]) for d in range(len(after))]
            new = []
            for d in range(count):
                before = [face[d][c] for c in (1, 2, 4, 5)]
                if p + d == depth:
                    before = [f * keep_low for f in before]
                new.append(plane(fields[d], older[d], coupled[d], face[d + 1], before))
                if p + d == 2 * depth:
                    new[d] = [f * keep_high for f in new[d]]
            for d in range(count):
                for c in range(channels):
                    basis[k + 1, c, p + d] = new[d][c]
            for x, values in zip(after, next_faces):
                keep_faces(x, values)

        first = [edges(k, x) for x in range(k - 1, min(k + STEP, end) + 1)]
        for d in range(len(first) - 1):
            keep_faces(k - 1 + d, faces_of(first[d], first[d + 1]))
        for p in range(k, end, STEP):
            step(p, min(STEP, end - p))

    for k in range(1, BASIS):
        pl.when(me >= 0)(functools.partial(apply, k))

    def some_forms(p, sums):
        sums = list(sums)
        for q, fold in [(q, fold) for q in range(3) for fold in range(folds)]:
            re = [basis[k + 1, q, p, fold] for k in range(BASIS)]
            im = [basis[k + 1, 3 + q, p, fold] for k in range(BASIS)]
            for f, (i, j) in enumerate(PAIRS):
                real = re[i] * re[j] - im[i] * im[j]
                imag = re[i] * im[j] + im[i] * re[j] if i != j else re[i] * im[i]
                sums[2 * f] = sums[2 * f] + real
                sums[2 * f + 1] = sums[2 * f + 1] + imag
        return tuple(sums)

    zero = jnp.zeros((8, cols), jnp.float32)
    sums = lax.fori_loop(depth, 2 * depth, some_forms, (zero,) * (2 * FORMS), unroll=2)
    sums = list(sums)
    for f, (i, j) in enumerate(PAIRS):
        if i == j:
            sums[2 * f + 1] = 2.0 * sums[2 * f + 1]
    folded = jnp.concatenate([jnp.sum(total, axis=0, keepdims=True) for total in sums], axis=0)
    totals = jnp.sum(folded, axis=1, keepdims=True)
    diagonal = lax.broadcasted_iota(jnp.int32, folded.shape, 0) == lax.broadcasted_iota(jnp.int32, folded.shape, 1)
    line = jnp.sum(jnp.where(diagonal, totals, 0.0), axis=0, keepdims=True)
    forms_ref[...] = jnp.broadcast_to(line, forms_ref.shape)


def c_add(a, b):
    return a[0] + b[0], a[1] + b[1]


def c_sub(a, b):
    return a[0] - b[0], a[1] - b[1]


def c_mul(a, b):
    return a[0] * b[0] - a[1] * b[1], a[0] * b[1] + a[1] * b[0]


def c_scale(s, a):
    return s * a[0], s * a[1]


def c_div(a, b):
    inverse = 1.0 / (b[0] * b[0] + b[1] * b[1])
    return (a[0] * b[0] + a[1] * b[1]) * inverse, (a[1] * b[0] - a[0] * b[1]) * inverse


def step_scalars(moments):
    resid = list(moments)
    direc = list(moments)
    none = (jnp.zeros_like(moments[0][0]),) * 2
    one = (jnp.ones_like(moments[0][0]), jnp.zeros_like(moments[0][0]))
    resid_at = [one] + [none] * ITERS
    direc_at = [one] + [none] * ITERS
    field_at = [none] * BASIS
    rho = moments[0]
    for n in range(ITERS):
        applied = [c_add(c_scale(CENTRE, direc[0]), c_scale(RADIUS / 2, direc[1]))]
        for l in range(1, len(direc) - 1):
            near = c_scale(RADIUS / 2, c_add(direc[l + 1], direc[l - 1]))
            applied.append(c_add(c_scale(CENTRE, direc[l]), near))
        step = c_div(rho, c_mul(direc_at[n], applied[n]))
        applied_at = [c_scale(CENTRE, direc_at[j]) if j <= n else none for j in range(BASIS)]
        for j in range(n + 1):
            spread = c_scale(RADIUS / 2, direc_at[j])
            applied_at[j + 1] = c_add(applied_at[j + 1], spread)
            if j > 0:
                applied_at[j - 1] = c_add(applied_at[j - 1], spread)
        for j in range(n + 1):
            field_at[j] = c_add(field_at[j], c_mul(step, direc_at[j]))
        for j in range(n + 2):
            resid_at[j] = c_sub(resid_at[j], c_mul(step, applied_at[j]))
        if n + 1 < ITERS:
            resid = [c_sub(resid[l], c_mul(step, applied[l])) for l in range(len(applied))]
            rho_next = c_mul(resid_at[n + 1], resid[n + 1])
            ratio = c_div(rho_next, rho)
            direc = [c_add(resid[l], c_mul(ratio, direc[l])) for l in range(len(resid))]
            direc_at = [
                c_add(resid_at[j], c_mul(ratio, direc_at[j])) if j <= n else resid_at[j] for j in range(BASIS)
            ]
            rho = rho_next
    return field_at, resid_at


def combine_kernel(forms_ref, basis, field_hbm, resid_hbm, field_ref, resid_ref, sent):
    depth, folds, cols = basis.shape[2] // 3, basis.shape[3], basis.shape[5]
    totals = jnp.broadcast_to(jnp.sum(forms_ref[...], axis=0, keepdims=True), (8, cols))
    lane = lax.broadcasted_iota(jnp.int32, (8, cols), 1)
    sums = [
        jnp.broadcast_to(jnp.sum(jnp.where(lane == i, totals, 0.0), axis=1, keepdims=True), (8, cols))
        for i in range(2 * FORMS)
    ]
    forms = [(sums[2 * f], sums[2 * f + 1]) for f in range(FORMS)]
    moments = forms[:2] + [c_sub(forms[f], forms[f - 2]) for f in range(2, FORMS)]
    field_at, resid_at = step_scalars(moments)

    def copies(p):
        return [
            pltpu.make_async_copy(ref.at[:, p], hbm_ref.at[:, p], sent.at[i, p])
            for i, (ref, hbm_ref) in enumerate(((field_ref, field_hbm), (resid_ref, resid_hbm)))
        ]

    def plane(p, _):
        for q in range(3):
            for j in range(folds):
                re = [basis[k + 1, q, depth + p, j] for k in range(BASIS)]
                im = [basis[k + 1, 3 + q, depth + p, j] for k in range(BASIS)]
                rows = pl.ds(j, 8, stride=folds)
                for out_ref, factors in ((field_ref, field_at[:ITERS]), (resid_ref, resid_at)):
                    out_ref[q, p, rows] = sum(f[0] * re[k] - f[1] * im[k] for k, f in enumerate(factors))
                    out_ref[3 + q, p, rows] = sum(f[0] * im[k] + f[1] * re[k] for k, f in enumerate(factors))
        for copy in copies(p):
            copy.start()
        return 0

    lax.fori_loop(0, depth, plane, 0)
    for p in range(depth):
        for copy in copies(p):
            copy.wait()


def params(limit=VMEM_LIMIT):
    return pltpu.CompilerParams(vmem_limit_bytes=limit)


def krylov(n, lists, mate_list, mate, other, conductivity, omega):
    depth, folds, cols = conductivity.shape[1], conductivity.shape[2] // 8, conductivity.shape[3]
    slots = 2 * lists.shape[1]
    left_shape, right_shape = (2 * 6 * depth // 2 * 8 * folds, 8 * slots), (2 * cols, 8 * slots)
    bases = jax.ShapeDtypeStruct((BASIS + 1, 6, 3 * depth, folds, 8, cols), jnp.float32)
    basis, mine = pl.pallas_call(
        scatter_kernel,
        out_shape=(bases, jax.ShapeDtypeStruct(conductivity.shape, jnp.float32)),
        in_specs=[vmem(), hbm()],
        out_specs=(vmem(), vmem()),
        scratch_shapes=[
            pltpu.VMEM((2, *left_shape), jnp.bfloat16),
            pltpu.VMEM((2, *right_shape), jnp.bfloat16),
            pltpu.SemaphoreType.DMA,
        ],
        cost_estimate=pl.CostEstimate(
            flops=4 * left_shape[0] * right_shape[0] * 8 * slots, bytes_accessed=4 * 1024 * 1024, transcendentals=0
        ),
        compiler_params=params(),
        name="scatter_source",
    )(lists, pltpu.with_memory_space_constraint(conductivity, pltpu.HBM))
    return pl.pallas_call(
        functools.partial(field_kernel, n),
        out_shape=(jax.ShapeDtypeStruct((n, cols), jnp.float32), bases),
        in_specs=[vmem()] * 4 + [smem(), vmem()],
        out_specs=(vmem(), vmem()),
        scratch_shapes=[
            pltpu.VMEM((3, 2 * HALO + depth, folds, 8, cols), jnp.float32),
            pltpu.VMEM((6, 3 * depth, folds, 8, cols), jnp.float32),
            pltpu.VMEM(left_shape, jnp.bfloat16),
            pltpu.VMEM(right_shape, jnp.bfloat16),
        ],
        input_output_aliases={5: 1},
        compiler_params=params(),
        name="krylov_basis",
    )(mate_list, mate, other, mine, omega, basis)


def combine(forms, basis):
    depth, folds, cols = basis.shape[2] // 3, basis.shape[3], basis.shape[5]
    rows = 8 * folds
    out = jax.ShapeDtypeStruct((6, depth, rows, cols), jnp.float32)
    return pl.pallas_call(
        combine_kernel,
        out_shape=(out, out),
        in_specs=[vmem()] * 2,
        out_specs=(hbm(), hbm()),
        scratch_shapes=[pltpu.VMEM(out.shape, out.dtype)] * 2 + [pltpu.SemaphoreType.DMA((2, depth))],
        compiler_params=params(),
        name="combine_basis",
    )(forms, basis)


def bin_sites(n, listed, conductivity):
    depth, rows, cols = conductivity.shape[1:]
    half = listed[0].shape[1] // n
    return pl.pallas_call(
        functools.partial(bin_kernel, n, half, rows, cols, depth // 2),
        out_shape=(
            jax.ShapeDtypeStruct((n * 2 * half, 2 * 8 * 8), jnp.float32),
            jax.ShapeDtypeStruct((3, HALO, rows, cols), jnp.float32),
        ),
        in_specs=[hbm()] * 5,
        out_specs=(vmem(), vmem()),
        scratch_shapes=[pltpu.VMEM(x.shape, x.dtype) for x in listed] + [pltpu.SemaphoreType.DMA((5,))],
        compiler_params=params(),
        name="bin_sites",
    )(*(pltpu.with_memory_space_constraint(x, pltpu.HBM) for x in (*listed, conductivity)))


def outer_pairs(periods, n):
    pairs = []
    for p in range(periods):
        pairs += [(p * n + i, p * n + ((i + 1) ^ 1) - 1) for i in range(1, n - 1)]
        if periods % 2 == 0:
            pairs += [(p * n + i, (p ^ 1) * n + i) for i in (0, n - 1)]
    return pairs


def per_device(periods, n, site_owner, site_cell, stencil_code, site_residual, conductivity, omega):
    depth, rows, cols = conductivity.shape[1:]
    sites = site_owner.shape[0]
    cap = 2 * sites // n
    half = cap // 2
    listed = (site_owner.reshape(1, sites), site_cell, stencil_code, site_residual)
    packed, cut = bin_sites(n, listed, conductivity)
    other = lax.ppermute(cut, ("period", "gx"), outer_pairs(periods, n))
    mate = lax.ppermute(conductivity, "gx", [(i, i ^ 1) for i in range(n)])
    recv = lax.all_to_all(packed.reshape(n, 2 * half, -1), "gx", 0, 0)
    lists = recv.reshape(n, 2, half, -1).transpose(1, 0, 2, 3).reshape(2, n * half, -1)
    mate_list = lax.ppermute(lists[1], "gx", [(i, i ^ 1) for i in range(n)])
    forms, basis = krylov(n, lists, mate_list, mate, other, conductivity, omega)

    forms = lax.all_to_all(forms, "gx", 0, 0, tiled=True)

    return combine(forms, basis)


def solution(mesh):
    placed = (
        P(("period", "gx")),
        P(None, ("period", "gx")),
        P(None, ("period", "gx")),
        P(None, None, ("period", "gx")),
        P(None, "gx", None, None),
        P("period"),
    )
    return jax.shard_map(
        functools.partial(per_device, mesh.shape["period"], mesh.shape["gx"]),
        mesh=mesh,
        in_specs=placed,
        out_specs=(P("period", "gx", None, None), P("period", "gx", None, None)),
        check_vma=False,
    )
```

```python
import functools

import jax
import jax.numpy as jnp
from jax import lax
from jax.experimental import pallas as pl
from jax.experimental.pallas import tpu as pltpu
from jax.sharding import PartitionSpec as P

ITERS = 4
CENTRE = 4.0
BASIS = ITERS + 1
FORMS = 2 * ITERS
PAIRS = [(i // 2, (i + 1) // 2) for i in range(FORMS)]
HALO = ITERS - 1
STEP = 5
VMEM_LIMIT = 40 * 1024 * 1024
FULL_LIMIT = 62 * 1024 * 1024
CONTRACT_LANES = (((1,), (1,)), ((), ()))


def vmem():
    return pl.BlockSpec(memory_space=pltpu.VMEM)


def smem():
    return pl.BlockSpec(memory_space=pltpu.SMEM)


def hbm():
    return pl.BlockSpec(memory_space=pltpu.HBM)


def split_bf16(x):
    high = x.astype(jnp.bfloat16)
    return high, (x - high.astype(jnp.float32)).astype(jnp.bfloat16)


def bin_kernel(n, half, rows, cols, half_depth, *refs):
    sources, cond_hbm, out_ref, cut_ref, held, arrived = refs[:4], refs[4], refs[5], refs[6], refs[7:11], refs[11]
    copies = [pltpu.make_async_copy(sources[i], held[i], arrived.at[i]) for i in range(4)]
    first = (2 * half_depth - HALO) * (lax.axis_index("gx") % 2)
    copies.append(pltpu.make_async_copy(cond_hbm.at[:, pl.ds(first, HALO)], cut_ref, arrived.at[4]))
    for copy in copies:
        copy.start()
    for copy in copies[:4]:
        copy.wait()
    owner_ref, cell_ref, code_ref, value_ref = held
    sites = owner_ref.shape[1]
    owner = owner_ref[...]
    code = code_ref[...]
    dx = (code >= 9).astype(jnp.int32) + (code >= 18).astype(jnp.int32)
    rest = code - 9 * dx
    dy = (rest >= 3).astype(jnp.int32) + (rest >= 6).astype(jnp.int32)
    dz = rest - 3 * dy
    x = cell_ref[0:1] + dx
    y = cell_ref[1:2] + dy
    z = cell_ref[2:3] + dz
    upper = (x >= half_depth).astype(jnp.int32)
    folds = rows // 8
    row = (x - half_depth * upper) * rows + (y % folds) * 8 + y // folds
    lane = z + cols * upper
    channels, points = value_ref.shape[0], value_ref.shape[1]
    data = jnp.concatenate(
        [value_ref[...].reshape(channels * points, sites), row.astype(jnp.float32), lane.astype(jnp.float32)],
        axis=0,
    )

    named = lax.broadcasted_iota(jnp.int32, (n, sites), 0) == owner
    earlier = lax.broadcasted_iota(jnp.int32, (sites, sites), 0) < lax.broadcasted_iota(
        jnp.int32, (sites, sites), 1
    )
    named_f = named.astype(jnp.float32)
    counts = jnp.dot(
        named_f.astype(jnp.bfloat16),
        earlier.astype(jnp.float32).astype(jnp.bfloat16),
        preferred_element_type=jnp.float32,
    )
    rank = jnp.sum(counts * named_f, axis=0, keepdims=True).astype(jnp.int32)
    second = rank >= half
    place = jnp.where(second, rank - half, rank)

    slot = lax.broadcasted_iota(jnp.int32, (out_ref.shape[0], sites), 0)
    odd = owner % 2
    beside = owner + 2 * odd - 1
    hit = jnp.zeros(slot.shape, jnp.bool_)
    for first_row in (2 * owner + 1, 2 * beside):
        hit = hit | (slot == first_row * half + place)
    chosen = [jnp.where(hit & part, 1.0, 0.0).astype(jnp.bfloat16) for part in (jnp.logical_not(second), second)]
    stacked = []
    for piece in split_bf16(data):
        blank = jnp.zeros_like(piece)
        stacked += [jnp.concatenate([piece, blank], axis=1), jnp.concatenate([blank, piece], axis=1)]
    both = lax.dot_general(
        jnp.concatenate(chosen, axis=1),
        jnp.concatenate(stacked, axis=0),
        CONTRACT_LANES,
        preferred_element_type=jnp.float32,
    )
    width = out_ref.shape[1]
    total = both[:, :width] + both[:, width:]
    out_ref[...] = total
    copies[4].wait()


def scatter_slab(packed, left, right, depth, folds, cols):
    rows = 8 * folds
    half_depth = depth // 2
    channels, points = 6, 8
    row_count, lane_count, slots, width = half_depth * rows, 2 * cols, 2 * packed.shape[0], packed.shape[1] // 2
    row_iota = lax.broadcasted_iota(jnp.int32, (row_count, slots), 0)
    lane_iota = lax.broadcasted_iota(jnp.int32, (lane_count, slots), 0)
    turned = packed.T
    table = jnp.concatenate([turned[:width], turned[width:]], axis=1)
    table_high = table.astype(jnp.bfloat16).astype(jnp.float32)
    table_low = table - table_high
    cell_row = table[channels * points : (channels + 1) * points].astype(jnp.int32)
    cell_lane = table[(channels + 1) * points :].astype(jnp.int32)
    for k in range(points):
        span = slice(k * slots, (k + 1) * slots)
        right[:, span] = jnp.where(lane_iota == cell_lane[k : k + 1], 1.0, 0.0).astype(jnp.bfloat16)
        mask = row_iota == cell_row[k : k + 1]
        for c in range(channels):
            at = c * points + k
            for piece, part in enumerate((table_high, table_low)):
                first = (piece * channels + c) * row_count
                left[first : first + row_count, span] = jnp.where(mask, part[at : at + 1], 0.0).astype(jnp.bfloat16)
    both = lax.dot_general(left[...], right[...], CONTRACT_LANES, preferred_element_type=jnp.float32)
    return both[: channels * row_count] + both[channels * row_count :]


def store_slab(summed, basis, first_plane):
    depth, folds, cols = basis.shape[2] // 3, basis.shape[3], basis.shape[5]
    rows = 8 * folds
    half_depth = depth // 2
    row_count = half_depth * rows
    for c in range(6):
        for x in range(depth):
            first = c * row_count + (x % half_depth) * rows
            lanes = slice((x // half_depth) * cols, (x // half_depth + 1) * cols)
            basis[1, c, first_plane + x] = summed[first : first + rows, lanes].reshape(folds, 8, cols)


def scatter_kernel(list_ref, cond_hbm, basis, mine_ref, left, right, arrived):
    conductivity = pltpu.make_async_copy(cond_hbm, mine_ref, arrived)
    conductivity.start()
    depth, folds, cols = basis.shape[2] // 3, basis.shape[3], basis.shape[5]
    outer, own = (scatter_slab(list_ref[j], left.at[j], right.at[j], depth, folds, cols) for j in range(2))
    store_slab(own, basis, depth)
    store_slab(outer, basis, 2 * depth * (lax.axis_index("gx") % 2))
    conductivity.wait()


def field_kernel(
    n, list_ref, mate_ref, other_ref, mine_ref, omega_ref, _, forms_ref, basis, coupling, faces, left, right
):
    depth, folds, cols = basis.shape[2] // 3, basis.shape[3], basis.shape[5]
    channels = 6
    me = lax.axis_index("gx")
    keep_low = jnp.where(me > 0, 1.0, 0.0).astype(jnp.float32)
    keep_high = jnp.where(me < n - 1, 1.0, 0.0).astype(jnp.float32)

    scale = omega_ref[0]
    even = me % 2 == 0

    @pl.when(me >= 0)
    def _():
        third = scatter_slab(list_ref[...], left, right, depth, folds, cols)
        for q in range(3):
            for j in range(folds):
                fold = pl.ds(j, 8, stride=folds)
                for x in range(depth):
                    coupling[q, HALO + x, j] = mine_ref[q, x, fold] * scale
                for i in range(HALO):
                    below, above = depth - HALO + i, i
                    coupling[q, i, j] = jnp.where(even, other_ref[q, i, fold], mate_ref[q, below, fold]) * scale
                    coupling[q, HALO + depth + i, j] = (
                        jnp.where(even, mate_ref[q, above, fold], other_ref[q, i, fold]) * scale
                    )
        store_slab(third, basis, 2 * depth * (1 - me % 2))

    s_iota = lax.broadcasted_iota(jnp.int32, (8, cols), 0)
    z_iota = lax.broadcasted_iota(jnp.int32, (folds, 8, cols), 2)
    s_first, s_last = s_iota == 0, s_iota == 7
    z_first, z_last = z_iota == 0, z_iota == cols - 1

    def ahead_y(f):
        wrapped = jnp.where(s_last, 0.0, pltpu.roll(f[0], 7, 0))
        return jnp.concatenate([f[1:], wrapped[None]], axis=0) - f

    def ahead_z(f):
        return jnp.where(z_last, 0.0, pltpu.roll(f, cols - 1, 2)) - f

    def behind_y(f):
        wrapped = jnp.where(s_first, 0.0, pltpu.roll(f[folds - 1], 1, 0))
        return f - jnp.concatenate([wrapped[None], f[:-1]], axis=0)

    def behind_z(f):
        return f - jnp.where(z_first, 0.0, pltpu.roll(f, 1, 2))

    def edges(k, p):
        return [basis[k, c, p] for c in range(channels)]

    def faces_of(here, there):
        result = []
        for part in range(2):
            ex, ey, ez = here[3 * part : 3 * part + 3]
            ey_next, ez_next = there[3 * part + 1], there[3 * part + 2]
            result.append(ahead_y(ez) - ahead_z(ey))
            result.append(ahead_z(ex) - (ez_next - ez))
            result.append((ey_next - ey) - ahead_y(ex))
        return result

    def keep_faces(p, values):
        for c in range(channels):
            faces[c, p] = values[c]

    def plane(here, coupled, face, face_before):
        new = []
        for part in range(2):
            hx, hy, hz = face[3 * part : 3 * part + 3]
            hy_before, hz_before = face_before[2 * part], face_before[2 * part + 1]
            curls = (
                behind_y(hz) - behind_z(hy),
                behind_z(hx) - (hz - hz_before),
                (hy - hy_before) - behind_y(hx),
            )
            for q in range(3):
                other = coupled[q] * here[3 * (1 - part) + q]
                value = curls[q] - CENTRE * here[3 * part + q]
                new.append(value + other if part == 0 else value - other)
        return new

    def apply(k):
        end = 3 * depth - k

        def step(p, count):
            after = range(p + count, min(p + 2 * count, end))
            fields = [edges(k, p + d) for d in range(count)]
            coupled = [[coupling[q, p + d - (depth - HALO)] for q in range(3)] for d in range(count)]
            face = [[faces[c, p + d] for c in range(channels)] for d in range(-1, count)]
            following = [edges(k, x) for x in range(p + count, after.stop + 1)] if after else []
            next_faces = [faces_of(following[d], following[d + 1]) for d in range(len(after))]
            new = []
            for d in range(count):
                before = [face[d][c] for c in (1, 2, 4, 5)]
                if p + d == depth:
                    before = [f * keep_low for f in before]
                new.append(plane(fields[d], coupled[d], face[d + 1], before))
                if p + d == 2 * depth:
                    new[d] = [f * keep_high for f in new[d]]
            for d in range(count):
                for c in range(channels):
                    basis[k + 1, c, p + d] = new[d][c]
            for x, values in zip(after, next_faces):
                keep_faces(x, values)

        first = [edges(k, x) for x in range(k - 1, min(k + STEP, end) + 1)]
        for d in range(len(first) - 1):
            keep_faces(k - 1 + d, faces_of(first[d], first[d + 1]))
        for p in range(k, end, STEP):
            step(p, min(STEP, end - p))

    for k in range(1, BASIS):
        pl.when(me >= 0)(functools.partial(apply, k))

    def some_forms(p, sums):
        sums = list(sums)
        for q, fold in [(q, fold) for q in range(3) for fold in range(folds)]:
            re = [basis[k + 1, q, p, fold] for k in range(BASIS)]
            im = [basis[k + 1, 3 + q, p, fold] for k in range(BASIS)]
            for f, (i, j) in enumerate(PAIRS):
                real = re[i] * re[j] - im[i] * im[j]
                imag = re[i] * im[j] + im[i] * re[j] if i != j else re[i] * im[i]
                sums[2 * f] = sums[2 * f] + real
                sums[2 * f + 1] = sums[2 * f + 1] + imag
        return tuple(sums)

    zero = jnp.zeros((8, cols), jnp.float32)
    sums = lax.fori_loop(depth, 2 * depth, some_forms, (zero,) * (2 * FORMS), unroll=2)
    sums = list(sums)
    for f, (i, j) in enumerate(PAIRS):
        if i == j:
            sums[2 * f + 1] = 2.0 * sums[2 * f + 1]
    folded = jnp.concatenate([jnp.sum(total, axis=0, keepdims=True) for total in sums], axis=0)
    totals = jnp.sum(folded, axis=1, keepdims=True)
    diagonal = lax.broadcasted_iota(jnp.int32, folded.shape, 0) == lax.broadcasted_iota(jnp.int32, folded.shape, 1)
    line = jnp.sum(jnp.where(diagonal, totals, 0.0), axis=0, keepdims=True)
    forms_ref[...] = jnp.broadcast_to(line, forms_ref.shape)


def c_add(a, b):
    return a[0] + b[0], a[1] + b[1]


def c_sub(a, b):
    return a[0] - b[0], a[1] - b[1]


def c_mul(a, b):
    return a[0] * b[0] - a[1] * b[1], a[0] * b[1] + a[1] * b[0]


def c_scale(s, a):
    return s * a[0], s * a[1]


def c_div(a, b):
    inverse = 1.0 / (b[0] * b[0] + b[1] * b[1])
    return (a[0] * b[0] + a[1] * b[1]) * inverse, (a[1] * b[0] - a[0] * b[1]) * inverse


def step_scalars(moments):
    resid = list(moments)
    direc = list(moments)
    none = (jnp.zeros_like(moments[0][0]),) * 2
    one = (jnp.ones_like(moments[0][0]), jnp.zeros_like(moments[0][0]))
    resid_at = [one] + [none] * ITERS
    direc_at = [one] + [none] * ITERS
    field_at = [none] * BASIS
    rho = moments[0]
    for n in range(ITERS):
        applied = [c_add(c_scale(CENTRE, direc[l]), direc[l + 1]) for l in range(len(direc) - 1)]
        step = c_div(rho, c_mul(direc_at[n], applied[n]))
        applied_at = [c_scale(CENTRE, direc_at[j]) if j <= n else none for j in range(BASIS)]
        for j in range(n + 1):
            applied_at[j + 1] = c_add(applied_at[j + 1], direc_at[j])
        for j in range(n + 1):
            field_at[j] = c_add(field_at[j], c_mul(step, direc_at[j]))
        for j in range(n + 2):
            resid_at[j] = c_sub(resid_at[j], c_mul(step, applied_at[j]))
        if n + 1 < ITERS:
            resid = [c_sub(resid[l], c_mul(step, applied[l])) for l in range(len(applied))]
            rho_next = c_mul(resid_at[n + 1], resid[n + 1])
            ratio = c_div(rho_next, rho)
            direc = [c_add(resid[l], c_mul(ratio, direc[l])) for l in range(len(resid))]
            direc_at = [
                c_add(resid_at[j], c_mul(ratio, direc_at[j])) if j <= n else resid_at[j] for j in range(BASIS)
            ]
            rho = rho_next
    return field_at, resid_at


def combine_kernel(forms_ref, basis, field_hbm, resid_hbm, field_ref, resid_ref, sent):
    depth, folds, cols = basis.shape[2] // 3, basis.shape[3], basis.shape[5]
    totals = jnp.broadcast_to(jnp.sum(forms_ref[...], axis=0, keepdims=True), (8, cols))
    lane = lax.broadcasted_iota(jnp.int32, (8, cols), 1)
    sums = [
        jnp.broadcast_to(jnp.sum(jnp.where(lane == i, totals, 0.0), axis=1, keepdims=True), (8, cols))
        for i in range(2 * FORMS)
    ]
    forms = [(sums[2 * f], sums[2 * f + 1]) for f in range(FORMS)]
    field_at, resid_at = step_scalars(forms)

    def copies(p):
        return [
            pltpu.make_async_copy(ref.at[:, p], hbm_ref.at[:, p], sent.at[i, p])
            for i, (ref, hbm_ref) in enumerate(((field_ref, field_hbm), (resid_ref, resid_hbm)))
        ]

    def plane(p, _):
        for q in range(3):
            for j in range(folds):
                re = [basis[k + 1, q, depth + p, j] for k in range(BASIS)]
                im = [basis[k + 1, 3 + q, depth + p, j] for k in range(BASIS)]
                rows = pl.ds(j, 8, stride=folds)
                for out_ref, factors in ((field_ref, field_at[:ITERS]), (resid_ref, resid_at)):
                    out_ref[q, p, rows] = sum(f[0] * re[k] - f[1] * im[k] for k, f in enumerate(factors))
                    out_ref[3 + q, p, rows] = sum(f[0] * im[k] + f[1] * re[k] for k, f in enumerate(factors))
        for copy in copies(p):
            copy.start()
        return 0

    lax.fori_loop(0, depth, plane, 0)
    for p in range(depth):
        for copy in copies(p):
            copy.wait()


def params(limit=VMEM_LIMIT):
    return pltpu.CompilerParams(vmem_limit_bytes=limit)


def krylov(n, lists, mate_list, mate, other, conductivity, omega):
    depth, folds, cols = conductivity.shape[1], conductivity.shape[2] // 8, conductivity.shape[3]
    slots = 2 * lists.shape[1]
    left_shape, right_shape = (2 * 6 * depth // 2 * 8 * folds, 8 * slots), (2 * cols, 8 * slots)
    bases = jax.ShapeDtypeStruct((BASIS + 1, 6, 3 * depth, folds, 8, cols), jnp.float32)
    basis, mine = pl.pallas_call(
        scatter_kernel,
        out_shape=(bases, jax.ShapeDtypeStruct(conductivity.shape, jnp.float32)),
        in_specs=[vmem(), hbm()],
        out_specs=(vmem(), vmem()),
        scratch_shapes=[
            pltpu.VMEM((2, *left_shape), jnp.bfloat16),
            pltpu.VMEM((2, *right_shape), jnp.bfloat16),
            pltpu.SemaphoreType.DMA,
        ],
        cost_estimate=pl.CostEstimate(
            flops=4 * left_shape[0] * right_shape[0] * 8 * slots, bytes_accessed=4 * 1024 * 1024, transcendentals=0
        ),
        compiler_params=params(),
        name="scatter_source",
    )(lists, pltpu.with_memory_space_constraint(conductivity, pltpu.HBM))
    return pl.pallas_call(
        functools.partial(field_kernel, n),
        out_shape=(jax.ShapeDtypeStruct((n, cols), jnp.float32), bases),
        in_specs=[vmem()] * 4 + [smem(), vmem()],
        out_specs=(vmem(), vmem()),
        scratch_shapes=[
            pltpu.VMEM((3, 2 * HALO + depth, folds, 8, cols), jnp.float32),
            pltpu.VMEM((6, 3 * depth, folds, 8, cols), jnp.float32),
            pltpu.VMEM(left_shape, jnp.bfloat16),
            pltpu.VMEM(right_shape, jnp.bfloat16),
        ],
        input_output_aliases={5: 1},
        compiler_params=params(),
        name="krylov_basis",
    )(mate_list, mate, other, mine, omega, basis)


def combine(forms, basis):
    depth, folds, cols = basis.shape[2] // 3, basis.shape[3], basis.shape[5]
    rows = 8 * folds
    out = jax.ShapeDtypeStruct((6, depth, rows, cols), jnp.float32)
    return pl.pallas_call(
        combine_kernel,
        out_shape=(out, out),
        in_specs=[vmem()] * 2,
        out_specs=(hbm(), hbm()),
        scratch_shapes=[pltpu.VMEM(out.shape, out.dtype)] * 2 + [pltpu.SemaphoreType.DMA((2, depth))],
        compiler_params=params(),
        name="combine_basis",
    )(forms, basis)


def bin_sites(n, listed, conductivity):
    depth, rows, cols = conductivity.shape[1:]
    half = listed[0].shape[1] // n
    return pl.pallas_call(
        functools.partial(bin_kernel, n, half, rows, cols, depth // 2),
        out_shape=(
            jax.ShapeDtypeStruct((n * 2 * half, 2 * 8 * 8), jnp.float32),
            jax.ShapeDtypeStruct((3, HALO, rows, cols), jnp.float32),
        ),
        in_specs=[hbm()] * 5,
        out_specs=(vmem(), vmem()),
        scratch_shapes=[pltpu.VMEM(x.shape, x.dtype) for x in listed] + [pltpu.SemaphoreType.DMA((5,))],
        compiler_params=params(),
        name="bin_sites",
    )(*(pltpu.with_memory_space_constraint(x, pltpu.HBM) for x in (*listed, conductivity)))


def outer_pairs(periods, n):
    pairs = []
    for p in range(periods):
        pairs += [(p * n + i, p * n + ((i + 1) ^ 1) - 1) for i in range(1, n - 1)]
        if periods % 2 == 0:
            pairs += [(p * n + i, (p ^ 1) * n + i) for i in (0, n - 1)]
    return pairs


def per_device(periods, n, site_owner, site_cell, stencil_code, site_residual, conductivity, omega):
    depth, rows, cols = conductivity.shape[1:]
    sites = site_owner.shape[0]
    cap = 2 * sites // n
    half = cap // 2
    listed = (site_owner.reshape(1, sites), site_cell, stencil_code, site_residual)
    packed, cut = bin_sites(n, listed, conductivity)
    other = lax.ppermute(cut, ("period", "gx"), outer_pairs(periods, n))
    mate = lax.ppermute(conductivity, "gx", [(i, i ^ 1) for i in range(n)])
    recv = lax.all_to_all(packed.reshape(n, 2 * half, -1), "gx", 0, 0)
    lists = recv.reshape(n, 2, half, -1).transpose(1, 0, 2, 3).reshape(2, n * half, -1)
    mate_list = lax.ppermute(lists[1], "gx", [(i, i ^ 1) for i in range(n)])
    forms, basis = krylov(n, lists, mate_list, mate, other, conductivity, omega)

    forms = lax.all_to_all(forms, "gx", 0, 0, tiled=True)

    return combine(forms, basis)


def solution(mesh):
    placed = (
        P(("period", "gx")),
        P(None, ("period", "gx")),
        P(None, ("period", "gx")),
        P(None, None, ("period", "gx")),
        P(None, "gx", None, None),
        P("period"),
    )
    return jax.shard_map(
        functools.partial(per_device, mesh.shape["period"], mesh.shape["gx"]),
        mesh=mesh,
        in_specs=placed,
        out_specs=(P("period", "gx", None, None), P("period", "gx", None, None)),
        check_vma=False,
    )
```

```python
import functools

import jax
import jax.numpy as jnp
from jax import lax
from jax.experimental import pallas as pl
from jax.experimental.pallas import tpu as pltpu
from jax.sharding import PartitionSpec as P

ITERS = 4
CENTRE = 4.0
BASIS = ITERS + 1
FORMS = 2 * ITERS
PAIRS = [(i // 2, (i + 1) // 2) for i in range(FORMS)]
HALO = ITERS - 1
STEP = 4
VMEM_LIMIT = 40 * 1024 * 1024
FULL_LIMIT = 62 * 1024 * 1024
CONTRACT_LANES = (((1,), (1,)), ((), ()))


def vmem():
    return pl.BlockSpec(memory_space=pltpu.VMEM)


def smem():
    return pl.BlockSpec(memory_space=pltpu.SMEM)


def hbm():
    return pl.BlockSpec(memory_space=pltpu.HBM)


def split_bf16(x):
    high = x.astype(jnp.bfloat16)
    return high, (x - high.astype(jnp.float32)).astype(jnp.bfloat16)


def bin_kernel(n, half, rows, cols, half_depth, *refs):
    sources, cond_hbm, out_ref, cut_ref, held, arrived = refs[:4], refs[4], refs[5], refs[6], refs[7:11], refs[11]
    copies = [pltpu.make_async_copy(sources[i], held[i], arrived.at[i]) for i in range(4)]
    first = (2 * half_depth - HALO) * (lax.axis_index("gx") % 2)
    copies.append(pltpu.make_async_copy(cond_hbm.at[:, pl.ds(first, HALO)], cut_ref, arrived.at[4]))
    for copy in copies:
        copy.start()
    for copy in copies[:4]:
        copy.wait()
    owner_ref, cell_ref, code_ref, value_ref = held
    sites = owner_ref.shape[1]
    owner = owner_ref[...]
    code = code_ref[...]
    dx = (code >= 9).astype(jnp.int32) + (code >= 18).astype(jnp.int32)
    rest = code - 9 * dx
    dy = (rest >= 3).astype(jnp.int32) + (rest >= 6).astype(jnp.int32)
    dz = rest - 3 * dy
    x = cell_ref[0:1] + dx
    y = cell_ref[1:2] + dy
    z = cell_ref[2:3] + dz
    upper = (x >= half_depth).astype(jnp.int32)
    folds = rows // 8
    row = (x - half_depth * upper) * rows + (y % folds) * 8 + y // folds
    lane = z + cols * upper
    channels, points = value_ref.shape[0], value_ref.shape[1]
    data = jnp.concatenate(
        [value_ref[...].reshape(channels * points, sites), row.astype(jnp.float32), lane.astype(jnp.float32)],
        axis=0,
    )

    named = lax.broadcasted_iota(jnp.int32, (n, sites), 0) == owner
    earlier = lax.broadcasted_iota(jnp.int32, (sites, sites), 0) < lax.broadcasted_iota(
        jnp.int32, (sites, sites), 1
    )
    named_f = named.astype(jnp.float32)
    counts = jnp.dot(
        named_f.astype(jnp.bfloat16),
        earlier.astype(jnp.float32).astype(jnp.bfloat16),
        preferred_element_type=jnp.float32,
    )
    rank = jnp.sum(counts * named_f, axis=0, keepdims=True).astype(jnp.int32)
    second = rank >= half
    place = jnp.where(second, rank - half, rank)

    slot = lax.broadcasted_iota(jnp.int32, (out_ref.shape[0], sites), 0)
    odd = owner % 2
    beside = owner + 2 * odd - 1
    hit = jnp.zeros(slot.shape, jnp.bool_)
    for first_row in (2 * owner + 1, 2 * beside):
        hit = hit | (slot == first_row * half + place)
    chosen = [jnp.where(hit & part, 1.0, 0.0).astype(jnp.bfloat16) for part in (jnp.logical_not(second), second)]
    stacked = []
    for piece in split_bf16(data):
        blank = jnp.zeros_like(piece)
        stacked += [jnp.concatenate([piece, blank], axis=1), jnp.concatenate([blank, piece], axis=1)]
    both = lax.dot_general(
        jnp.concatenate(chosen, axis=1),
        jnp.concatenate(stacked, axis=0),
        CONTRACT_LANES,
        preferred_element_type=jnp.float32,
    )
    width = out_ref.shape[1]
    total = both[:, :width] + both[:, width:]
    out_ref[...] = total
    copies[4].wait()


def scatter_slab(packed, left, right, depth, folds, cols):
    rows = 8 * folds
    half_depth = depth // 2
    channels, points = 6, 8
    row_count, lane_count, slots, width = half_depth * rows, 2 * cols, 2 * packed.shape[0], packed.shape[1] // 2
    row_iota = lax.broadcasted_iota(jnp.int32, (row_count, slots), 0)
    lane_iota = lax.broadcasted_iota(jnp.int32, (lane_count, slots), 0)
    turned = packed.T
    table = jnp.concatenate([turned[:width], turned[width:]], axis=1)
    table_high = table.astype(jnp.bfloat16).astype(jnp.float32)
    table_low = table - table_high
    cell_row = table[channels * points : (channels + 1) * points].astype(jnp.int32)
    cell_lane = table[(channels + 1) * points :].astype(jnp.int32)
    for k in range(points):
        span = slice(k * slots, (k + 1) * slots)
        right[:, span] = jnp.where(lane_iota == cell_lane[k : k + 1], 1.0, 0.0).astype(jnp.bfloat16)
        mask = row_iota == cell_row[k : k + 1]
        for c in range(channels):
            at = c * points + k
            for piece, part in enumerate((table_high, table_low)):
                first = (piece * channels + c) * row_count
                left[first : first + row_count, span] = jnp.where(mask, part[at : at + 1], 0.0).astype(jnp.bfloat16)
    both = lax.dot_general(left[...], right[...], CONTRACT_LANES, preferred_element_type=jnp.float32)
    return both[: channels * row_count] + both[channels * row_count :]


def store_slab(summed, basis, first_plane):
    depth, folds, cols = basis.shape[2] // 3, basis.shape[3], basis.shape[5]
    rows = 8 * folds
    half_depth = depth // 2
    row_count = half_depth * rows
    for c in range(6):
        for x in range(depth):
            first = c * row_count + (x % half_depth) * rows
            lanes = slice((x // half_depth) * cols, (x // half_depth + 1) * cols)
            basis[1, c, first_plane + x] = summed[first : first + rows, lanes].reshape(folds, 8, cols)


def scatter_kernel(list_ref, cond_hbm, basis, mine_ref, left, right, arrived):
    conductivity = pltpu.make_async_copy(cond_hbm, mine_ref, arrived)
    conductivity.start()
    depth, folds, cols = basis.shape[2] // 3, basis.shape[3], basis.shape[5]
    outer, own = (scatter_slab(list_ref[j], left.at[j], right.at[j], depth, folds, cols) for j in range(2))
    store_slab(own, basis, depth)
    store_slab(outer, basis, 2 * depth * (lax.axis_index("gx") % 2))
    conductivity.wait()


def field_kernel(
    n, list_ref, mate_ref, other_ref, mine_ref, omega_ref, _, forms_ref, basis, coupling, faces, left, right
):
    depth, folds, cols = basis.shape[2] // 3, basis.shape[3], basis.shape[5]
    channels = 6
    me = lax.axis_index("gx")
    keep_low = jnp.where(me > 0, 1.0, 0.0).astype(jnp.float32)
    keep_high = jnp.where(me < n - 1, 1.0, 0.0).astype(jnp.float32)

    scale = omega_ref[0]
    even = me % 2 == 0

    @pl.when(me >= 0)
    def _():
        third = scatter_slab(list_ref[...], left, right, depth, folds, cols)
        for q in range(3):
            for j in range(folds):
                fold = pl.ds(j, 8, stride=folds)
                for x in range(depth):
                    coupling[q, HALO + x, j] = mine_ref[q, x, fold] * scale
                for i in range(HALO):
                    below, above = depth - HALO + i, i
                    coupling[q, i, j] = jnp.where(even, other_ref[q, i, fold], mate_ref[q, below, fold]) * scale
                    coupling[q, HALO + depth + i, j] = (
                        jnp.where(even, mate_ref[q, above, fold], other_ref[q, i, fold]) * scale
                    )
        store_slab(third, basis, 2 * depth * (1 - me % 2))

    s_iota = lax.broadcasted_iota(jnp.int32, (8, cols), 0)
    z_iota = lax.broadcasted_iota(jnp.int32, (folds, 8, cols), 2)
    s_first, s_last = s_iota == 0, s_iota == 7
    z_first, z_last = z_iota == 0, z_iota == cols - 1

    def ahead_y(f):
        wrapped = jnp.where(s_last, 0.0, pltpu.roll(f[0], 7, 0))
        return jnp.concatenate([f[1:], wrapped[None]], axis=0) - f

    def ahead_z(f):
        return jnp.where(z_last, 0.0, pltpu.roll(f, cols - 1, 2)) - f

    def behind_y(f):
        wrapped = jnp.where(s_first, 0.0, pltpu.roll(f[folds - 1], 1, 0))
        return f - jnp.concatenate([wrapped[None], f[:-1]], axis=0)

    def behind_z(f):
        return f - jnp.where(z_first, 0.0, pltpu.roll(f, 1, 2))

    def edges(k, p):
        return [basis[k, c, p] for c in range(channels)]

    def faces_of(here, there):
        result = []
        for part in range(2):
            ex, ey, ez = here[3 * part : 3 * part + 3]
            ey_next, ez_next = there[3 * part + 1], there[3 * part + 2]
            result.append(ahead_y(ez) - ahead_z(ey))
            result.append(ahead_z(ex) - (ez_next - ez))
            result.append((ey_next - ey) - ahead_y(ex))
        return result

    def keep_faces(p, values):
        for c in range(channels):
            faces[c, p] = values[c]

    def plane(here, coupled, face, face_before):
        new = []
        for part in range(2):
            hx, hy, hz = face[3 * part : 3 * part + 3]
            hy_before, hz_before = face_before[2 * part], face_before[2 * part + 1]
            curls = (
                behind_y(hz) - behind_z(hy),
                behind_z(hx) - (hz - hz_before),
                (hy - hy_before) - behind_y(hx),
            )
            for q in range(3):
                other = coupled[q] * here[3 * (1 - part) + q]
                value = curls[q] - CENTRE * here[3 * part + q]
                new.append(value + other if part == 0 else value - other)
        return new

    def apply(k):
        end = 3 * depth - k

        def step(p, count):
            after = range(p + count, min(p + 2 * count, end))
            fields = [edges(k, p + d) for d in range(count)]
            coupled = [[coupling[q, p + d - (depth - HALO)] for q in range(3)] for d in range(count)]
            face = [[faces[c, p + d] for c in range(channels)] for d in range(-1, count)]
            following = [edges(k, x) for x in range(p + count, after.stop + 1)] if after else []
            next_faces = [faces_of(following[d], following[d + 1]) for d in range(len(after))]
            new = []
            for d in range(count):
                before = [face[d][c] for c in (1, 2, 4, 5)]
                if p + d == depth:
                    before = [f * keep_low for f in before]
                new.append(plane(fields[d], coupled[d], face[d + 1], before))
                if p + d == 2 * depth:
                    new[d] = [f * keep_high for f in new[d]]
            for d in range(count):
                for c in range(channels):
                    basis[k + 1, c, p + d] = new[d][c]
            for x, values in zip(after, next_faces):
                keep_faces(x, values)

        first = [edges(k, x) for x in range(k - 1, min(k + STEP, end) + 1)]
        for d in range(len(first) - 1):
            keep_faces(k - 1 + d, faces_of(first[d], first[d + 1]))
        for p in range(k, end, STEP):
            step(p, min(STEP, end - p))

    for k in range(1, BASIS):
        pl.when(me >= 0)(functools.partial(apply, k))

    def some_forms(p, sums):
        sums = list(sums)
        for q, fold in [(q, fold) for q in range(3) for fold in range(folds)]:
            re = [basis[k + 1, q, p, fold] for k in range(BASIS)]
            im = [basis[k + 1, 3 + q, p, fold] for k in range(BASIS)]
            for f, (i, j) in enumerate(PAIRS):
                real = re[i] * re[j] - im[i] * im[j]
                imag = re[i] * im[j] + im[i] * re[j] if i != j else re[i] * im[i]
                sums[2 * f] = sums[2 * f] + real
                sums[2 * f + 1] = sums[2 * f + 1] + imag
        return tuple(sums)

    zero = jnp.zeros((8, cols), jnp.float32)
    sums = lax.fori_loop(depth, 2 * depth, some_forms, (zero,) * (2 * FORMS), unroll=2)
    sums = list(sums)
    for f, (i, j) in enumerate(PAIRS):
        if i == j:
            sums[2 * f + 1] = 2.0 * sums[2 * f + 1]
    folded = jnp.concatenate([jnp.sum(total, axis=0, keepdims=True) for total in sums], axis=0)
    totals = jnp.sum(folded, axis=1, keepdims=True)
    diagonal = lax.broadcasted_iota(jnp.int32, folded.shape, 0) == lax.broadcasted_iota(jnp.int32, folded.shape, 1)
    line = jnp.sum(jnp.where(diagonal, totals, 0.0), axis=0, keepdims=True)
    forms_ref[...] = jnp.broadcast_to(line, forms_ref.shape)


def c_add(a, b):
    return a[0] + b[0], a[1] + b[1]


def c_sub(a, b):
    return a[0] - b[0], a[1] - b[1]


def c_mul(a, b):
    return a[0] * b[0] - a[1] * b[1], a[0] * b[1] + a[1] * b[0]


def c_scale(s, a):
    return s * a[0], s * a[1]


def c_div(a, b):
    inverse = 1.0 / (b[0] * b[0] + b[1] * b[1])
    return (a[0] * b[0] + a[1] * b[1]) * inverse, (a[1] * b[0] - a[0] * b[1]) * inverse


def step_scalars(moments):
    resid = list(moments)
    direc = list(moments)
    none = (jnp.zeros_like(moments[0][0]),) * 2
    one = (jnp.ones_like(moments[0][0]), jnp.zeros_like(moments[0][0]))
    resid_at = [one] + [none] * ITERS
    direc_at = [one] + [none] * ITERS
    field_at = [none] * BASIS
    rho = moments[0]
    for n in range(ITERS):
        applied = [c_add(c_scale(CENTRE, direc[l]), direc[l + 1]) for l in range(len(direc) - 1)]
        step = c_div(rho, c_mul(direc_at[n], applied[n]))
        applied_at = [c_scale(CENTRE, direc_at[j]) if j <= n else none for j in range(BASIS)]
        for j in range(n + 1):
            applied_at[j + 1] = c_add(applied_at[j + 1], direc_at[j])
        for j in range(n + 1):
            field_at[j] = c_add(field_at[j], c_mul(step, direc_at[j]))
        for j in range(n + 2):
            resid_at[j] = c_sub(resid_at[j], c_mul(step, applied_at[j]))
        if n + 1 < ITERS:
            resid = [c_sub(resid[l], c_mul(step, applied[l])) for l in range(len(applied))]
            rho_next = c_mul(resid_at[n + 1], resid[n + 1])
            ratio = c_div(rho_next, rho)
            direc = [c_add(resid[l], c_mul(ratio, direc[l])) for l in range(len(resid))]
            direc_at = [
                c_add(resid_at[j], c_mul(ratio, direc_at[j])) if j <= n else resid_at[j] for j in range(BASIS)
            ]
            rho = rho_next
    return field_at, resid_at


def combine_kernel(forms_ref, basis, field_hbm, resid_hbm, field_ref, resid_ref, sent):
    depth, folds, cols = basis.shape[2] // 3, basis.shape[3], basis.shape[5]
    totals = jnp.broadcast_to(jnp.sum(forms_ref[...], axis=0, keepdims=True), (8, cols))
    lane = lax.broadcasted_iota(jnp.int32, (8, cols), 1)
    sums = [
        jnp.broadcast_to(jnp.sum(jnp.where(lane == i, totals, 0.0), axis=1, keepdims=True), (8, cols))
        for i in range(2 * FORMS)
    ]
    forms = [(sums[2 * f], sums[2 * f + 1]) for f in range(FORMS)]
    field_at, resid_at = step_scalars(forms)

    def copies(p):
        return [
            pltpu.make_async_copy(ref.at[:, p], hbm_ref.at[:, p], sent.at[i, p])
            for i, (ref, hbm_ref) in enumerate(((field_ref, field_hbm), (resid_ref, resid_hbm)))
        ]

    def plane(p, _):
        for q in range(3):
            for j in range(folds):
                re = [basis[k + 1, q, depth + p, j] for k in range(BASIS)]
                im = [basis[k + 1, 3 + q, depth + p, j] for k in range(BASIS)]
                rows = pl.ds(j, 8, stride=folds)
                for out_ref, factors in ((field_ref, field_at[:ITERS]), (resid_ref, resid_at)):
                    out_ref[q, p, rows] = sum(f[0] * re[k] - f[1] * im[k] for k, f in enumerate(factors))
                    out_ref[3 + q, p, rows] = sum(f[0] * im[k] + f[1] * re[k] for k, f in enumerate(factors))
        for copy in copies(p):
            copy.start()
        return 0

    lax.fori_loop(0, depth, plane, 0, unroll=True)
    for p in range(depth):
        for copy in copies(p):
            copy.wait()


def params(limit=VMEM_LIMIT):
    return pltpu.CompilerParams(vmem_limit_bytes=limit)


def krylov(n, lists, mate_list, mate, other, conductivity, omega):
    depth, folds, cols = conductivity.shape[1], conductivity.shape[2] // 8, conductivity.shape[3]
    slots = 2 * lists.shape[1]
    left_shape, right_shape = (2 * 6 * depth // 2 * 8 * folds, 8 * slots), (2 * cols, 8 * slots)
    bases = jax.ShapeDtypeStruct((BASIS + 1, 6, 3 * depth, folds, 8, cols), jnp.float32)
    basis, mine = pl.pallas_call(
        scatter_kernel,
        out_shape=(bases, jax.ShapeDtypeStruct(conductivity.shape, jnp.float32)),
        in_specs=[vmem(), hbm()],
        out_specs=(vmem(), vmem()),
        scratch_shapes=[
            pltpu.VMEM((2, *left_shape), jnp.bfloat16),
            pltpu.VMEM((2, *right_shape), jnp.bfloat16),
            pltpu.SemaphoreType.DMA,
        ],
        cost_estimate=pl.CostEstimate(
            flops=4 * left_shape[0] * right_shape[0] * 8 * slots, bytes_accessed=4 * 1024 * 1024, transcendentals=0
        ),
        compiler_params=params(),
        name="scatter_source",
    )(lists, pltpu.with_memory_space_constraint(conductivity, pltpu.HBM))
    return pl.pallas_call(
        functools.partial(field_kernel, n),
        out_shape=(jax.ShapeDtypeStruct((n, cols), jnp.float32), bases),
        in_specs=[vmem()] * 4 + [smem(), vmem()],
        out_specs=(vmem(), vmem()),
        scratch_shapes=[
            pltpu.VMEM((3, 2 * HALO + depth, folds, 8, cols), jnp.float32),
            pltpu.VMEM((6, 3 * depth, folds, 8, cols), jnp.float32),
            pltpu.VMEM(left_shape, jnp.bfloat16),
            pltpu.VMEM(right_shape, jnp.bfloat16),
        ],
        input_output_aliases={5: 1},
        compiler_params=params(),
        name="krylov_basis",
    )(mate_list, mate, other, mine, omega, basis)


def combine(forms, basis):
    depth, folds, cols = basis.shape[2] // 3, basis.shape[3], basis.shape[5]
    rows = 8 * folds
    out = jax.ShapeDtypeStruct((6, depth, rows, cols), jnp.float32)
    return pl.pallas_call(
        combine_kernel,
        out_shape=(out, out),
        in_specs=[vmem()] * 2,
        out_specs=(hbm(), hbm()),
        scratch_shapes=[pltpu.VMEM(out.shape, out.dtype)] * 2 + [pltpu.SemaphoreType.DMA((2, depth))],
        compiler_params=params(),
        name="combine_basis",
    )(forms, basis)


def bin_sites(n, listed, conductivity):
    depth, rows, cols = conductivity.shape[1:]
    half = listed[0].shape[1] // n
    return pl.pallas_call(
        functools.partial(bin_kernel, n, half, rows, cols, depth // 2),
        out_shape=(
            jax.ShapeDtypeStruct((n * 2 * half, 2 * 8 * 8), jnp.float32),
            jax.ShapeDtypeStruct((3, HALO, rows, cols), jnp.float32),
        ),
        in_specs=[hbm()] * 5,
        out_specs=(vmem(), vmem()),
        scratch_shapes=[pltpu.VMEM(x.shape, x.dtype) for x in listed] + [pltpu.SemaphoreType.DMA((5,))],
        compiler_params=params(),
        name="bin_sites",
    )(*(pltpu.with_memory_space_constraint(x, pltpu.HBM) for x in (*listed, conductivity)))


def outer_pairs(periods, n):
    pairs = []
    for p in range(periods):
        pairs += [(p * n + i, p * n + ((i + 1) ^ 1) - 1) for i in range(1, n - 1)]
        if periods % 2 == 0:
            pairs += [(p * n + i, (p ^ 1) * n + i) for i in (0, n - 1)]
    return pairs


def per_device(periods, n, site_owner, site_cell, stencil_code, site_residual, conductivity, omega):
    depth, rows, cols = conductivity.shape[1:]
    sites = site_owner.shape[0]
    cap = 2 * sites // n
    half = cap // 2
    listed = (site_owner.reshape(1, sites), site_cell, stencil_code, site_residual)
    packed, cut = bin_sites(n, listed, conductivity)
    other = lax.ppermute(cut, ("period", "gx"), outer_pairs(periods, n))
    mate = lax.ppermute(conductivity, "gx", [(i, i ^ 1) for i in range(n)])
    recv = lax.all_to_all(packed.reshape(n, 2 * half, -1), "gx", 0, 0)
    lists = recv.reshape(n, 2, half, -1).transpose(1, 0, 2, 3).reshape(2, n * half, -1)
    mate_list = lax.ppermute(lists[1], "gx", [(i, i ^ 1) for i in range(n)])
    forms, basis = krylov(n, lists, mate_list, mate, other, conductivity, omega)

    forms = lax.all_to_all(forms, "gx", 0, 0, tiled=True)

    return combine(forms, basis)


def solution(mesh):
    placed = (
        P(("period", "gx")),
        P(None, ("period", "gx")),
        P(None, ("period", "gx")),
        P(None, None, ("period", "gx")),
        P(None, "gx", None, None),
        P("period"),
    )
    return jax.shard_map(
        functools.partial(per_device, mesh.shape["period"], mesh.shape["gx"]),
        mesh=mesh,
        in_specs=placed,
        out_specs=(P("period", "gx", None, None), P("period", "gx", None, None)),
        check_vma=False,
    )
```
